32 devices in a mesh: dp: 4 (over y, x), fsdp: 8 (over z, core).
Axes of the slice: x: 2, y: 2, z: 4, core: 2. Of those that a mesh axis runs over, the one named last changes fastest.
Arguments:
- tokens: bfloat16 [128, 196, 768], P(('dp', 'fsdp')), may hold values from -6 to 6
- image_counts: int32 [32], P(('dp', 'fsdp')), may hold values from 1 to 4, as said below
- skip_mask: int32 [128, 2, 2], P(('dp', 'fsdp')), may hold values 0 or 1
- norm1_gain: bfloat16 [2, 768], P(None, 'fsdp'), may hold values from 0.5 to 1.5
- norm1_bias: bfloat16 [2, 768], P(None, 'fsdp'), may hold values from -2 to 2
- token_in: bfloat16 [2, 196, 384], P(None, None, 'fsdp'), may hold values from -0.4375 to 0.4375
- token_in_bias: bfloat16 [2, 384], P(None, 'fsdp'), may hold values from -2 to 2
- token_out: bfloat16 [2, 384, 196], P(None, 'fsdp'), may hold values from -0.3125 to 0.3125
- token_out_bias: bfloat16 [2, 196], replicated, may hold values from -2 to 2
- norm2_gain: bfloat16 [2, 768], P(None, 'fsdp'), may hold values from 0.5 to 1.5
- norm2_bias: bfloat16 [2, 768], P(None, 'fsdp'), may hold values from -2 to 2
- channel_in: bfloat16 [2, 768, 3072], P(None, 'fsdp'), may hold values from -0.21875 to 0.21875
- channel_in_bias: bfloat16 [2, 3072], P(None, 'fsdp'), may hold values from -2 to 2
- channel_out: bfloat16 [2, 3072, 768], P(None, 'fsdp'), may hold values from -0.109375 to 0.109375
- channel_out_bias: bfloat16 [2, 768], P(None, 'fsdp'), may hold values from -2 to 2
- cotangent: bfloat16 [128, 196, 768], P(('dp', 'fsdp')), may hold values from -6 to 6
Outputs:
- output: bfloat16 [128, 196, 768], P(('dp', 'fsdp'))
- input_grad: float32 [128, 196, 768], P(('dp', 'fsdp'))
- grad_norm1_gain: float32 [2, 768], P(None, 'fsdp')
- grad_norm1_bias: float32 [2, 768], P(None, 'fsdp')
- grad_token_in: float32 [2, 196, 384], P(None, None, 'fsdp')
- grad_token_in_bias: float32 [2, 384], P(None, 'fsdp')
- grad_token_out: float32 [2, 384, 196], P(None, 'fsdp')
- grad_token_out_bias: float32 [2, 196], replicated
- grad_norm2_gain: float32 [2, 768], P(None, 'fsdp')
- grad_norm2_bias: float32 [2, 768], P(None, 'fsdp')
- grad_channel_in: float32 [2, 768, 3072], P(None, 'fsdp')
- grad_channel_in_bias: float32 [2, 3072], P(None, 'fsdp')
- grad_channel_out: float32 [2, 3072, 768], P(None, 'fsdp')
- grad_channel_out_bias: float32 [2, 768], P(None, 'fsdp')
The draws below stay inside these ranges and needn't reach their ends.
Inputs may be any that keep to these rules, and one draw needn't show every extreme that they name: `image_counts`: some device holds 4 live images.
All inputs are finite; a program needn't handle non-finite values. No bound on the sum of `skip_mask` on one device may be relied on, other than what follows from the above.
Results may differ from the reference program's by a relative error of at most 0.014.
Values may be sent and summed in bfloat16 or wider, within the bound.
No kernel may reach another device: no remote copies, remote signals or barrier semaphores. Data moves between devices by JAX's collectives and lax.ppermute only.
A program may use at most 256 MiB of HBM per device.

```python
import math
import jax
import jax.numpy as jnp
from jax import lax

D = 768
S = 196
DS = 384
DC = 3072
LAYERS = 2
SLOTS = 4
IMAGES = 128


def draw_image_counts(key, part):
    key = jax.random.fold_in(key, 11)
    devices = IMAGES // SLOTS
    first, second = jax.random.split(key)
    counts = jax.random.randint(first, (devices,), 1, SLOTS + 1)
    fullest = jax.random.randint(second, (), 0, devices)
    return jnp.where(jnp.arange(devices) == fullest, SLOTS, counts).astype(jnp.int32)


def plant(drawn, stream_key, low, largest):
    longest = drawn.shape.index(max(drawn.shape))
    spots = []
    for shift in (0, 1):
        where = [jax.random.randint(jax.random.fold_in(stream_key, axis), (), 0, length) for axis, length in enumerate(drawn.shape)]
        where[longest] = (where[longest] + shift) % drawn.shape[longest]
        spots.append(tuple(where))
    return drawn.at[spots[0]].set(low).at[spots[1]].set(largest)


def levels(rng, dims, shards, least, largest):
    level = 1.0
    for dim, blocks in shards:
        draws = jax.random.uniform(jax.random.fold_in(jax.random.fold_in(rng, 6), dim), (blocks,), jnp.float32, least / len(shards), largest / len(shards))
        level = level * jnp.repeat(jnp.exp(draws), dims[dim] // blocks).reshape((-1,) + (1,) * (len(dims) - 1 - dim))
    return level


def bell_draw(rng, shape, width, bound, cuts=(), held_as=jnp.bfloat16):
    level = levels(rng, shape, cuts, -0.22, 0.18) if cuts else 1.0
    values = jax.random.normal(rng, shape, jnp.float32) * width * level
    return jnp.minimum(jnp.maximum(values, -bound), bound).astype(held_as)


def setup_inputs(seed: int = 0) -> dict:
    keys = jax.random.split(jax.random.key(seed), 17)
    return {
        "tokens": bell_draw(keys[0], (IMAGES, S, D), 1.0, 6.0, ((0, 32),)),
        "image_counts": draw_image_counts(jax.random.fold_in(keys[16], 71), 0),
        "skip_mask": plant((jax.random.randint(keys[2], (IMAGES, LAYERS, 2), 0, 4) < 3).astype(jnp.int32), jax.random.fold_in(keys[2], 1), 0, 1),
        "norm1_gain": jnp.clip(1.0 + 0.1 * jax.random.normal(keys[3], (LAYERS, D), jnp.float32), 0.5, 1.5).astype(jnp.bfloat16),
        "norm1_bias": bell_draw(keys[4], (LAYERS, D), 0.3, 2.0, ((1, 8),)),
        "token_in": bell_draw(keys[5], (LAYERS, S, DS), S ** -0.5, 0.4375, ((2, 8),)),
        "token_in_bias": bell_draw(keys[6], (LAYERS, DS), 0.3, 2.0, ((1, 8),)),
        "token_out": bell_draw(keys[7], (LAYERS, DS, S), DS ** -0.5, 0.3125, ((1, 8),)),
        "token_out_bias": bell_draw(keys[8], (LAYERS, S), 0.3, 2.0),
        "norm2_gain": jnp.clip(1.0 + 0.1 * jax.random.normal(keys[9], (LAYERS, D), jnp.float32), 0.5, 1.5).astype(jnp.bfloat16),
        "norm2_bias": bell_draw(keys[10], (LAYERS, D), 0.3, 2.0, ((1, 8),)),
        "channel_in": bell_draw(keys[11], (LAYERS, D, DC), D ** -0.5, 0.21875, ((1, 8),)),
        "channel_in_bias": bell_draw(keys[12], (LAYERS, DC), 0.3, 2.0, ((1, 8),)),
        "channel_out": bell_draw(keys[13], (LAYERS, DC, D), DC ** -0.5, 0.109375, ((1, 8),)),
        "channel_out_bias": bell_draw(keys[14], (LAYERS, D), 0.3, 2.0, ((1, 8),)),
        "cotangent": bell_draw(keys[15], (IMAGES, S, D), 1.0, 6.0, ((0, 32),)),
    }


EPSILON = 1e-06
HIGH = lax.Precision.HIGHEST

@jax.custom_vjp
def low(v):
    return lax.optimization_barrier(v.astype(jnp.bfloat16)).astype(jnp.float32)

@jax.custom_vjp
def low_back(v):
    return v

def low_keep(v):
    return (low(v), None)

def low_pass(kept, grad):
    return (grad,)

def back_keep(v):
    return (v, None)

def back_low(kept, grad):
    return (low(grad),)
low.defvjp(low_keep, low_pass)
low_back.defvjp(back_keep, back_low)

def layer_norm(values, gain, shift):
    center = values - lax.optimization_barrier(jnp.mean(values, -1, keepdims=True))
    inv_std = lax.rsqrt(lax.optimization_barrier(jnp.mean(center * center, -1, keepdims=True)) + EPSILON)
    return center * inv_std * gain + shift

def forward(params, values, scale):
    gain1, shift1, w_tin, b_tin, w_tout, b_tout, gain2, shift2, w_cin, b_cin, w_cout, b_cout = params
    for index in range(LAYERS):
        normed = low(layer_norm(values, gain1[index], shift1[index]))
        pre_tok = low_back(jnp.einsum('isd,sk->idk', normed, w_tin[index], precision=HIGH)) + b_tin[index]
        hidden = low(jax.nn.gelu(pre_tok))
        branch = low_back(jnp.einsum('idk,ks->isd', hidden, w_tout[index], precision=HIGH)) + b_tout[index][None, :, None]
        values = values + scale[:, index, 0][:, None, None] * branch
        normed = low(layer_norm(values, gain2[index], shift2[index]))
        pre_chan = low_back(jnp.einsum('isd,df->isf', normed, w_cin[index], precision=HIGH)) + b_cin[index]
        hidden = low(jax.nn.gelu(pre_chan))
        branch = low_back(jnp.einsum('isf,fd->isd', hidden, w_cout[index], precision=HIGH)) + b_cout[index]
        values = values + scale[:, index, 1][:, None, None] * branch
    return values

def reference(tokens, image_counts, skip_mask, norm1_gain, norm1_bias, token_in, token_in_bias, token_out, token_out_bias, norm2_gain, norm2_bias, channel_in, channel_in_bias, channel_out, channel_out_bias, cotangent):
    params = tuple((w.astype(jnp.float32) for w in (norm1_gain, norm1_bias, token_in, token_in_bias, token_out, token_out_bias, norm2_gain, norm2_bias, channel_in, channel_in_bias, channel_out, channel_out_bias)))
    slot_ids = jnp.arange(IMAGES, dtype=jnp.int32)
    owner = slot_ids // SLOTS
    live = (slot_ids % SLOTS < image_counts[owner]).astype(jnp.float32)
    scale = live[:, None, None] * skip_mask.astype(jnp.float32)
    group = math.gcd(IMAGES, 16)
    groups = IMAGES // group
    inputs = tokens.astype(jnp.float32).reshape(groups, group, S, D)
    scales = scale.reshape(groups, group, LAYERS, 2)
    cotans = cotangent.astype(jnp.float32).reshape(groups, group, S, D)

    def step(total, item):
        block_in, block_scale, block_cot = item
        result, pull = jax.vjp(lambda p, v: forward(p, v, block_scale), params, block_in)
        grad_params, grad_in = pull(block_cot)
        total = jax.tree.map(lambda a, b: a + b, total, grad_params)
        return (total, (result, grad_in))
    zeros = jax.tree.map(jnp.zeros_like, params)
    total, (results, grads_in) = lax.scan(step, zeros, (inputs, scales, cotans))
    output = results.reshape(IMAGES, S, D).astype(jnp.bfloat16)
    input_grad = grads_in.reshape(IMAGES, S, D)
    return (output, input_grad) + tuple(total)
```

```python
import functools
import math

import jax
import jax.numpy as jnp
from jax import lax
from jax.experimental import pallas as pl
from jax.experimental.pallas import tpu as pltpu
from jax.sharding import PartitionSpec as P

EPSILON = 1e-06
GELU_A = math.sqrt(2.0 / math.pi)
GELU_B = 0.044715 * GELU_A
IMAGES = 2
VMEM_BYTES = 60 * 2**20


def as_sent(shard):

    def short(part):
        return part.astype(jnp.bfloat16) if part.dtype == jnp.float32 else part

    return jax.tree.map(short, shard)


def layer_norm(values, gain, shift):
    center = values - jnp.mean(values, -1, keepdims=True)
    inv_std = lax.rsqrt(jnp.mean(center * center, -1, keepdims=True) + EPSILON)
    normed = center * inv_std
    return (normed * gain + shift, normed, inv_std)


def norm_back(grad_out, normed, inv_std, gain):
    grad_gain = jnp.sum(grad_out * normed, axis=(0, 1))
    grad_shift = jnp.sum(grad_out, axis=(0, 1))
    scaled = grad_out * gain
    grad_in = inv_std * (
        scaled
        - jnp.mean(scaled, -1, keepdims=True)
        - normed * jnp.mean(scaled * normed, -1, keepdims=True)
    )
    return (grad_in, grad_gain, grad_shift)


def gelu_back(pre_act, grad_out):
    return jax.vjp(jax.nn.gelu, pre_act)[1](grad_out)[0]


def fetch_forward(pieces):
    return (
        lax.all_gather(pieces[0], "fsdp", axis=0, tiled=True),
        lax.all_gather(pieces[1], "fsdp", axis=0, tiled=True),
        lax.all_gather(pieces[2], "fsdp", axis=1, tiled=True),
        lax.all_gather(pieces[3], "fsdp", axis=0, tiled=True),
        lax.all_gather(pieces[4], "fsdp", axis=0, tiled=True),
        lax.all_gather(pieces[5], "fsdp", axis=0, tiled=True),
        lax.all_gather(pieces[6], "fsdp", axis=0, tiled=True),
        lax.all_gather(pieces[7], "fsdp", axis=0, tiled=True),
        lax.all_gather(pieces[8], "fsdp", axis=0, tiled=True),
        lax.all_gather(pieces[9], "fsdp", axis=0, tiled=True),
        lax.all_gather(pieces[10], "fsdp", axis=0, tiled=True),
    )


def fetch_backward(pieces):
    return (
        lax.all_gather(pieces[0], "fsdp", axis=0, tiled=True),
        lax.all_gather(pieces[1], "fsdp", axis=0, tiled=True),
        lax.all_gather(pieces[2], "fsdp", axis=1, tiled=True),
        lax.all_gather(pieces[3], "fsdp", axis=0, tiled=True),
        lax.all_gather(pieces[4], "fsdp", axis=0, tiled=True),
        lax.all_gather(pieces[5], "fsdp", axis=0, tiled=True),
        lax.all_gather(pieces[6], "fsdp", axis=0, tiled=True),
        lax.all_gather(pieces[7], "fsdp", axis=0, tiled=True),
        lax.all_gather(pieces[8], "fsdp", axis=0, tiled=True),
        lax.all_gather(pieces[9], "fsdp", axis=0, tiled=True),
        lax.all_gather(pieces[10], "fsdp", axis=0, tiled=True),
    )


def shards(
    tokens,
    image_counts,
    skip_mask,
    norm1_gain,
    norm1_bias,
    token_in,
    token_in_bias,
    token_out,
    token_out_bias,
    norm2_gain,
    norm2_bias,
    channel_in,
    channel_in_bias,
    channel_out,
    channel_out_bias,
    cotangent,
):
    f32 = jnp.float32
    bf16 = jnp.bfloat16
    slots = tokens.shape[0]
    layers = norm1_gain.shape[0]
    live = (jnp.arange(slots, dtype=jnp.int32) < image_counts[0]).astype(f32)
    branch_scale = live[:, None, None] * skip_mask.astype(f32)

    def layer_pieces(index):
        return (
            norm1_gain[index],
            norm1_bias[index],
            token_in[index],
            token_in_bias[index],
            token_out[index],
            norm2_gain[index],
            norm2_bias[index],
            channel_in[index],
            channel_in_bias[index],
            channel_out[index],
            channel_out_bias[index],
        )

    values = tokens.astype(f32)
    saved = []
    kept_weights = []
    for index in range(layers):
        weights = fetch_forward(layer_pieces(index))
        kept_weights.append(weights)
        gain1, shift1, w_tin, b_tin, w_tout, gain2, shift2, w_cin, b_cin, w_cout, b_cout = weights
        tok_bias = token_out_bias[index].astype(f32)
        normed1, plain1, inv1 = layer_norm(values, gain1.astype(f32), shift1.astype(f32))
        normed1 = normed1.astype(bf16)
        pre_tok = jnp.einsum(
            "isd,sk->idk", normed1, w_tin, preferred_element_type=f32
        ) + b_tin.astype(f32)
        hidden1 = jax.nn.gelu(pre_tok).astype(bf16)
        branch = (
            jnp.einsum("idk,ks->isd", hidden1, w_tout, preferred_element_type=f32)
            + tok_bias[None, :, None]
        )
        middle = values + branch_scale[:, index, 0][:, None, None] * branch
        normed2, plain2, inv2 = layer_norm(middle, gain2.astype(f32), shift2.astype(f32))
        normed2 = normed2.astype(bf16)
        pre_chan = jnp.einsum(
            "isd,df->isf", normed2, w_cin, preferred_element_type=f32
        ) + b_cin.astype(f32)
        hidden2 = jax.nn.gelu(pre_chan).astype(bf16)
        branch = jnp.einsum(
            "isf,fd->isd", hidden2, w_cout, preferred_element_type=f32
        ) + b_cout.astype(f32)
        values = middle + branch_scale[:, index, 1][:, None, None] * branch
        saved.append(
            (normed1, plain1, inv1, pre_tok, hidden1, normed2, plain2, inv2, pre_chan, hidden2)
        )
    output = values.astype(bf16)
    grad = cotangent.astype(f32)
    local_grads = [None] * layers
    bias_grads = [None] * layers
    for index in reversed(range(layers)):
        weights = fetch_backward(layer_pieces(index))
        gain1, shift1, w_tin, b_tin, w_tout, gain2, shift2, w_cin, b_cin, w_cout, b_cout = weights
        normed1, plain1, inv1, pre_tok, hidden1, normed2, plain2, inv2, pre_chan, hidden2 = saved[
            index
        ]
        out_chan = branch_scale[:, index, 1][:, None, None] * grad
        grad_b_cout = jnp.sum(out_chan, axis=(0, 1))
        low_chan = out_chan.astype(bf16)
        grad_w_cout = jnp.einsum("isf,isd->fd", hidden2, low_chan, preferred_element_type=f32)
        back_hidden = jnp.einsum("isd,fd->isf", low_chan, w_cout, preferred_element_type=f32)
        pre_grad = gelu_back(pre_chan, back_hidden)
        grad_b_cin = jnp.sum(pre_grad, axis=(0, 1))
        low_pre = pre_grad.astype(bf16)
        grad_w_cin = jnp.einsum("isd,isf->df", normed2, low_pre, preferred_element_type=f32)
        back_norm = jnp.einsum("isf,df->isd", low_pre, w_cin, preferred_element_type=f32)
        norm_in, grad_gain2, grad_shift2 = norm_back(back_norm, plain2, inv2, gain2.astype(f32))
        grad_mid = grad + norm_in
        out_tok = branch_scale[:, index, 0][:, None, None] * grad_mid
        bias_grads[index] = jnp.sum(out_tok, axis=(0, 2))
        low_tok = out_tok.astype(bf16)
        grad_w_tout = jnp.einsum("idk,isd->ks", hidden1, low_tok, preferred_element_type=f32)
        back_hidden = jnp.einsum("isd,ks->idk", low_tok, w_tout, preferred_element_type=f32)
        pre_grad = gelu_back(pre_tok, back_hidden)
        grad_b_tin = jnp.sum(pre_grad, axis=(0, 1))
        low_pre = pre_grad.astype(bf16)
        grad_w_tin = jnp.einsum("isd,idk->sk", normed1, low_pre, preferred_element_type=f32)
        back_norm = jnp.einsum("idk,sk->isd", low_pre, w_tin, preferred_element_type=f32)
        norm_in, grad_gain1, grad_shift1 = norm_back(back_norm, plain1, inv1, gain1.astype(f32))
        grad = grad_mid + norm_in
        local = (
            grad_gain1,
            grad_shift1,
            grad_w_tin,
            grad_b_tin,
            grad_w_tout,
            grad_gain2,
            grad_shift2,
            grad_w_cin,
            grad_b_cin,
            grad_w_cout,
            grad_b_cout,
        )
        local_grads[index] = local
    token_bias_total = lax.psum(jnp.stack(bias_grads), ("dp", "fsdp"))
    joined = tuple(
        (
            jnp.stack([local_grads[index][position] for index in range(layers)])
            for position in range(11)
        )
    )
    owned = (
        lax.psum_scatter(joined[0], "fsdp", scatter_dimension=1, tiled=True),
        lax.psum_scatter(joined[1], "fsdp", scatter_dimension=1, tiled=True),
        lax.psum_scatter(joined[2], "fsdp", scatter_dimension=2, tiled=True),
        lax.psum_scatter(joined[3], "fsdp", scatter_dimension=1, tiled=True),
        lax.psum_scatter(joined[4], "fsdp", scatter_dimension=1, tiled=True),
        lax.psum_scatter(joined[5], "fsdp", scatter_dimension=1, tiled=True),
        lax.psum_scatter(joined[6], "fsdp", scatter_dimension=1, tiled=True),
        lax.psum_scatter(joined[7], "fsdp", scatter_dimension=1, tiled=True),
        lax.psum_scatter(joined[8], "fsdp", scatter_dimension=1, tiled=True),
        lax.psum_scatter(joined[9], "fsdp", scatter_dimension=1, tiled=True),
        lax.psum_scatter(joined[10], "fsdp", scatter_dimension=1, tiled=True),
    )
    results = jax.tree.map(lambda part: part.astype(jnp.float32), lax.psum(as_sent(owned), "dp"))
    return (
        output,
        grad,
        results[0],
        results[1],
        results[2],
        results[3],
        results[4],
        token_bias_total,
        results[5],
        results[6],
        results[7],
        results[8],
        results[9],
        results[10],
    )


def norm_parts(values):
    center = values - jnp.mean(values, -1, keepdims=True)
    inv_std = lax.rsqrt(jnp.mean(center * center, -1, keepdims=True) + EPSILON)
    return center * inv_std, inv_std


def norm_input_grad(grad, normed, inv_std):
    return inv_std * (
        grad
        - jnp.mean(grad, -1, keepdims=True)
        - normed * jnp.mean(grad * normed, -1, keepdims=True)
    )


def gelu_pair(value):
    square = value * value
    gate = 0.5 + 0.5 * jnp.tanh(value * (GELU_A + GELU_B * square))
    result = value * gate
    slope = gate + result * (1.0 - gate) * (2.0 * GELU_A + 6.0 * GELU_B * square)
    return result.astype(jnp.bfloat16), slope.astype(jnp.bfloat16)


def dot(left, right, left_dim, right_dim):
    return lax.dot_general(
        left, right, (((left_dim,), (right_dim,)), ((), ())), preferred_element_type=jnp.float32
    )


def chunks(size, count):
    return [slice(k * size // count, (k + 1) * size // count) for k in range(count)]


def position(copy):
    odd = copy & 1
    return 2 * odd + (odd ^ (copy >> 1))


def clear(first, *refs):
    @pl.when(first)
    def _():
        for ref in refs:
            ref[...] = jnp.zeros_like(ref)


def unpack_small(place, own, other, *refs):
    vectors = refs[-1]
    z, c = place[0], place[1]
    lines, rows, _ = own.shape
    layers, extra, wide = vectors.shape[1:]
    keys = rows // layers
    for layer in range(layers):
        w_in, w_in_t, w_out, w_out_t, *rest = refs[10 * layer : 10 * layer + 10]
        base = layer * keys
        for source, side in ((own, c), (other, 1 - c)):
            for i in range(lines):
                shard = 2 * (i ^ z) + side
                start = pl.multiple_of(shard * keys, keys)
                w_in[pl.ds(start, keys)] = source[i, base : base + keys, :wide]
                w_out[pl.ds(start, keys)] = source[i, base : base + keys, wide : 2 * wide]
                vectors[shard, layer] = source[i, base : base + extra, 2 * wide :]
        w_in_t[...] = w_in[...].T
        w_out_t[...] = w_out[...].T
        held = [vectors[shard, layer].astype(jnp.float32) for shard in range(vectors.shape[0])]
        for row, target in enumerate(rest[:5]):
            size = target.shape[1] // len(held)
            target[...] = jnp.concatenate([part[row : row + 1, :size] for part in held], axis=1)
        biases = rest[5]
        size = biases.shape[1] // len(held)
        for shard, part in enumerate(held):
            whole = jnp.concatenate([part[5:6], part[6:7]], axis=1)
            biases[:, shard * size : (shard + 1) * size] = whole[:, :size]


def token_branch(values, scale, small, b_out, u_out, hidden_out, slope_out):
    gain1, shift1, w_in, w_out, gain2, shift2 = small
    rows, wide = values.shape[0], w_in.shape[1]
    normed, _ = norm_parts(values)
    u_out[:rows] = (normed * gain1[...] + shift1[...]).astype(jnp.bfloat16)
    below = lax.broadcasted_iota(jnp.int32, (wide - rows, values.shape[1]), 0)
    u_out[rows:] = jnp.where(below == 0, 1.0, 0.0).astype(jnp.bfloat16)
    hidden, slope = gelu_pair(dot(w_in[...], u_out[...], 1, 0))
    hidden_out[...] = hidden
    slope_out[...] = slope
    middle = values + scale * (dot(w_out[:rows], hidden, 1, 0) + b_out[0, :rows])
    normed, _ = norm_parts(middle)
    return middle, (normed * gain2[...] + shift2[...]).astype(jnp.bfloat16)


def token_forward(place, scale, x, b_out, *rest, layer):
    small, (u_out, hidden_out, slope_out, middle_out, v_out) = rest[:6], rest[6:]
    count, rows = x.shape[:2]
    for k in range(count):
        part = scale[count * pl.program_id(0) + k, 2 * layer]
        middle, v = token_branch(
            x[k].astype(jnp.float32), part, small, b_out, u_out.at[k], hidden_out.at[k], slope_out.at[k]
        )
        middle_out[k] = middle
        v_out[k * rows : (k + 1) * rows] = v


def token_grads(scale, grad, back_v, middle, x, u, hidden, slope, w_in, w_out, gain1, gain2, padded):
    rows, width = grad.shape
    normed, inv_std = norm_parts(middle)
    moved = back_v * normed
    sums = [jnp.sum(moved, 0, keepdims=True), jnp.sum(back_v, 0, keepdims=True)]
    grad_mid = grad + norm_input_grad(back_v * gain2[...], normed, inv_std)
    padded[:rows] = (scale * grad_mid).astype(jnp.bfloat16)
    low = padded[...]
    b_out = dot(jnp.ones((8, width), jnp.bfloat16), low, 1, 1)[:1]
    w_out_grad = dot(hidden, low, 1, 1)
    pre = (dot(w_out[...], low, 1, 0) * slope.astype(jnp.float32)).astype(jnp.bfloat16)
    w_in_grad = dot(pre, u, 1, 1)
    back = dot(w_in[:rows], pre, 1, 0)
    normed, inv_std = norm_parts(x)
    sums = [jnp.sum(back * normed, 0, keepdims=True), jnp.sum(back, 0, keepdims=True)] + sums
    return grad_mid + norm_input_grad(back * gain1[...], normed, inv_std), sums, b_out, w_in_grad, w_out_grad


def token_blocks(place, w_in_grad, w_out_grad, whole, put):
    z, c = place[0], place[1]
    keys = whole.shape[1] // 8
    for which, total in ((0, w_in_grad), (1, w_out_grad)):
        whole[which] = total[...].astype(jnp.bfloat16)
        for i in range(4):
            for side, core in ((0, c), (1, 1 - c)):
                start = pl.multiple_of((2 * (i ^ z) + core) * keys, keys)
                put(which, i, side, whole[which, pl.ds(start, keys)])


def token_backward(place, scale, grad, back_v, middle, x, u, hidden, slope, w_in, w_out, gain1, gain2, *rest):
    image = pl.program_id(0)
    g_cout, g_cin = rest[:2]
    last = len(rest) == 2 + 6 + 4
    if last:
        grad_out, mine_out, other_out, vector, low_out, above_grad = rest[2:8]
        layer = 1
    else:
        earlier, grad_out, mine_out, other_out, vector = rest[2:5], *rest[7:11]
        layer = 0
    padded, w_in_grad, w_out_grad, whole = rest[-4:]
    count, rows = x.shape[:2]
    first = image == 0
    clear(first, padded, vector, w_in_grad, w_out_grad)

    @pl.when(first)
    def _():
        vector[4:5] = g_cout[...]
        for j in range(g_cin.shape[0]):
            vector[8 + j : 9 + j] = g_cin[j]
        if not last:
            vector[16:] = earlier[2][...]

    if last:
        clear(first, above_grad)
    found = []
    for k in range(count):
        part = slice(k * rows, (k + 1) * rows)
        result, *sums = token_grads(
            scale[count * image + k, 2 * layer], grad[k].astype(jnp.float32), back_v[part], middle[k],
            x[k].astype(jnp.float32), u[k], hidden[k], slope[k], w_in, w_out, gain1, gain2, padded.at[k],
        )
        grad_out[k] = result
        if last:
            out = scale[count * image + k, 1] * result
            above_grad[...] += jnp.sum(out, 0, keepdims=True)
            low_out[part] = out.astype(jnp.bfloat16)
        found.append(sums)
    for k in range(4):
        vector[k : k + 1] += sum(sums[0][k] for sums in found)
    vector[5:6, : padded.shape[1]] += sum(sums[1] for sums in found)
    w_in_grad[...] += sum(sums[2] for sums in found)
    w_out_grad[...] += sum(sums[3] for sums in found)

    @pl.when(image == pl.num_programs(0) - 1)
    def _():
        targets = (mine_out, other_out)
        if last:

            def put(which, i, side, part):
                targets[side][which, i] = part

        else:

            def put(which, i, side, part):
                place_tokens(targets[side], position(which ^ place[2]), i, part)

            for side in range(2):
                for which in range(2):
                    for i in range(4):
                        part = earlier[side][which, i]
                        place_tokens(targets[side], position((2 + which) ^ place[2]), i, part)
        token_blocks(place, w_in_grad, w_out_grad, whole, put)


def place_tokens(target, j, i, part):
    rows, wide = target.shape[2], part.shape[1]
    for k in range(part.shape[0] // rows):
        target[j, i, :, k * wide : (k + 1) * wide] = part[k * rows : (k + 1) * rows]


def out_weight_grad(place, low, hidden, mine_out, other_out, turned, whole):
    @pl.when(pl.program_id(0) == 0)
    def _():
        turned[...] = low[...].T

    out_blocks(place, turned, hidden[0], mine_out, other_out, whole)


class Weight:
    def __init__(self, refs, which):
        self.which = which
        self.shards, self.parts = (refs[which], refs[2 + which]), (refs[4 : 4 + 4], refs[8:12])

    def blocks(self, copy, i):
        for side, (line, from_x, from_y, corner) in enumerate(self.parts):
            yield side, (line, from_x, from_y, corner)[copy].at[i - 1, self.which], 0


def fetch_in(place, layer, weight, target, sem):
    z, c, q = place[0], place[1], place[2]
    copies, _, columns = target.shape
    rows = weight.shards[0].shape[1]
    for copy in range(copies):
        j = copy ^ q

        def put(ref, i, side, first):
            start = pl.multiple_of((2 * (i ^ z) + (c ^ side)) * rows + first, 16)
            goal = target.at[j, pl.ds(start, ref.shape[0])]
            pltpu.make_async_copy(ref, goal, sem.at[j]).start()

        for side, shard in enumerate(weight.shards):
            put(shard.at[layer, :, pl.ds(pl.multiple_of(j * columns, columns), columns)], 0, side, 0)
        for i in range(1, copies):
            for side, ref, first in weight.blocks(copy, i):
                put(ref, i, side, first)


def fetch_out(place, layer, weight, target, sem):
    z, c, q = place[0], place[1], place[2]
    lines, part, _ = target.shape
    for i in range(lines):

        def put(ref, start):
            goal = target.at[i ^ z, pl.ds(pl.multiple_of(start, 16), ref.shape[0])]
            pltpu.make_async_copy(ref, goal, sem.at[i ^ z]).start()

        if i == 0:
            for side, shard in enumerate(weight.shards):
                put(shard.at[layer], (c ^ side) * (part // 2))
            continue
        for copy in range(4):
            for side, ref, first in weight.blocks(copy, i):
                put(ref, (c ^ side) * (part // 2) + (copy ^ q) * (part // 8) + first)


def arrive(weight, sem, step):
    pltpu.make_async_copy(weight.at[step], weight.at[step], sem.at[step]).wait()


def out_blocks(place, turned, hidden, mine_out, other_out, whole):
    c, q = place[1], place[2]
    whole[...] = dot(turned[...], hidden, 1, 0).astype(jnp.bfloat16)
    copies, _, rows, columns = mine_out.shape
    size = columns // 2
    for side, target in ((c, mine_out), (1 - c, other_out)):
        units = pl.ds(pl.multiple_of(side * size, 128), size)
        for j in range(copies):
            start = 2 * j * rows
            target[position(j ^ q), 0, :, :size] = whole[start : start + rows, units]
            target[position(j ^ q), 0, :, size:] = whole[start + rows : start + 2 * rows, units]


def first_forward(place, scale, v, middle, bias_in, bias_out, *rest):
    weight_in, weight_out = Weight(rest[:12], 0), Weight(rest[:12], 1)
    hidden_out, slope_out, x_out, w_in, w_out, hidden, total, sem_in, sem_out = rest[12:]
    step = pl.program_id(0)
    rows = middle.shape[1]

    @pl.when(step == 0)
    def _():
        fetch_in(place, 0, weight_in, w_in, sem_in)
        fetch_out(place, 0, weight_out, w_out, sem_out)
        total[...] = jnp.zeros_like(total)

    @pl.when(step < 4)
    def _():
        j = (step & 3) ^ place[2]
        arrive(w_in, sem_in, j)
        for part in chunks(v.shape[0], 2):
            value, slope = gelu_pair(dot(v[part], w_in[j], 1, 0) + bias_in[...])
            hidden_out[0, part] = value
            hidden[j, part] = value
            slope_out[0, part] = slope

    @pl.when(step >= 4)
    def _():
        j = (step & 3) ^ place[0]
        arrive(w_out, sem_out, j)
        total[...] += dot(hidden[j], w_out[j], 1, 0)

    @pl.when(step == 7)
    def _():
        for image in range(middle.shape[0]):
            branch = total[image * rows : (image + 1) * rows] + bias_out[...]
            x_out[image] = middle[image] + scale[image, 1] * branch


def last_hidden(place, scale, v, bias, grad, *rest):
    weight = Weight(rest[:12], 0)
    (
        hidden_out, slope_out, mine_out, other_out, low_out, bias_grad, w_in, hidden, turned, whole, sem,
    ) = rest[12:]
    step = pl.program_id(0)

    @pl.when(step == 0)
    def _():
        fetch_in(place, 1, weight, w_in, sem)
        rows = grad.shape[1]
        sums = 0.0
        for image in range(grad.shape[0]):
            out = scale[image, 3] * grad[image].astype(jnp.float32)
            sums = sums + jnp.sum(out, 0, keepdims=True)
            low_out[image * rows : (image + 1) * rows] = out.astype(jnp.bfloat16)
        bias_grad[...] = sums
        turned[...] = low_out[...].T

    @pl.when(step < 4)
    def _():
        j = (step & 3) ^ place[2]
        arrive(w_in, sem, j)
        for part in chunks(v.shape[0], 2):
            value, slope = gelu_pair(dot(v[part], w_in[j], 1, 0) + bias[...])
            hidden_out[0, part] = value
            hidden[j, part] = value
            slope_out[0, part] = slope

    @pl.when(step >= 4)
    def _():
        out_blocks(place, turned, hidden[(step & 3) ^ place[0]], mine_out, other_out, whole)


def out_forward(place, scale, hidden, middle, bias, *rest, layer):
    x_out, weight, total, sem = rest[12:]
    step = pl.program_id(0)

    @pl.when(step == 0)
    def _():
        fetch_out(place, layer, Weight(rest[:12], 1), weight, sem)
        total[...] = jnp.zeros_like(total)

    j = step ^ place[0]
    arrive(weight, sem, j)
    total[...] += dot(hidden[0], weight[j], 1, 0)

    @pl.when(step == pl.num_programs(0) - 1)
    def _():
        for image in range(middle.shape[0]):
            rows = middle.shape[1]
            branch = total[image * rows : (image + 1) * rows] + bias[...]
            x_out[image] = (middle[image] + scale[image, 2 * layer + 1] * branch).astype(x_out.dtype)


def channel_backward(place, low, v, slope, *rest, layer):
    mine, theirs, back_out, bias_grad, w_out, w_in, turned, pre, whole, sem_out, sem_in = rest[12:]
    z, c = place[0], place[1]
    step = pl.program_id(0)

    @pl.when(step == 0)
    def _():
        fetch_out(place, layer, Weight(rest[:12], 1), w_out, sem_out)
        fetch_in(place, layer, Weight(rest[:12], 0), w_in, sem_in)
        turned[...] = v[...].T
        back_out[...] = jnp.zeros_like(back_out)

    j = step ^ z
    arrive(w_out, sem_out, j)
    arrive(w_in, sem_in, j)
    sums = 0.0
    for part in chunks(low.shape[0], 2):
        grad = dot(low[part], w_out[j], 1, 1) * slope[0, part].astype(jnp.float32)
        sums = sums + jnp.sum(grad, 0, keepdims=True)
        pre[part] = grad.astype(jnp.bfloat16)
    bias_grad[0] = sums
    for part in chunks(turned.shape[0], 3):
        whole[part] = dot(turned[part], pre[...], 1, 0).astype(jnp.bfloat16)
    lines = mine.shape[1]
    rows = whole.shape[0] // (2 * lines)
    for i in range(lines):
        for side, target in ((c, mine), (1 - c, theirs)):
            start = pl.multiple_of((2 * (i ^ z) + side) * rows, rows)
            target[0, i] = whole[pl.ds(start, rows)]
    back_out[...] += dot(pre[...], w_in[j], 1, 1)


def finish_out(place, *refs):
    parts, out, whole = refs[:4], refs[-2], refs[-1]
    for j in range(4):
        rows, columns = parts[j].shape[1:]
        for half in range(2):
            start = pl.multiple_of((2 * (j ^ place[2]) + half) * rows, rows)
            part = parts[j][0, :, half * columns // 2 : (half + 1) * columns // 2]
            whole[pl.ds(start, rows)] = part.astype(jnp.float32)
    out[0] = whole[...].T


def finish_in(place, *refs, tokens):
    parts, out = refs[:4], refs[-2] if tokens else refs[-1]
    rows = out.shape[1]
    for j in range(4):
        columns = parts[j].shape[2]
        start = pl.multiple_of((j ^ place[2]) * columns, columns)
        out[0, :, pl.ds(start, columns)] = parts[j][0, :rows].astype(jnp.float32)
        if tokens:
            wide = refs[-1].shape[2]
            for k in range(columns // wide):
                part = parts[j][0, rows:, k * wide : (k + 1) * wide]
                refs[-1][j ^ place[2], 16 * k : 16 * k + 16] = part.astype(jnp.float32)


class Kernels:
    def __init__(self, place, slots, rows, width, inner, hidden, lines, block):
        self.place = place
        self.slots, self.rows, self.width = slots, rows, width
        self.inner, self.hidden = inner, hidden
        self.lines, self.block = lines, block
        self.part = hidden // 4
        self.wide = 256

    def run(self, body, steps, inputs, outputs, scratch, flops, aliases=None, **fixed):
        sizes = sum(a.size * a.dtype.itemsize for a, _, _ in inputs)
        sizes += sum(math.prod(o[0]) * jnp.dtype(o[1]).itemsize for o in outputs)

        def spec(block, index):
            if isinstance(block, tuple):
                return pl.BlockSpec(block, index)
            return pl.BlockSpec(memory_space=block)

        return pl.pallas_call(
            functools.partial(body, **fixed) if fixed else body,
            name=body.__name__,
            grid_spec=pltpu.PrefetchScalarGridSpec(
                num_scalar_prefetch=1,
                grid=(steps,),
                in_specs=[spec(block, index) for _, block, index in inputs],
                out_specs=[spec(o[2], o[3]) for o in outputs],
                scratch_shapes=scratch,
            ),
            out_shape=[jax.ShapeDtypeStruct(o[0], o[1]) for o in outputs],
            input_output_aliases=aliases or {},
            compiler_params=pltpu.CompilerParams(
                dimension_semantics=("arbitrary",), vmem_limit_bytes=VMEM_BYTES
            ),
            cost_estimate=pl.CostEstimate(flops=flops, bytes_accessed=sizes, transcendentals=0),
        )(self.place, *[a for a, _, _ in inputs])

    def image(self, array):
        return (array, (1,) + array.shape[1:], lambda i, s: (i, 0, 0))

    def fixed(self, array):
        zeros = (0,) * array.ndim
        return (array, array.shape, lambda i, s: zeros)

    def scalars(self, array):
        return (array, pltpu.SMEM, None)

    def in_hbm(self, arrays):
        return [(a, pltpu.HBM, None) for a in arrays]

    def fixed_out(self, shape, dtype):
        zeros = (0,) * len(shape)
        return (shape, dtype, shape, lambda i, s: zeros)

    def columns(self, array, count):
        return (array, (array.shape[0], array.shape[1] // count), lambda i, s: (0, i))

    def columns_out(self, rows, columns, count, dtype):
        return ((rows, columns), dtype, (rows, columns // count), lambda i, s: (0, i))

    def late(self, step, start):
        return jnp.clip(step - start, 0, 3)

    def images_out(self, rows, dtype):
        block = (IMAGES, rows, self.width)
        return ((self.slots, rows, self.width), dtype, block, lambda i, s: (i, 0, 0))

    def images(self, array):
        return (array, (IMAGES,) + array.shape[1:], lambda i, s: (i, 0, 0))

    def rows_out(self):
        shape = (self.slots * self.rows, self.width)
        return (shape, jnp.bfloat16, (IMAGES * self.rows, self.width), lambda i, s: (i, 0))

    def quarters(self, array, which, start=0):
        return (array, (1,) + array.shape[1:], lambda i, s: (self.late(i, start) ^ s[which], 0, 0))

    def quarters_out(self, which, start=0):
        rows = self.slots * self.rows
        block = (1, rows, self.part)
        return ((4,) + block[1:], jnp.bfloat16, block, lambda i, s: (self.late(i, start) ^ s[which], 0, 0))

    def row(self, array, which, start=0):
        return (array, (1, self.part), lambda i, s: (0, self.late(i, start) ^ s[which]))

    def out_blocks_out(self, start=0):
        block = (4, 1, self.block, self.width)
        shape = (4, self.lines) + block[2:]
        return (shape, jnp.bfloat16, block, lambda i, s: (0, self.late(i, start), 0, 0))

    def product(self):
        return 2 * self.slots * self.rows * self.width * self.hidden

    def unpack_small(self, own, other, layers, shards, extra):
        bf16, f32 = jnp.bfloat16, jnp.float32
        inner, wide, width = self.inner, self.wide, self.width
        outputs = [((inner, wide), bf16), ((wide, inner), bf16)] * 2
        outputs += [((1, width), f32)] * 5 + [((1, self.hidden), f32)]
        found = self.run(
            unpack_small,
            1,
            [self.fixed(own), self.fixed(other)],
            [self.fixed_out(*part) for part in outputs * layers],
            [pltpu.VMEM((shards, layers, extra, wide), bf16)],
            0,
        )
        return [list(found[10 * layer : 10 * layer + 10]) for layer in range(layers)]

    def token_product(self):
        return 2 * self.slots * self.wide * self.width * self.inner

    def b_out(self, array, layer):
        return (array, (1,) + array.shape[1:], lambda i, s: (layer, 0, 0))

    def token_outs(self):
        bf16 = jnp.bfloat16
        outs = [self.images_out(rows, bf16) for rows in (self.wide, self.inner, self.inner)]
        return outs + [self.images_out(self.rows, jnp.float32), self.rows_out()]

    def token_forward(self, scale, x, b_out, small, layer):
        return self.run(
            token_forward,
            self.slots // IMAGES,
            [self.scalars(scale), self.images(x), self.b_out(b_out, layer)] + [self.fixed(a) for a in small],
            self.token_outs(),
            [],
            2 * self.token_product(),
            layer=layer,
        )

    def first_forward(self, scale, v, middle, bias_in, bias_out, weights):
        bf16, f32 = jnp.bfloat16, jnp.float32
        rows = self.slots * self.rows
        return self.run(
            first_forward,
            8,
            [self.scalars(scale), self.fixed(v), self.fixed(middle), self.row(bias_in, 2), self.fixed(bias_out)]
            + self.in_hbm(weights),
            [self.quarters_out(2)] * 2 + [self.fixed_out((self.slots, self.rows, self.width), f32)],
            [
                self.weight(),
                self.weight(),
                pltpu.VMEM((4, rows, self.part), bf16),
                pltpu.VMEM((rows, self.width), f32),
                pltpu.SemaphoreType.DMA((4,)),
                pltpu.SemaphoreType.DMA((4,)),
            ],
            2 * self.product(),
        )

    def last_hidden(self, scale, v, bias, grad, weights):
        bf16, f32 = jnp.bfloat16, jnp.float32
        rows = self.slots * self.rows
        return self.run(
            last_hidden,
            8,
            [self.scalars(scale), self.fixed(v), self.row(bias, 2), self.fixed(grad)] + self.in_hbm(weights),
            [self.quarters_out(2)] * 2
            + [self.out_blocks_out(4)] * 2
            + [self.fixed_out((rows, self.width), bf16), self.fixed_out((1, self.width), f32)],
            [
                self.weight(),
                pltpu.VMEM((4, rows, self.part), bf16),
                pltpu.VMEM((self.width, rows), bf16),
                pltpu.VMEM((self.width, self.part), bf16),
                pltpu.SemaphoreType.DMA((4,)),
            ],
            2 * self.product(),
        )

    def token_backward(self, scale, grad, back, kept, small, g_cout, g_cin, keys, earlier=(), blocks=()):
        bf16, f32 = jnp.bfloat16, jnp.float32
        rows, width = self.slots * self.rows, self.width
        middle, x, u, hidden, slope = kept
        inputs = [self.scalars(scale), self.images(grad)]
        inputs += [(back, (IMAGES * self.rows, width), lambda i, s: (i, 0))]
        inputs += [self.images(a) for a in (middle, x, u, hidden, slope)]
        inputs += [self.fixed(a) for a in tuple(small) + (g_cout, g_cin) + tuple(earlier)]
        outputs = [self.images_out(self.rows, f32)]
        aliases = None
        if earlier:
            aliases = {1 + len(inputs): 1, 2 + len(inputs): 2}
            inputs += self.in_hbm(blocks)
            extra = blocks[0].shape[2] - self.block
            block = (4, self.lines, extra, width)
            outputs += [(blocks[0].shape, bf16, block, lambda i, s: (0, 0, self.block // extra, 0))] * 2
            outputs += [self.fixed_out((32, width), f32)]
        else:
            outputs += [self.fixed_out((2, self.lines, keys, self.wide), bf16)] * 2
            outputs += [self.fixed_out((16, width), f32), self.rows_out(), self.fixed_out((1, width), f32)]
        return self.run(
            token_backward,
            self.slots // IMAGES,
            inputs,
            outputs,
            [
                pltpu.VMEM((IMAGES, self.wide, width), bf16),
                pltpu.VMEM((self.inner, self.wide), f32),
                pltpu.VMEM((self.inner, self.wide), f32),
                pltpu.VMEM((2, self.inner, self.wide), bf16),
            ],
            4 * self.token_product(),
            aliases,
        )

    def out_weight_grad(self, low, hidden):
        rows = self.slots * self.rows
        return self.run(
            out_weight_grad,
            4,
            [self.fixed(low), self.quarters(hidden, 0)],
            [self.out_blocks_out()] * 2,
            [pltpu.VMEM((self.width, rows), jnp.bfloat16), pltpu.VMEM((self.width, self.part), jnp.bfloat16)],
            self.product(),
        )

    def weight(self):
        return pltpu.VMEM((4, self.width, self.part), jnp.bfloat16)

    def out_forward(self, scale, hidden, middle, bias, weights, layer, dtype):
        return self.run(
            out_forward,
            4,
            [self.scalars(scale), self.quarters(hidden, 0), self.fixed(middle), self.fixed(bias)]
            + self.in_hbm(weights),
            [self.fixed_out(middle.shape, dtype)],
            [
                self.weight(),
                pltpu.VMEM((self.slots * self.rows, self.width), jnp.float32),
                pltpu.SemaphoreType.DMA((4,)),
            ],
            self.product(),
            layer=layer,
        )[0]

    def channel_backward(self, low, v, slope, weights, layer, extra=0):
        bf16, f32 = jnp.bfloat16, jnp.float32
        rows = self.slots * self.rows
        block = (1, self.lines, self.block, self.width)
        shape = (4, self.lines, self.block + extra, self.width)
        blocks = (shape, bf16, block, lambda j, s: (position(j ^ s[0] ^ s[2]), 0, 0, 0))
        return self.run(
            channel_backward,
            4,
            [self.fixed(low), self.fixed(v), self.quarters(slope, 0)]
            + self.in_hbm(weights),
            [
                blocks,
                blocks,
                self.fixed_out((rows, self.width), f32),
                ((4, 1, self.part), f32, (1, 1, self.part), lambda i, s: (i ^ s[0], 0, 0)),
            ],
            [
                self.weight(),
                self.weight(),
                pltpu.VMEM((self.width, rows), bf16),
                pltpu.VMEM((rows, self.part), bf16),
                pltpu.VMEM((self.width, self.part), bf16),
                pltpu.SemaphoreType.DMA((4,)),
                pltpu.SemaphoreType.DMA((4,)),
            ],
            3 * self.product(),
            layer=layer,
        )

    def parts(self, parts):
        def one(array, index):
            return (array, (1,) + array.shape[1:], lambda i, s: (index, 0, 0))

        return [one(*part) for part in parts]

    def finish_out(self, parts, layer, layers, earlier=()):
        shape = (layers, self.part // 2, self.width)
        return self.run(
            finish_out,
            1,
            self.parts(parts) + self.in_hbm(earlier),
            [(shape, jnp.float32, (1,) + shape[1:], lambda i, s: (layer, 0, 0))],
            [pltpu.VMEM((self.width, self.part // 2), jnp.float32)],
            0,
            {1 + len(parts): 0} if earlier else None,
        )

    def finish_in(self, parts, layer, layers, keys=0, earlier=()):
        shape = (layers, self.block, self.hidden)
        outputs = [(shape, jnp.float32, (1,) + shape[1:], lambda i, s: (layer, 0, 0))]
        if keys:
            outputs.append(self.fixed_out((4, keys, self.wide), jnp.float32))
        return self.run(
            finish_in,
            1,
            self.parts(parts) + self.in_hbm(earlier),
            outputs,
            [],
            0,
            {1 + len(parts): 0} if earlier else None,
            tokens=bool(keys),
        )


class Moves:
    def __init__(self):
        self.lines = lax.axis_size("fsdp") // 2
        self.copies = lax.axis_size("dp")
        me = lax.axis_index("fsdp")
        self.z, self.c, self.q = me // 2, me % 2, lax.axis_index("dp")

    def along(self, values, bits):
        return lax.ppermute(values, "fsdp", [(f, f ^ (2 * bits)) for f in range(2 * self.lines)])

    def core(self, values):
        return lax.ppermute(values, "fsdp", [(f, f ^ 1) for f in range(2 * self.lines)])

    def across(self, values, bits):
        return lax.ppermute(values, "dp", [(q, q ^ bits) for q in range(self.copies)])


class Held:
    def __init__(self, moves):
        self.moves, self.fresh = moves, []
        self.half = moves.lines // 2

    def bring(self, **arrays):
        for name, array in arrays.items():
            setattr(self, name, array)
            self.fresh.append(name)


def settle(held, *values):
    names = [(part, name) for part in held for name in part.fresh]
    arrays = tuple(getattr(part, name) for part, name in names)
    arrays = lax.optimization_barrier(tuple(values) + arrays)
    for (part, name), array in zip(names, arrays[len(values) :]):
        setattr(part, name, array)
    for part in held:
        part.fresh = []
    return arrays[: len(values)]


class Gather(Held):
    def __init__(self, moves, part):
        super().__init__(moves)
        self.part = part

    def direct(self):
        self.bring(**{"z%d" % i: self.moves.along(self.part, i) for i in range(1, self.moves.lines)})

    def join(self):
        self.line = jnp.stack([getattr(self, "z%d" % i) for i in range(1, self.moves.lines)])

    def first(self):
        self.bring(x=self.moves.across(self.line, 1), y=self.moves.across(self.line, 2))

    def second(self):
        self.bring(low=self.moves.across(self.y[:, :1], 1), high=self.moves.across(self.x[:, 1:], 2))

    def corner_core(self):
        self.corner = jnp.concatenate([self.low, self.high], 1)
        self.core("corner")

    def core(self, *names):
        self.bring(**{name + "_core": self.moves.core(getattr(self, name)) for name in names})

    def whole(self):
        names = ("line", "x", "y", "corner")
        return [getattr(self, name) for name in names] + [getattr(self, name + "_core") for name in names]


class Sum(Held):
    def __init__(self, moves, mine, other):
        super().__init__(moves)
        self.mine, self.theirs = mine, other
        self.low, self.high = slice(0, self.half), slice(self.half, None)

    def both(self, copies, part):
        return self.mine[copies, part] + self.got[copies, part]

    def core(self):
        self.bring(got=self.moves.core(self.theirs))

    def first(self):
        self.bring(
            from_x=self.moves.across(self.both(slice(2, 4), self.low), 1),
            from_y=self.moves.across(self.both(slice(1, 3), self.high), 2),
        )

    def second(self):
        self.bring(
            low2=self.moves.across(self.both(1, self.low) + self.from_x[0], 2),
            high1=self.moves.across(self.both(3, self.high) + self.from_y[1], 1),
        )

    def halves(self):
        low = self.both(0, self.low) + self.from_x[1] + self.low2
        high = self.both(0, self.high) + self.from_y[0] + self.high1
        return low, high

    def once(self):
        low, high = self.halves()
        self.block = low[0]
        blocks = [low[i] for i in range(1, self.half)] + [high[i] for i in range(self.half)]
        self.bring(**{"z%d" % (i + 1): self.moves.along(block, i + 1) for i, block in enumerate(blocks)})

    def far(self):
        self.block, high = self.halves()
        self.bring(z=self.moves.along(high, 2))

    def near(self):
        pair = self.block + self.z
        self.block = pair[0]
        self.bring(z1=self.moves.along(pair[1], 1))

    def total(self):
        total = self.block.astype(jnp.float32)
        for i in range(1, self.moves.lines):
            if hasattr(self, "z%d" % i):
                total = total + getattr(self, "z%d" % i).astype(jnp.float32)
        return total.astype(jnp.bfloat16)


class Share(Held):
    def __init__(self, moves, part, axis):
        super().__init__(moves)
        self.part, self.axis = part, axis

    def first(self):
        self.bring(near=self.moves.across(self.part, self.axis))

    def second(self):
        self.bring(far=self.moves.across(jnp.stack([self.part, self.near]), 3 - self.axis))

    def parts(self):
        near, far = (self.near[None], 0), (self.far, 0)
        return [(self.part[None], 0)] + ([near, far] if self.axis == 1 else [far, near]) + [(self.far, 1)]


class SumAll(Held):
    def __init__(self, moves, value):
        super().__init__(moves)
        self.value = value
        self.steps = [(axis, 2**k) for axis in ("fsdp", "dp") for k in range((lax.axis_size(axis) - 1).bit_length())]

    def step(self):
        axis, bit = self.steps.pop(0)
        count = lax.axis_size(axis)
        got = lax.ppermute(self.value, axis, [(i, i ^ bit) for i in range(count)])
        self.bring(value=self.value + got)


def blocked_shards(
    tokens, image_counts, skip_mask, norm1_gain, norm1_bias, token_in, token_in_bias, token_out,
    token_out_bias, norm2_gain, norm2_bias, channel_in, channel_in_bias, channel_out,
    channel_out_bias, cotangent,
):
    f32, bf16 = jnp.float32, jnp.bfloat16
    slots, patches, width = tokens.shape
    layers, in_rows, hidden = channel_in.shape
    keys = token_out.shape[1]
    moves = Moves()
    shards_count = 2 * moves.lines
    inner = keys * shards_count
    rows = -(-patches // 16) * 16
    place = jnp.stack([moves.z, moves.c, moves.q]).astype(jnp.int32)
    kernels = Kernels(place, slots, rows, width, inner, hidden, moves.lines, in_rows)
    wide = kernels.wide

    live = (jnp.arange(slots, dtype=jnp.int32) < image_counts[0]).astype(f32)
    scale = live[:, None, None] * skip_mask.astype(f32)

    def padded(images):
        return jnp.pad(images, ((0, 0), (0, rows - patches), (0, 0)))

    def quarter(array, axis):
        size = array.shape[axis] // 4
        return lax.dynamic_slice_in_dim(array, moves.q * size, size, axis)

    def widen(array):
        return jnp.pad(array, ((0, 0), (0, 0), (0, wide - array.shape[2])))

    gap = jnp.zeros((layers, keys, rows - patches), bf16)
    with_bias = jnp.concatenate([jnp.swapaxes(token_in, 1, 2), gap, token_in_bias[:, :, None]], 2)
    vectors = jnp.stack([norm1_gain, norm1_bias, norm2_gain, norm2_bias, channel_out_bias], 1)
    biases = jnp.pad(channel_in_bias, ((0, 0), (0, 2 * wide - channel_in_bias.shape[1])))
    vectors = jnp.concatenate([widen(vectors), biases.reshape(layers, 2, wide)], 1)
    extra = 16
    vectors = jnp.pad(vectors, ((0, 0), (0, extra - vectors.shape[1]), (0, 0)))
    vectors = jnp.pad(vectors, ((0, 0), (0, keys - extra), (0, 0)))
    packs = jnp.concatenate([widen(with_bias), widen(token_out), vectors], 2).reshape(layers * keys, width)
    b_outs = jnp.pad(token_out_bias.astype(f32), ((0, 0), (0, wide - patches)))[:, :, None]
    scale = scale.reshape(slots, 2 * layers)

    def both(layer):
        return jnp.stack([quarter(channel_in[layer], 1), quarter(channel_out[layer], 0)])

    first, last = Gather(moves, both(0)), Gather(moves, both(1))
    small = Gather(moves, packs)
    shards_held = Held(moves)
    first.direct()
    shards_held.bring(ins=moves.core(channel_in), outs=moves.core(channel_out))
    small.part, last.part = settle((first, shards_held), small.part, last.part)
    first.join()

    def weights(gather):
        return [channel_in, channel_out, shards_held.ins, shards_held.outs] + gather.whole()

    first.first()
    began, first.fresh = first.fresh, []
    first.core("line")
    small.direct()
    (last.part, first.line) = settle((first, small), last.part, first.line)
    first.fresh = began
    small.line = jnp.stack([small.part, small.z1, small.z2, small.z3])
    small.core("line")
    last.direct()
    last.fresh = ["z1"]
    settle((first, small, last))
    first.second()
    found = kernels.unpack_small(small.line, small.line_core, layers, shards_count, extra)
    x0 = padded(tokens)
    (w_in0, w_in_t0, w_out0, w_out_t0, gain1_0, shift1_0, gain2_0, shift2_0, b_cout0, b_cin0) = found[0]
    (w_in1, w_in_t1, w_out1, w_out_t1, gain1_1, shift1_1, gain2_1, shift2_1, b_cout1, b_cin1) = found[1]

    u0, h0, d0, mid0, v0 = kernels.token_forward(
        scale, x0, b_outs, (gain1_0, shift1_0, w_in0, w_out_t0, gain2_0, shift2_0), 0
    )
    last.fresh = ["z2"]
    (v0,) = settle((first, last), v0)
    first.core("x", "y")
    first.corner_core()
    last.fresh = ["z3"]
    (v0,) = settle((first, last), v0)

    last.join()
    last.first()
    hid0, slope0, x1 = kernels.first_forward(scale, v0, mid0, b_cin0, b_cout0, weights(first))
    (x1,) = settle((last,), x1)

    last.second()
    last.core("line", "x", "y")
    u1, h1, d1, mid1, v1 = kernels.token_forward(
        scale, x1, b_outs, (gain1_1, shift1_1, w_in1, w_out_t1, gain2_1, shift2_1), 1
    )
    (v1,) = settle((last,), v1)
    last.corner_core()
    grad2 = padded(cotangent)
    hid1, slope1, mine, theirs, low1, g_cout1 = kernels.last_hidden(scale, v1, b_cin1, grad2, weights(last))
    mine, theirs, low1 = settle((last,), mine, theirs, low1)

    sum_out1 = Sum(moves, mine, theirs)
    sum_out1.core()
    mine, theirs, back, g_cin1 = kernels.channel_backward(low1, v1, slope1, weights(last), 1)
    mine, theirs, back = settle((sum_out1,), mine, theirs, back)

    sum_in1 = Sum(moves, mine, theirs)
    sum_in1.core()
    sum_out1.first()
    grads1 = kernels.token_backward(
        scale, grad2, back, (mid1, x1, u1, h1, d1), (w_in_t1, w_out1, gain1_1, gain2_1), g_cout1, g_cin1, keys
    )
    grad1, *tokens1, vector1, low0, g_cout0 = settle((sum_out1, sum_in1), *grads1)

    sum_out1.second()
    sum_in1.first()
    mine, theirs = kernels.out_weight_grad(low0, hid0)
    mine, theirs = settle((sum_out1, sum_in1), mine, theirs)

    sum_out0 = Sum(moves, mine, theirs)
    sum_out0.core()
    sum_in1.second()
    sum_out1.far()
    *blocks, back, g_cin0 = kernels.channel_backward(low0, v0, slope0, weights(first), 0, 16)
    *blocks, back = settle((sum_out1, sum_in1, sum_out0), *blocks, back)

    sum_out0.first()
    sum_in1.far()
    sum_out1.near()
    grad0, mine, theirs, vector = kernels.token_backward(
        scale, grad1, back, (mid0, x0, u0, h0, d0), (w_in_t0, w_out0, gain1_0, gain2_0), g_cout0, g_cin0, keys,
        (*tokens1, vector1), blocks,
    )
    hid1, grad0, mine, theirs, vector = settle((sum_out1, sum_in1, sum_out0), hid1, grad0, mine, theirs, vector)

    sum_in0 = Sum(moves, mine, theirs)
    sum_in0.core()
    sum_out0.second()
    sum_in1.near()
    vector_sum = SumAll(moves, vector)
    vector_sum.step()
    output = kernels.out_forward(scale, hid1, mid1, b_cout1, weights(last), 1, bf16)
    (output,) = settle((sum_in0, sum_out0, sum_in1, vector_sum), output)
    output = output[:, :patches]
    input_grad = grad0[:, :patches]

    sum_in0.first()
    sum_out0.far()
    vector_sum.step()
    share_out1 = Share(moves, sum_out1.total(), 1)
    share_out1.first()
    settle((sum_in0, sum_out0, share_out1, vector_sum))

    sum_in0.second()
    sum_out0.near()
    vector_sum.step()
    share_in1 = Share(moves, sum_in1.total(), 2)
    share_in1.first()
    share_out1.second()
    settle((sum_in0, sum_out0, share_in1, share_out1, vector_sum))

    sum_in0.once()
    share_in1.second()
    share_out0 = Share(moves, sum_out0.total(), 1)
    share_out0.first()
    vector_sum.step()
    settle((sum_in0, share_in1, share_out0, vector_sum))

    total = sum_in0.total()
    vector_sum.step()
    share_out0.second()
    near = [moves.across(total, bits) for bits in (1, 2, 3)]
    (done_in,) = kernels.finish_in(share_in1.parts(), 1, layers)
    (done_out,) = kernels.finish_out(share_out1.parts(), 1, layers)
    done_in, done_out, *near = settle((share_out0, vector_sum), done_in, done_out, *near)
    (grad_out,) = kernels.finish_out(share_out0.parts(), 0, layers, (done_out,))
    parts = [(part[None], 0) for part in [total] + near]
    grad_in, near = kernels.finish_in(parts, 0, layers, keys, (done_in,))

    near = near.reshape(layers, 2, keys, wide)
    grad_t_in = jnp.swapaxes(near[:, 0, :, :patches], 1, 2)
    grad_b_in = near[:, 0, :, rows]
    grad_t_out = near[:, 1, :, :patches]
    sums = vector_sum.value.reshape(layers, 16, width)
    me = lax.axis_index("fsdp")

    def owned(row):
        size = width // shards_count
        return lax.dynamic_slice_in_dim(sums[:, row], me * size, size, 1)

    grad_gain1, grad_shift1, grad_gain2, grad_shift2, grad_b_cout = [owned(row) for row in range(5)]
    size = hidden // shards_count
    grad_b_cin = lax.dynamic_slice(sums, (0, 8 + me // 2, (me % 2) * size), (layers, 1, size))[:, 0]
    bias_total = sums[:, 5, :patches]
    return (
        output, input_grad, grad_gain1, grad_shift1, grad_t_in, grad_b_in, grad_t_out, bias_total,
        grad_gain2, grad_shift2, grad_in, grad_b_cin, grad_out, grad_b_cout,
    )


def fits(mesh):
    return mesh.shape["dp"] == 4 and mesh.shape["fsdp"] == 8


def solution(mesh):
    in_specs = (
        P(("dp", "fsdp"), None, None),
        P(("dp", "fsdp")),
        P(("dp", "fsdp"), None, None),
        P(None, "fsdp"),
        P(None, "fsdp"),
        P(None, None, "fsdp"),
        P(None, "fsdp"),
        P(None, "fsdp", None),
        P(),
        P(None, "fsdp"),
        P(None, "fsdp"),
        P(None, "fsdp", None),
        P(None, "fsdp"),
        P(None, "fsdp", None),
        P(None, "fsdp"),
        P(("dp", "fsdp"), None, None),
    )
    out_specs = (
        P(("dp", "fsdp"), None, None),
        P(("dp", "fsdp"), None, None),
        P(None, "fsdp"),
        P(None, "fsdp"),
        P(None, None, "fsdp"),
        P(None, "fsdp"),
        P(None, "fsdp", None),
        P(),
        P(None, "fsdp"),
        P(None, "fsdp"),
        P(None, "fsdp", None),
        P(None, "fsdp"),
        P(None, "fsdp", None),
        P(None, "fsdp"),
    )
    program = blocked_shards if fits(mesh) else shards
    return jax.shard_map(program, mesh=mesh, in_specs=in_specs, out_specs=out_specs, check_vma=False)
```

```python
import functools
import math

import jax
import jax.numpy as jnp
from jax import lax
from jax.experimental import pallas as pl
from jax.experimental.pallas import tpu as pltpu
from jax.sharding import PartitionSpec as P

EPSILON = 1e-06
GELU_A = math.sqrt(2.0 / math.pi)
GELU_B = 0.044715 * GELU_A
IMAGES = 2
VMEM_BYTES = 60 * 2**20


def as_sent(shard):

    def short(part):
        return part.astype(jnp.bfloat16) if part.dtype == jnp.float32 else part

    return jax.tree.map(short, shard)


def layer_norm(values, gain, shift):
    center = values - jnp.mean(values, -1, keepdims=True)
    inv_std = lax.rsqrt(jnp.mean(center * center, -1, keepdims=True) + EPSILON)
    normed = center * inv_std
    return (normed * gain + shift, normed, inv_std)


def norm_back(grad_out, normed, inv_std, gain):
    grad_gain = jnp.sum(grad_out * normed, axis=(0, 1))
    grad_shift = jnp.sum(grad_out, axis=(0, 1))
    scaled = grad_out * gain
    grad_in = inv_std * (
        scaled
        - jnp.mean(scaled, -1, keepdims=True)
        - normed * jnp.mean(scaled * normed, -1, keepdims=True)
    )
    return (grad_in, grad_gain, grad_shift)


def gelu_back(pre_act, grad_out):
    return jax.vjp(jax.nn.gelu, pre_act)[1](grad_out)[0]


def fetch_forward(pieces):
    return (
        lax.all_gather(pieces[0], "fsdp", axis=0, tiled=True),
        lax.all_gather(pieces[1], "fsdp", axis=0, tiled=True),
        lax.all_gather(pieces[2], "fsdp", axis=1, tiled=True),
        lax.all_gather(pieces[3], "fsdp", axis=0, tiled=True),
        lax.all_gather(pieces[4], "fsdp", axis=0, tiled=True),
        lax.all_gather(pieces[5], "fsdp", axis=0, tiled=True),
        lax.all_gather(pieces[6], "fsdp", axis=0, tiled=True),
        lax.all_gather(pieces[7], "fsdp", axis=0, tiled=True),
        lax.all_gather(pieces[8], "fsdp", axis=0, tiled=True),
        lax.all_gather(pieces[9], "fsdp", axis=0, tiled=True),
        lax.all_gather(pieces[10], "fsdp", axis=0, tiled=True),
    )


def fetch_backward(pieces):
    return (
        lax.all_gather(pieces[0], "fsdp", axis=0, tiled=True),
        lax.all_gather(pieces[1], "fsdp", axis=0, tiled=True),
        lax.all_gather(pieces[2], "fsdp", axis=1, tiled=True),
        lax.all_gather(pieces[3], "fsdp", axis=0, tiled=True),
        lax.all_gather(pieces[4], "fsdp", axis=0, tiled=True),
        lax.all_gather(pieces[5], "fsdp", axis=0, tiled=True),
        lax.all_gather(pieces[6], "fsdp", axis=0, tiled=True),
        lax.all_gather(pieces[7], "fsdp", axis=0, tiled=True),
        lax.all_gather(pieces[8], "fsdp", axis=0, tiled=True),
        lax.all_gather(pieces[9], "fsdp", axis=0, tiled=True),
        lax.all_gather(pieces[10], "fsdp", axis=0, tiled=True),
    )


def shards(
    tokens,
    image_counts,
    skip_mask,
    norm1_gain,
    norm1_bias,
    token_in,
    token_in_bias,
    token_out,
    token_out_bias,
    norm2_gain,
    norm2_bias,
    channel_in,
    channel_in_bias,
    channel_out,
    channel_out_bias,
    cotangent,
):
    f32 = jnp.float32
    bf16 = jnp.bfloat16
    slots = tokens.shape[0]
    layers = norm1_gain.shape[0]
    live = (jnp.arange(slots, dtype=jnp.int32) < image_counts[0]).astype(f32)
    branch_scale = live[:, None, None] * skip_mask.astype(f32)

    def layer_pieces(index):
        return (
            norm1_gain[index],
            norm1_bias[index],
            token_in[index],
            token_in_bias[index],
            token_out[index],
            norm2_gain[index],
            norm2_bias[index],
            channel_in[index],
            channel_in_bias[index],
            channel_out[index],
            channel_out_bias[index],
        )

    values = tokens.astype(f32)
    saved = []
    kept_weights = []
    for index in range(layers):
        weights = fetch_forward(layer_pieces(index))
        kept_weights.append(weights)
        gain1, shift1, w_tin, b_tin, w_tout, gain2, shift2, w_cin, b_cin, w_cout, b_cout = weights
        tok_bias = token_out_bias[index].astype(f32)
        normed1, plain1, inv1 = layer_norm(values, gain1.astype(f32), shift1.astype(f32))
        normed1 = normed1.astype(bf16)
        pre_tok = jnp.einsum(
            "isd,sk->idk", normed1, w_tin, preferred_element_type=f32
        ) + b_tin.astype(f32)
        hidden1 = jax.nn.gelu(pre_tok).astype(bf16)
        branch = (
            jnp.einsum("idk,ks->isd", hidden1, w_tout, preferred_element_type=f32)
            + tok_bias[None, :, None]
        )
        middle = values + branch_scale[:, index, 0][:, None, None] * branch
        normed2, plain2, inv2 = layer_norm(middle, gain2.astype(f32), shift2.astype(f32))
        normed2 = normed2.astype(bf16)
        pre_chan = jnp.einsum(
            "isd,df->isf", normed2, w_cin, preferred_element_type=f32
        ) + b_cin.astype(f32)
        hidden2 = jax.nn.gelu(pre_chan).astype(bf16)
        branch = jnp.einsum(
            "isf,fd->isd", hidden2, w_cout, preferred_element_type=f32
        ) + b_cout.astype(f32)
        values = middle + branch_scale[:, index, 1][:, None, None] * branch
        saved.append(
            (normed1, plain1, inv1, pre_tok, hidden1, normed2, plain2, inv2, pre_chan, hidden2)
        )
    output = values.astype(bf16)
    grad = cotangent.astype(f32)
    local_grads = [None] * layers
    bias_grads = [None] * layers
    for index in reversed(range(layers)):
        weights = fetch_backward(layer_pieces(index))
        gain1, shift1, w_tin, b_tin, w_tout, gain2, shift2, w_cin, b_cin, w_cout, b_cout = weights
        normed1, plain1, inv1, pre_tok, hidden1, normed2, plain2, inv2, pre_chan, hidden2 = saved[
            index
        ]
        out_chan = branch_scale[:, index, 1][:, None, None] * grad
        grad_b_cout = jnp.sum(out_chan, axis=(0, 1))
        low_chan = out_chan.astype(bf16)
        grad_w_cout = jnp.einsum("isf,isd->fd", hidden2, low_chan, preferred_element_type=f32)
        back_hidden = jnp.einsum("isd,fd->isf", low_chan, w_cout, preferred_element_type=f32)
        pre_grad = gelu_back(pre_chan, back_hidden)
        grad_b_cin = jnp.sum(pre_grad, axis=(0, 1))
        low_pre = pre_grad.astype(bf16)
        grad_w_cin = jnp.einsum("isd,isf->df", normed2, low_pre, preferred_element_type=f32)
        back_norm = jnp.einsum("isf,df->isd", low_pre, w_cin, preferred_element_type=f32)
        norm_in, grad_gain2, grad_shift2 = norm_back(back_norm, plain2, inv2, gain2.astype(f32))
        grad_mid = grad + norm_in
        out_tok = branch_scale[:, index, 0][:, None, None] * grad_mid
        bias_grads[index] = jnp.sum(out_tok, axis=(0, 2))
        low_tok = out_tok.astype(bf16)
        grad_w_tout = jnp.einsum("idk,isd->ks", hidden1, low_tok, preferred_element_type=f32)
        back_hidden = jnp.einsum("isd,ks->idk", low_tok, w_tout, preferred_element_type=f32)
        pre_grad = gelu_back(pre_tok, back_hidden)
        grad_b_tin = jnp.sum(pre_grad, axis=(0, 1))
        low_pre = pre_grad.astype(bf16)
        grad_w_tin = jnp.einsum("isd,idk->sk", normed1, low_pre, preferred_element_type=f32)
        back_norm = jnp.einsum("idk,sk->isd", low_pre, w_tin, preferred_element_type=f32)
        norm_in, grad_gain1, grad_shift1 = norm_back(back_norm, plain1, inv1, gain1.astype(f32))
        grad = grad_mid + norm_in
        local = (
            grad_gain1,
            grad_shift1,
            grad_w_tin,
            grad_b_tin,
            grad_w_tout,
            grad_gain2,
            grad_shift2,
            grad_w_cin,
            grad_b_cin,
            grad_w_cout,
            grad_b_cout,
        )
        local_grads[index] = local
    token_bias_total = lax.psum(jnp.stack(bias_grads), ("dp", "fsdp"))
    joined = tuple(
        (
            jnp.stack([local_grads[index][position] for index in range(layers)])
            for position in range(11)
        )
    )
    owned = (
        lax.psum_scatter(joined[0], "fsdp", scatter_dimension=1, tiled=True),
        lax.psum_scatter(joined[1], "fsdp", scatter_dimension=1, tiled=True),
        lax.psum_scatter(joined[2], "fsdp", scatter_dimension=2, tiled=True),
        lax.psum_scatter(joined[3], "fsdp", scatter_dimension=1, tiled=True),
        lax.psum_scatter(joined[4], "fsdp", scatter_dimension=1, tiled=True),
        lax.psum_scatter(joined[5], "fsdp", scatter_dimension=1, tiled=True),
        lax.psum_scatter(joined[6], "fsdp", scatter_dimension=1, tiled=True),
        lax.psum_scatter(joined[7], "fsdp", scatter_dimension=1, tiled=True),
        lax.psum_scatter(joined[8], "fsdp", scatter_dimension=1, tiled=True),
        lax.psum_scatter(joined[9], "fsdp", scatter_dimension=1, tiled=True),
        lax.psum_scatter(joined[10], "fsdp", scatter_dimension=1, tiled=True),
    )
    results = jax.tree.map(lambda part: part.astype(jnp.float32), lax.psum(as_sent(owned), "dp"))
    return (
        output,
        grad,
        results[0],
        results[1],
        results[2],
        results[3],
        results[4],
        token_bias_total,
        results[5],
        results[6],
        results[7],
        results[8],
        results[9],
        results[10],
    )


def norm_parts(values):
    center = values - jnp.mean(values, -1, keepdims=True)
    inv_std = lax.rsqrt(jnp.mean(center * center, -1, keepdims=True) + EPSILON)
    return center * inv_std, inv_std


def norm_input_grad(grad, normed, inv_std):
    return inv_std * (
        grad
        - jnp.mean(grad, -1, keepdims=True)
        - normed * jnp.mean(grad * normed, -1, keepdims=True)
    )


def gelu_pair(value):
    square = value * value
    gate = 0.5 + 0.5 * jnp.tanh(value * (GELU_A + GELU_B * square))
    result = value * gate
    slope = gate + result * (1.0 - gate) * (2.0 * GELU_A + 6.0 * GELU_B * square)
    return result.astype(jnp.bfloat16), slope.astype(jnp.bfloat16)


def dot(left, right, left_dim, right_dim):
    return lax.dot_general(
        left, right, (((left_dim,), (right_dim,)), ((), ())), preferred_element_type=jnp.float32
    )


def chunks(size, count):
    return [slice(k * size // count, (k + 1) * size // count) for k in range(count)]


def position(copy):
    odd = copy & 1
    return 2 * odd + (odd ^ (copy >> 1))


def staggered(parts, product, finish):
    held = product(parts[0])
    for k, part in enumerate(parts):
        later = product(parts[k + 1]) if k + 1 < len(parts) else None
        finish(part, held)
        held = later


def clear(first, *refs):
    @pl.when(first)
    def _():
        for ref in refs:
            ref[...] = jnp.zeros_like(ref)


def unpack_small(place, own, other, *refs):
    vectors = refs[-1]
    z, c = place[0], place[1]
    lines, rows, _ = own.shape
    layers, extra, wide = vectors.shape[1:]
    keys = rows // layers
    for layer in range(layers):
        w_in, w_in_t, w_out, w_out_t, *rest = refs[10 * layer : 10 * layer + 10]
        base = layer * keys
        for source, side in ((own, c), (other, 1 - c)):
            for i in range(lines):
                shard = 2 * (i ^ z) + side
                start = pl.multiple_of(shard * keys, keys)
                w_in[pl.ds(start, keys)] = source[i, base : base + keys, :wide]
                w_out[pl.ds(start, keys)] = source[i, base : base + keys, wide : 2 * wide]
                vectors[shard, layer] = source[i, base : base + extra, 2 * wide :]
        w_in_t[...] = w_in[...].T
        w_out_t[...] = w_out[...].T
        held = [vectors[shard, layer].astype(jnp.float32) for shard in range(vectors.shape[0])]
        for row, target in enumerate(rest[:5]):
            size = target.shape[1] // len(held)
            target[...] = jnp.concatenate([part[row : row + 1, :size] for part in held], axis=1)
        biases = rest[5]
        size = biases.shape[1] // len(held)
        for shard, part in enumerate(held):
            whole = jnp.concatenate([part[5:6], part[6:7]], axis=1)
            biases[:, shard * size : (shard + 1) * size] = whole[:, :size]


def token_branch(values, scale, small, b_out, u_out, hidden_out, slope_out):
    gain1, shift1, w_in, w_out, gain2, shift2 = small
    rows, wide = values.shape[0], w_in.shape[1]
    normed, _ = norm_parts(values)
    u_out[:rows] = (normed * gain1[...] + shift1[...]).astype(jnp.bfloat16)
    below = lax.broadcasted_iota(jnp.int32, (wide - rows, values.shape[1]), 0)
    u_out[rows:] = jnp.where(below == 0, 1.0, 0.0).astype(jnp.bfloat16)
    hidden, slope = gelu_pair(dot(w_in[...], u_out[...], 1, 0))
    hidden_out[...] = hidden
    slope_out[...] = slope
    middle = values + scale * (dot(w_out[:rows], hidden, 1, 0) + b_out[0, :rows])
    normed, _ = norm_parts(middle)
    return middle, (normed * gain2[...] + shift2[...]).astype(jnp.bfloat16)


def token_forward(place, scale, x, b_out, *rest, layer):
    small, (u_out, hidden_out, slope_out, middle_out, v_out) = rest[:6], rest[6:]
    count, rows = x.shape[:2]
    for k in range(count):
        part = scale[count * pl.program_id(0) + k, 2 * layer]
        middle, v = token_branch(
            x[k].astype(jnp.float32), part, small, b_out, u_out.at[k], hidden_out.at[k], slope_out.at[k]
        )
        middle_out[k] = middle
        v_out[k * rows : (k + 1) * rows] = v


def token_grads(scale, grad, back_v, middle, x, u, hidden, slope, w_in, w_out, gain1, gain2, padded):
    rows, width = grad.shape
    normed, inv_std = norm_parts(middle)
    moved = back_v * normed
    sums = [jnp.sum(moved, 0, keepdims=True), jnp.sum(back_v, 0, keepdims=True)]
    grad_mid = grad + norm_input_grad(back_v * gain2[...], normed, inv_std)
    padded[:rows] = (scale * grad_mid).astype(jnp.bfloat16)
    low = padded[...]
    b_out = dot(jnp.ones((8, width), jnp.bfloat16), low, 1, 1)[:1]
    w_out_grad = dot(hidden, low, 1, 1)
    pre = (dot(w_out[...], low, 1, 0) * slope.astype(jnp.float32)).astype(jnp.bfloat16)
    w_in_grad = dot(pre, u, 1, 1)
    back = dot(w_in[:rows], pre, 1, 0)
    normed, inv_std = norm_parts(x)
    sums = [jnp.sum(back * normed, 0, keepdims=True), jnp.sum(back, 0, keepdims=True)] + sums
    return grad_mid + norm_input_grad(back * gain1[...], normed, inv_std), sums, b_out, w_in_grad, w_out_grad


def token_blocks(place, w_in_grad, w_out_grad, whole, put):
    z, c = place[0], place[1]
    keys = whole.shape[1] // 8
    for which, total in ((0, w_in_grad), (1, w_out_grad)):
        whole[which] = total[...].astype(jnp.bfloat16)
        for i in range(4):
            for side, core in ((0, c), (1, 1 - c)):
                start = pl.multiple_of((2 * (i ^ z) + core) * keys, keys)
                put(which, i, side, whole[which, pl.ds(start, keys)])


def token_backward(place, scale, grad, back_v, middle, x, u, hidden, slope, w_in, w_out, gain1, gain2, *rest):
    image = pl.program_id(0)
    g_cout, g_cin = rest[:2]
    last = len(rest) == 2 + 6 + 4
    if last:
        grad_out, mine_out, other_out, vector, low_out, above_grad = rest[2:8]
        layer = 1
    else:
        earlier, grad_out, mine_out, other_out, vector = rest[2:5], *rest[5:9]
        layer = 0
    padded, w_in_grad, w_out_grad, whole = rest[-4:]
    count, rows = x.shape[:2]
    first = image == 0
    clear(first, padded, vector, w_in_grad, w_out_grad)

    @pl.when(first)
    def _():
        vector[4:5] = g_cout[...]
        for j in range(g_cin.shape[0]):
            vector[8 + j : 9 + j] = g_cin[j]
        if not last:
            vector[16:] = earlier[2][...]

    if last:
        clear(first, above_grad)
    found = []
    for k in range(count):
        part = slice(k * rows, (k + 1) * rows)
        result, *sums = token_grads(
            scale[count * image + k, 2 * layer], grad[k].astype(jnp.float32), back_v[part], middle[k],
            x[k].astype(jnp.float32), u[k], hidden[k], slope[k], w_in, w_out, gain1, gain2, padded.at[k],
        )
        grad_out[k] = result
        if last:
            out = scale[count * image + k, 1] * result
            above_grad[...] += jnp.sum(out, 0, keepdims=True)
            low_out[part] = out.astype(jnp.bfloat16)
        found.append(sums)
    for k in range(4):
        vector[k : k + 1] += sum(sums[0][k] for sums in found)
    vector[5:6, : padded.shape[1]] += sum(sums[1] for sums in found)
    w_in_grad[...] += sum(sums[2] for sums in found)
    w_out_grad[...] += sum(sums[3] for sums in found)

    @pl.when(image == pl.num_programs(0) - 1)
    def _():
        targets = (mine_out, other_out)

        def put(which, i, side, part):
            targets[side][i, which] = part

        if not last:
            for side in range(2):
                targets[side][:, 2:] = earlier[side][...]
        token_blocks(place, w_in_grad, w_out_grad, whole, put)


def out_weight_grad(place, low, hidden, mine_out, other_out, turned, whole):
    @pl.when(pl.program_id(0) == 0)
    def _():
        turned[...] = low[...].T

    out_blocks(place, turned, hidden[0], mine_out, other_out, whole)


class Weight:
    def __init__(self, refs, which):
        self.which = which
        self.shards, self.parts = (refs[which], refs[2 + which]), (refs[4 : 4 + 4], refs[8:12])

    def blocks(self, copy, i):
        for side, (line, from_x, from_y, corner) in enumerate(self.parts):
            yield side, (line, from_x, from_y, corner)[copy].at[i - 1, self.which], 0


def fetch_in(place, layer, weight, target, sem):
    z, c, q = place[0], place[1], place[2]
    copies, _, columns = target.shape
    rows = weight.shards[0].shape[1]
    for copy in range(copies):
        j = copy ^ q

        def put(ref, i, side, first):
            start = pl.multiple_of((2 * (i ^ z) + (c ^ side)) * rows + first, 16)
            goal = target.at[j, pl.ds(start, ref.shape[0])]
            pltpu.make_async_copy(ref, goal, sem.at[j]).start()

        for side, shard in enumerate(weight.shards):
            put(shard.at[layer, :, pl.ds(pl.multiple_of(j * columns, columns), columns)], 0, side, 0)
        for i in range(1, copies):
            for side, ref, first in weight.blocks(copy, i):
                put(ref, i, side, first)


def fetch_out(place, layer, weight, target, sem):
    z, c, q = place[0], place[1], place[2]
    lines, part, _ = target.shape
    for i in range(lines):

        def put(ref, start):
            goal = target.at[i ^ z, pl.ds(pl.multiple_of(start, 16), ref.shape[0])]
            pltpu.make_async_copy(ref, goal, sem.at[i ^ z]).start()

        if i == 0:
            for side, shard in enumerate(weight.shards):
                put(shard.at[layer], (c ^ side) * (part // 2))
            continue
        for copy in range(4):
            for side, ref, first in weight.blocks(copy, i):
                put(ref, (c ^ side) * (part // 2) + (copy ^ q) * (part // 8) + first)


def arrive(weight, sem, step):
    pltpu.make_async_copy(weight.at[step], weight.at[step], sem.at[step]).wait()


def out_blocks(place, turned, hidden, mine_out, other_out, whole):
    c, q = place[1], place[2]
    whole[...] = dot(turned[...], hidden, 1, 0).astype(jnp.bfloat16)
    copies, _, rows, columns = mine_out.shape
    size = columns // 2
    for side, target in ((c, mine_out), (1 - c, other_out)):
        units = pl.ds(pl.multiple_of(side * size, 128), size)
        for j in range(copies):
            start = 2 * j * rows
            target[position(j ^ q), 0, :, :size] = whole[start : start + rows, units]
            target[position(j ^ q), 0, :, size:] = whole[start + rows : start + 2 * rows, units]


def first_forward(place, scale, v, middle, bias_in, bias_out, *rest):
    weight_in, weight_out = Weight(rest[:12], 0), Weight(rest[:12], 1)
    hidden_out, slope_out, x_out, w_in, w_out, hidden, total, sem_in, sem_out = rest[12:]
    step = pl.program_id(0)
    rows = middle.shape[1]

    @pl.when(step == 0)
    def _():
        fetch_in(place, 0, weight_in, w_in, sem_in)
        fetch_out(place, 0, weight_out, w_out, sem_out)
        total[...] = jnp.zeros_like(total)

    @pl.when(step < 4)
    def _():
        j = (step & 3) ^ place[2]
        arrive(w_in, sem_in, j)
        def product(part):
            return dot(v[part], w_in[j], 1, 0) + bias_in[...]

        def finish(part, found):
            value, slope = gelu_pair(found)
            hidden_out[0, part] = value
            hidden[j, part] = value
            slope_out[0, part] = slope

        staggered(chunks(v.shape[0], 4), product, finish)

    @pl.when(step >= 4)
    def _():
        j = (step & 3) ^ place[0]
        arrive(w_out, sem_out, j)
        total[...] += dot(hidden[j], w_out[j], 1, 0)

    @pl.when(step == 7)
    def _():
        for image in range(middle.shape[0]):
            branch = total[image * rows : (image + 1) * rows] + bias_out[...]
            x_out[image] = middle[image] + scale[image, 1] * branch


def last_hidden(place, scale, v, bias, grad, *rest):
    weight = Weight(rest[:12], 0)
    (
        hidden_out, slope_out, mine_out, other_out, low_out, bias_grad, w_in, hidden, turned, whole, sem,
    ) = rest[12:]
    step = pl.program_id(0)

    @pl.when(step == 0)
    def _():
        fetch_in(place, 1, weight, w_in, sem)
        rows = grad.shape[1]
        sums = 0.0
        for image in range(grad.shape[0]):
            out = scale[image, 3] * grad[image].astype(jnp.float32)
            sums = sums + jnp.sum(out, 0, keepdims=True)
            low_out[image * rows : (image + 1) * rows] = out.astype(jnp.bfloat16)
        bias_grad[...] = sums
        turned[...] = low_out[...].T

    @pl.when(step < 4)
    def _():
        j = (step & 3) ^ place[2]
        arrive(w_in, sem, j)
        def product(part):
            return dot(v[part], w_in[j], 1, 0) + bias[...]

        def finish(part, found):
            value, slope = gelu_pair(found)
            hidden_out[0, part] = value
            hidden[j, part] = value
            slope_out[0, part] = slope

        staggered(chunks(v.shape[0], 4), product, finish)

    @pl.when(step >= 4)
    def _():
        out_blocks(place, turned, hidden[(step & 3) ^ place[0]], mine_out, other_out, whole)


def out_forward(place, scale, hidden, middle, bias, *rest, layer):
    x_out, weight, total, sem = rest[12:]
    step = pl.program_id(0)

    @pl.when(step == 0)
    def _():
        fetch_out(place, layer, Weight(rest[:12], 1), weight, sem)
        total[...] = jnp.zeros_like(total)

    j = step ^ place[0]
    arrive(weight, sem, j)
    total[...] += dot(hidden[0], weight[j], 1, 0)

    @pl.when(step == pl.num_programs(0) - 1)
    def _():
        for image in range(middle.shape[0]):
            rows = middle.shape[1]
            branch = total[image * rows : (image + 1) * rows] + bias[...]
            x_out[image] = (middle[image] + scale[image, 2 * layer + 1] * branch).astype(x_out.dtype)


def channel_backward(place, low, v, slope, *rest, layer):
    mine, theirs, back_out, bias_grad, w_out, w_in, turned, pre, whole, sem_out, sem_in = rest[12:]
    z, c = place[0], place[1]
    step = pl.program_id(0)

    @pl.when(step == 0)
    def _():
        fetch_out(place, layer, Weight(rest[:12], 1), w_out, sem_out)
        fetch_in(place, layer, Weight(rest[:12], 0), w_in, sem_in)
        turned[...] = v[...].T
        back_out[...] = jnp.zeros_like(back_out)

    j = step ^ z
    arrive(w_out, sem_out, j)
    arrive(w_in, sem_in, j)
    sums = []

    def product(part):
        return dot(low[part], w_out[j], 1, 1)

    def finish(part, found):
        grad = found * slope[0, part].astype(jnp.float32)
        sums.append(jnp.sum(grad, 0, keepdims=True))
        pre[part] = grad.astype(jnp.bfloat16)

    staggered(chunks(low.shape[0], 4), product, finish)
    bias_grad[0] = sum(sums)
    for part in chunks(turned.shape[0], 3):
        whole[part] = dot(turned[part], pre[...], 1, 0).astype(jnp.bfloat16)
    lines = mine.shape[1]
    rows = whole.shape[0] // (2 * lines)
    for i in range(lines):
        for side, target in ((c, mine), (1 - c, theirs)):
            start = pl.multiple_of((2 * (i ^ z) + side) * rows, rows)
            target[0, i] = whole[pl.ds(start, rows)]
    back_out[...] += dot(pre[...], w_in[j], 1, 1)


def finish_out(place, *refs):
    parts, out, whole = refs[:4], refs[-2], refs[-1]
    for j in range(4):
        rows, columns = parts[j].shape[1:]
        for half in range(2):
            start = pl.multiple_of((2 * (j ^ place[2]) + half) * rows, rows)
            part = parts[j][0, :, half * columns // 2 : (half + 1) * columns // 2]
            whole[pl.ds(start, rows)] = part.astype(jnp.float32)
    out[0] = whole[...].T


def finish_in(place, *refs):
    parts, out = refs[:4], refs[-1]
    for j in range(4):
        columns = parts[j].shape[2]
        start = pl.multiple_of((j ^ place[2]) * columns, columns)
        out[0, :, pl.ds(start, columns)] = parts[j][0].astype(jnp.float32)


class Kernels:
    def __init__(self, place, slots, rows, width, inner, hidden, lines, block):
        self.place = place
        self.slots, self.rows, self.width = slots, rows, width
        self.inner, self.hidden = inner, hidden
        self.lines, self.block = lines, block
        self.part = hidden // 4
        self.wide = 256

    def run(self, body, steps, inputs, outputs, scratch, flops, aliases=None, **fixed):
        sizes = sum(a.size * a.dtype.itemsize for a, _, _ in inputs)
        sizes += sum(math.prod(o[0]) * jnp.dtype(o[1]).itemsize for o in outputs)

        def spec(block, index):
            if isinstance(block, tuple):
                return pl.BlockSpec(block, index)
            return pl.BlockSpec(memory_space=block)

        return pl.pallas_call(
            functools.partial(body, **fixed) if fixed else body,
            name=body.__name__,
            grid_spec=pltpu.PrefetchScalarGridSpec(
                num_scalar_prefetch=1,
                grid=(steps,),
                in_specs=[spec(block, index) for _, block, index in inputs],
                out_specs=[spec(o[2], o[3]) for o in outputs],
                scratch_shapes=scratch,
            ),
            out_shape=[jax.ShapeDtypeStruct(o[0], o[1]) for o in outputs],
            input_output_aliases=aliases or {},
            compiler_params=pltpu.CompilerParams(
                dimension_semantics=("arbitrary",), vmem_limit_bytes=VMEM_BYTES
            ),
            cost_estimate=pl.CostEstimate(flops=flops, bytes_accessed=sizes, transcendentals=0),
        )(self.place, *[a for a, _, _ in inputs])

    def image(self, array):
        return (array, (1,) + array.shape[1:], lambda i, s: (i, 0, 0))

    def fixed(self, array):
        zeros = (0,) * array.ndim
        return (array, array.shape, lambda i, s: zeros)

    def scalars(self, array):
        return (array, pltpu.SMEM, None)

    def in_hbm(self, arrays):
        return [(a, pltpu.HBM, None) for a in arrays]

    def fixed_out(self, shape, dtype):
        zeros = (0,) * len(shape)
        return (shape, dtype, shape, lambda i, s: zeros)

    def columns(self, array, count):
        return (array, (array.shape[0], array.shape[1] // count), lambda i, s: (0, i))

    def columns_out(self, rows, columns, count, dtype):
        return ((rows, columns), dtype, (rows, columns // count), lambda i, s: (0, i))

    def late(self, step, start):
        return jnp.clip(step - start, 0, 3)

    def images_out(self, rows, dtype):
        block = (IMAGES, rows, self.width)
        return ((self.slots, rows, self.width), dtype, block, lambda i, s: (i, 0, 0))

    def images(self, array):
        return (array, (IMAGES,) + array.shape[1:], lambda i, s: (i, 0, 0))

    def rows_out(self):
        shape = (self.slots * self.rows, self.width)
        return (shape, jnp.bfloat16, (IMAGES * self.rows, self.width), lambda i, s: (i, 0))

    def quarters(self, array, which, start=0):
        return (array, (1,) + array.shape[1:], lambda i, s: (self.late(i, start) ^ s[which], 0, 0))

    def quarters_out(self, which, start=0):
        rows = self.slots * self.rows
        block = (1, rows, self.part)
        return ((4,) + block[1:], jnp.bfloat16, block, lambda i, s: (self.late(i, start) ^ s[which], 0, 0))

    def row(self, array, which, start=0):
        return (array, (1, self.part), lambda i, s: (0, self.late(i, start) ^ s[which]))

    def out_blocks_out(self, start=0):
        block = (4, 1, self.block, self.width)
        shape = (4, self.lines) + block[2:]
        return (shape, jnp.bfloat16, block, lambda i, s: (0, self.late(i, start), 0, 0))

    def product(self):
        return 2 * self.slots * self.rows * self.width * self.hidden

    def unpack_small(self, own, other, layers, shards, extra):
        bf16, f32 = jnp.bfloat16, jnp.float32
        inner, wide, width = self.inner, self.wide, self.width
        outputs = [((inner, wide), bf16), ((wide, inner), bf16)] * 2
        outputs += [((1, width), f32)] * 5 + [((1, self.hidden), f32)]
        found = self.run(
            unpack_small,
            1,
            [self.fixed(own), self.fixed(other)],
            [self.fixed_out(*part) for part in outputs * layers],
            [pltpu.VMEM((shards, layers, extra, wide), bf16)],
            0,
        )
        return [list(found[10 * layer : 10 * layer + 10]) for layer in range(layers)]

    def token_product(self):
        return 2 * self.slots * self.wide * self.width * self.inner

    def b_out(self, array, layer):
        return (array, (1,) + array.shape[1:], lambda i, s: (layer, 0, 0))

    def token_outs(self):
        bf16 = jnp.bfloat16
        outs = [self.images_out(rows, bf16) for rows in (self.wide, self.inner, self.inner)]
        return outs + [self.images_out(self.rows, jnp.float32), self.rows_out()]

    def token_forward(self, scale, x, b_out, small, layer):
        return self.run(
            token_forward,
            self.slots // IMAGES,
            [self.scalars(scale), self.images(x), self.b_out(b_out, layer)] + [self.fixed(a) for a in small],
            self.token_outs(),
            [],
            2 * self.token_product(),
            layer=layer,
        )

    def first_forward(self, scale, v, middle, bias_in, bias_out, weights):
        bf16, f32 = jnp.bfloat16, jnp.float32
        rows = self.slots * self.rows
        return self.run(
            first_forward,
            8,
            [self.scalars(scale), self.fixed(v), self.fixed(middle), self.row(bias_in, 2), self.fixed(bias_out)]
            + self.in_hbm(weights),
            [self.quarters_out(2)] * 2 + [self.fixed_out((self.slots, self.rows, self.width), f32)],
            [
                self.weight(),
                self.weight(),
                pltpu.VMEM((4, rows, self.part), bf16),
                pltpu.VMEM((rows, self.width), f32),
                pltpu.SemaphoreType.DMA((4,)),
                pltpu.SemaphoreType.DMA((4,)),
            ],
            2 * self.product(),
        )

    def last_hidden(self, scale, v, bias, grad, weights):
        bf16, f32 = jnp.bfloat16, jnp.float32
        rows = self.slots * self.rows
        return self.run(
            last_hidden,
            8,
            [self.scalars(scale), self.fixed(v), self.row(bias, 2), self.fixed(grad)] + self.in_hbm(weights),
            [self.quarters_out(2)] * 2
            + [self.out_blocks_out(4)] * 2
            + [self.fixed_out((rows, self.width), bf16), self.fixed_out((1, self.width), f32)],
            [
                self.weight(),
                pltpu.VMEM((4, rows, self.part), bf16),
                pltpu.VMEM((self.width, rows), bf16),
                pltpu.VMEM((self.width, self.part), bf16),
                pltpu.SemaphoreType.DMA((4,)),
            ],
            2 * self.product(),
        )

    def token_backward(self, scale, grad, back, kept, small, g_cout, g_cin, keys, earlier=()):
        bf16, f32 = jnp.bfloat16, jnp.float32
        width = self.width
        middle, x, u, hidden, slope = kept
        inputs = [self.scalars(scale), self.images(grad)]
        inputs += [(back, (IMAGES * self.rows, width), lambda i, s: (i, 0))]
        inputs += [self.images(a) for a in (middle, x, u, hidden, slope)]
        inputs += [self.fixed(a) for a in tuple(small) + (g_cout, g_cin) + tuple(earlier)]
        outputs = [self.images_out(self.rows, f32)]
        outputs += [self.fixed_out((self.lines, 4 if earlier else 2, keys, self.wide), bf16)] * 2
        outputs += [self.fixed_out((32 if earlier else 16, width), f32)]
        if not earlier:
            outputs += [self.rows_out(), self.fixed_out((1, width), f32)]
        return self.run(
            token_backward,
            self.slots // IMAGES,
            inputs,
            outputs,
            [
                pltpu.VMEM((IMAGES, self.wide, width), bf16),
                pltpu.VMEM((self.inner, self.wide), f32),
                pltpu.VMEM((self.inner, self.wide), f32),
                pltpu.VMEM((2, self.inner, self.wide), bf16),
            ],
            4 * self.token_product(),
        )

    def out_weight_grad(self, low, hidden):
        rows = self.slots * self.rows
        return self.run(
            out_weight_grad,
            4,
            [self.fixed(low), self.quarters(hidden, 0)],
            [self.out_blocks_out()] * 2,
            [pltpu.VMEM((self.width, rows), jnp.bfloat16), pltpu.VMEM((self.width, self.part), jnp.bfloat16)],
            self.product(),
        )

    def weight(self):
        return pltpu.VMEM((4, self.width, self.part), jnp.bfloat16)

    def out_forward(self, scale, hidden, middle, bias, weights, layer, dtype):
        return self.run(
            out_forward,
            4,
            [self.scalars(scale), self.quarters(hidden, 0), self.fixed(middle), self.fixed(bias)]
            + self.in_hbm(weights),
            [self.fixed_out(middle.shape, dtype)],
            [
                self.weight(),
                pltpu.VMEM((self.slots * self.rows, self.width), jnp.float32),
                pltpu.SemaphoreType.DMA((4,)),
            ],
            self.product(),
            layer=layer,
        )[0]

    def channel_backward(self, low, v, slope, weights, layer):
        bf16, f32 = jnp.bfloat16, jnp.float32
        rows = self.slots * self.rows
        block = (1, self.lines, self.block, self.width)
        shape = (4, self.lines, self.block, self.width)
        blocks = (shape, bf16, block, lambda j, s: (position(j ^ s[0] ^ s[2]), 0, 0, 0))
        return self.run(
            channel_backward,
            4,
            [self.fixed(low), self.fixed(v), self.quarters(slope, 0)]
            + self.in_hbm(weights),
            [
                blocks,
                blocks,
                self.fixed_out((rows, self.width), f32),
                ((4, 1, self.part), f32, (1, 1, self.part), lambda i, s: (i ^ s[0], 0, 0)),
            ],
            [
                self.weight(),
                self.weight(),
                pltpu.VMEM((self.width, rows), bf16),
                pltpu.VMEM((rows, self.part), bf16),
                pltpu.VMEM((self.width, self.part), bf16),
                pltpu.SemaphoreType.DMA((4,)),
                pltpu.SemaphoreType.DMA((4,)),
            ],
            3 * self.product(),
            layer=layer,
        )

    def parts(self, parts):
        def one(array, index):
            return (array, (1,) + array.shape[1:], lambda i, s: (index, 0, 0))

        return [one(*part) for part in parts]

    def finish_out(self, parts, layer, layers, earlier=()):
        shape = (layers, self.part // 2, self.width)
        return self.run(
            finish_out,
            1,
            self.parts(parts) + self.in_hbm(earlier),
            [(shape, jnp.float32, (1,) + shape[1:], lambda i, s: (layer, 0, 0))],
            [pltpu.VMEM((self.width, self.part // 2), jnp.float32)],
            0,
            {1 + len(parts): 0} if earlier else None,
        )

    def finish_in(self, parts, layer, layers, earlier=()):
        shape = (layers, self.block, self.hidden)
        return self.run(
            finish_in,
            1,
            self.parts(parts) + self.in_hbm(earlier),
            [(shape, jnp.float32, (1,) + shape[1:], lambda i, s: (layer, 0, 0))],
            [],
            0,
            {1 + len(parts): 0} if earlier else None,
        )


class Moves:
    def __init__(self):
        self.lines = lax.axis_size("fsdp") // 2
        self.copies = lax.axis_size("dp")
        me = lax.axis_index("fsdp")
        self.z, self.c, self.q = me // 2, me % 2, lax.axis_index("dp")

    def along(self, values, bits):
        return lax.ppermute(values, "fsdp", [(f, f ^ (2 * bits)) for f in range(2 * self.lines)])

    def core(self, values):
        return lax.ppermute(values, "fsdp", [(f, f ^ 1) for f in range(2 * self.lines)])

    def across(self, values, bits):
        return lax.ppermute(values, "dp", [(q, q ^ bits) for q in range(self.copies)])


class Held:
    def __init__(self, moves):
        self.moves, self.fresh = moves, []
        self.half = moves.lines // 2

    def bring(self, **arrays):
        for name, array in arrays.items():
            setattr(self, name, array)
            self.fresh.append(name)


def settle(held, *values):
    names = [(part, name) for part in held for name in part.fresh]
    arrays = tuple(getattr(part, name) for part, name in names)
    arrays = lax.optimization_barrier(tuple(values) + arrays)
    for (part, name), array in zip(names, arrays[len(values) :]):
        setattr(part, name, array)
    for part in held:
        part.fresh = []
    return arrays[: len(values)]


class Gather(Held):
    def __init__(self, moves, part):
        super().__init__(moves)
        self.part = part

    def direct(self):
        self.bring(**{"z%d" % i: self.moves.along(self.part, i) for i in range(1, self.moves.lines)})

    def join(self):
        self.line = jnp.stack([getattr(self, "z%d" % i) for i in range(1, self.moves.lines)])

    def first(self):
        self.bring(x=self.moves.across(self.line, 1), y=self.moves.across(self.line, 2))

    def second(self):
        self.bring(low=self.moves.across(self.y[:, :1], 1), high=self.moves.across(self.x[:, 1:], 2))

    def corner_core(self):
        self.corner = jnp.concatenate([self.low, self.high], 1)
        self.core("corner")

    def core(self, *names):
        self.bring(**{name + "_core": self.moves.core(getattr(self, name)) for name in names})

    def whole(self):
        names = ("line", "x", "y", "corner")
        return [getattr(self, name) for name in names] + [getattr(self, name + "_core") for name in names]


class Sum(Held):
    def __init__(self, moves, mine, other):
        super().__init__(moves)
        self.mine, self.theirs = mine, other
        self.low, self.high = slice(0, self.half), slice(self.half, None)

    def both(self, copies, part):
        return self.mine[copies, part] + self.got[copies, part]

    def core(self):
        self.bring(got=self.moves.core(self.theirs))

    def first(self):
        self.bring(
            from_x=self.moves.across(self.both(slice(2, 4), self.low), 1),
            from_y=self.moves.across(self.both(slice(1, 3), self.high), 2),
        )

    def second(self):
        self.bring(
            low2=self.moves.across(self.both(1, self.low) + self.from_x[0], 2),
            high1=self.moves.across(self.both(3, self.high) + self.from_y[1], 1),
        )

    def halves(self):
        low = self.both(0, self.low) + self.from_x[1] + self.low2
        high = self.both(0, self.high) + self.from_y[0] + self.high1
        return low, high

    def once(self):
        low, high = self.halves()
        self.block = low[0]
        blocks = [low[i] for i in range(1, self.half)] + [high[i] for i in range(self.half)]
        self.bring(**{"z%d" % (i + 1): self.moves.along(block, i + 1) for i, block in enumerate(blocks)})

    def far(self):
        self.block, high = self.halves()
        self.bring(z=self.moves.along(high, 2))

    def near(self):
        pair = self.block + self.z
        self.block = pair[0]
        self.bring(z1=self.moves.along(pair[1], 1))

    def total(self):
        total = self.block.astype(jnp.float32)
        for i in range(1, self.moves.lines):
            if hasattr(self, "z%d" % i):
                total = total + getattr(self, "z%d" % i).astype(jnp.float32)
        return total.astype(jnp.bfloat16)


class Share(Held):
    def __init__(self, moves, part, axis):
        super().__init__(moves)
        self.part, self.axis = part, axis

    def first(self):
        self.bring(near=self.moves.across(self.part, self.axis))

    def second(self):
        self.bring(far=self.moves.across(jnp.stack([self.part, self.near]), 3 - self.axis))

    def parts(self):
        near, far = (self.near[None], 0), (self.far, 0)
        return [(self.part[None], 0)] + ([near, far] if self.axis == 1 else [far, near]) + [(self.far, 1)]


class SumSmall(Held):
    def __init__(self, moves, mine, other):
        super().__init__(moves)
        self.value, self.theirs = mine, other

    def core(self):
        self.bring(got=self.moves.core(self.theirs))

    def across(self, bits):
        self.value = self.value + self.got
        self.bring(got=self.moves.across(self.value, bits))

    def along(self):
        self.value = self.value + self.got
        self.bring(**{"z%d" % i: self.moves.along(self.value[i], i) for i in range(1, self.moves.lines)})

    def total(self):
        parts = [self.value[0]] + [getattr(self, "z%d" % i) for i in range(1, self.moves.lines)]
        return sum(part.astype(jnp.float32) for part in parts)


class SumAll(Held):
    def __init__(self, moves, value):
        super().__init__(moves)
        self.value = value
        self.steps = [(axis, 2**k) for axis in ("fsdp", "dp") for k in range((lax.axis_size(axis) - 1).bit_length())]

    def step(self):
        axis, bit = self.steps.pop(0)
        count = lax.axis_size(axis)
        got = lax.ppermute(self.value, axis, [(i, i ^ bit) for i in range(count)])
        self.bring(value=self.value + got)


def blocked_shards(
    tokens, image_counts, skip_mask, norm1_gain, norm1_bias, token_in, token_in_bias, token_out,
    token_out_bias, norm2_gain, norm2_bias, channel_in, channel_in_bias, channel_out,
    channel_out_bias, cotangent,
):
    f32, bf16 = jnp.float32, jnp.bfloat16
    slots, patches, width = tokens.shape
    layers, in_rows, hidden = channel_in.shape
    keys = token_out.shape[1]
    moves = Moves()
    shards_count = 2 * moves.lines
    inner = keys * shards_count
    rows = -(-patches // 16) * 16
    place = jnp.stack([moves.z, moves.c, moves.q]).astype(jnp.int32)
    kernels = Kernels(place, slots, rows, width, inner, hidden, moves.lines, in_rows)
    wide = kernels.wide

    live = (jnp.arange(slots, dtype=jnp.int32) < image_counts[0]).astype(f32)
    scale = live[:, None, None] * skip_mask.astype(f32)

    def padded(images):
        return jnp.pad(images, ((0, 0), (0, rows - patches), (0, 0)))

    def quarter(array, axis):
        size = array.shape[axis] // 4
        return lax.dynamic_slice_in_dim(array, moves.q * size, size, axis)

    def widen(array):
        return jnp.pad(array, ((0, 0), (0, 0), (0, wide - array.shape[2])))

    gap = jnp.zeros((layers, keys, rows - patches), bf16)
    with_bias = jnp.concatenate([jnp.swapaxes(token_in, 1, 2), gap, token_in_bias[:, :, None]], 2)
    vectors = jnp.stack([norm1_gain, norm1_bias, norm2_gain, norm2_bias, channel_out_bias], 1)
    biases = jnp.pad(channel_in_bias, ((0, 0), (0, 2 * wide - channel_in_bias.shape[1])))
    vectors = jnp.concatenate([widen(vectors), biases.reshape(layers, 2, wide)], 1)
    extra = 16
    vectors = jnp.pad(vectors, ((0, 0), (0, extra - vectors.shape[1]), (0, 0)))
    vectors = jnp.pad(vectors, ((0, 0), (0, keys - extra), (0, 0)))
    packs = jnp.concatenate([widen(with_bias), widen(token_out), vectors], 2).reshape(layers * keys, width)
    b_outs = jnp.pad(token_out_bias.astype(f32), ((0, 0), (0, wide - patches)))[:, :, None]
    scale = scale.reshape(slots, 2 * layers)

    def both(layer):
        return jnp.stack([quarter(channel_in[layer], 1), quarter(channel_out[layer], 0)])

    first, last = Gather(moves, both(0)), Gather(moves, both(1))
    small = Gather(moves, packs)
    shards_held = Held(moves)
    first.direct()
    shards_held.bring(ins=moves.core(channel_in), outs=moves.core(channel_out))
    small.part, last.part = settle((first, shards_held), small.part, last.part)
    first.join()

    def weights(gather):
        return [channel_in, channel_out, shards_held.ins, shards_held.outs] + gather.whole()

    first.first()
    began, first.fresh = first.fresh, []
    first.core("line")
    small.direct()
    (last.part, first.line) = settle((first, small), last.part, first.line)
    first.fresh = began
    small.line = jnp.stack([small.part, small.z1, small.z2, small.z3])
    small.core("line")
    last.direct()
    last.fresh = ["z2"]
    found = kernels.unpack_small(small.line, small.line_core, layers, shards_count, extra)
    x0 = padded(tokens)
    (w_in0, w_in_t0, w_out0, w_out_t0, gain1_0, shift1_0, gain2_0, shift2_0, b_cout0, b_cin0) = found[0]
    (w_in1, w_in_t1, w_out1, w_out_t1, gain1_1, shift1_1, gain2_1, shift2_1, b_cout1, b_cin1) = found[1]

    u0, h0, d0, mid0, v0 = kernels.token_forward(
        scale, x0, b_outs, (gain1_0, shift1_0, w_in0, w_out_t0, gain2_0, shift2_0), 0
    )
    (v0,) = settle((first, small, last), v0)

    first.second()
    last.fresh = ["z3"]
    (v0, first.x, first.y) = settle((first, last), v0, first.x, first.y)
    first.core("x", "y")
    first.corner_core()
    last.fresh = ["z1"]
    (v0,) = settle((first, last), v0)

    last.join()
    last.first()
    hid0, slope0, x1 = kernels.first_forward(scale, v0, mid0, b_cin0, b_cout0, weights(first))
    (x1,) = settle((last,), x1)

    last.second()
    last.core("line", "x", "y")
    u1, h1, d1, mid1, v1 = kernels.token_forward(
        scale, x1, b_outs, (gain1_1, shift1_1, w_in1, w_out_t1, gain2_1, shift2_1), 1
    )
    (v1,) = settle((last,), v1)
    last.corner_core()
    grad2 = padded(cotangent)
    hid1, slope1, mine, theirs, low1, g_cout1 = kernels.last_hidden(scale, v1, b_cin1, grad2, weights(last))
    mine, theirs, low1 = settle((last,), mine, theirs, low1)

    sum_out1 = Sum(moves, mine, theirs)
    sum_out1.core()
    mine, theirs, back, g_cin1 = kernels.channel_backward(low1, v1, slope1, weights(last), 1)
    mine, theirs, back = settle((sum_out1,), mine, theirs, back)

    sum_in1 = Sum(moves, mine, theirs)
    sum_in1.core()
    sum_out1.first()
    grads1 = kernels.token_backward(
        scale, grad2, back, (mid1, x1, u1, h1, d1), (w_in_t1, w_out1, gain1_1, gain2_1), g_cout1, g_cin1, keys
    )
    grad1, *tokens1, vector1, low0, g_cout0 = settle((sum_out1, sum_in1), *grads1)

    sum_out1.second()
    sum_in1.first()
    mine, theirs = kernels.out_weight_grad(low0, hid0)
    mine, theirs = settle((sum_out1, sum_in1), mine, theirs)

    sum_out0 = Sum(moves, mine, theirs)
    sum_out0.core()
    sum_in1.second()
    sum_out1.far()
    mine, theirs, back, g_cin0 = kernels.channel_backward(low0, v0, slope0, weights(first), 0)
    mine, theirs, back = settle((sum_out1, sum_in1, sum_out0), mine, theirs, back)

    sum_in0 = Sum(moves, mine, theirs)
    sum_in0.core()
    sum_out0.first()
    sum_in1.far()
    sum_out1.near()
    grad0, *tokens, vector = kernels.token_backward(
        scale, grad1, back, (mid0, x0, u0, h0, d0), (w_in_t0, w_out0, gain1_0, gain2_0), g_cout0, g_cin0, keys,
        (*tokens1, vector1),
    )
    hid1, grad0, *tokens, vector = settle((sum_out1, sum_in1, sum_in0, sum_out0), hid1, grad0, *tokens, vector)

    sum_tokens = SumSmall(moves, *tokens)
    sum_tokens.core()
    sum_in0.first()
    sum_out0.second()
    vector_sum = SumAll(moves, vector)
    vector_sum.step()
    output = kernels.out_forward(scale, hid1, mid1, b_cout1, weights(last), 1, bf16)
    (output,) = settle((sum_in0, sum_out0, sum_tokens, vector_sum), output)

    sum_in0.second()
    sum_out0.once()
    sum_in1.near()
    sum_tokens.across(1)
    vector_sum.step()
    share_out1 = Share(moves, sum_out1.total(), 2)
    share_out1.first()
    output = output[:, :patches]
    (output,) = settle((sum_in0, sum_out0, sum_in1, sum_tokens, share_out1, vector_sum), output)

    sum_in0.once()
    sum_tokens.across(2)
    vector_sum.step()
    share_out0, share_in1 = Share(moves, sum_out0.total(), 2), Share(moves, sum_in1.total(), 1)
    share_out0.first()
    share_in1.first()
    share_out1.second()
    input_grad = grad0[:, :patches]
    (input_grad,) = settle(
        (sum_in0, sum_tokens, share_out0, share_in1, share_out1, vector_sum), input_grad
    )

    total = sum_in0.total()
    near = [moves.across(total, bits) for bits in (1, 2, 3)]
    share_out0.second()
    share_in1.second()
    sum_tokens.along()
    vector_sum.step()
    (done_out,) = kernels.finish_out(share_out1.parts(), 1, layers)
    done_out, *near = settle((sum_tokens, share_out0, share_in1, vector_sum), done_out, *near)
    vector_sum.step()
    (done_in,) = kernels.finish_in(share_in1.parts(), 1, layers)
    (grad_out,) = kernels.finish_out(share_out0.parts(), 0, layers, (done_out,))
    parts = [(part[None], 0) for part in [total] + near]
    (grad_in,) = kernels.finish_in(parts, 0, layers, (done_in,))
    near = sum_tokens.total()

    near = near.reshape(layers, 2, keys, wide)
    grad_t_in = jnp.swapaxes(near[:, 0, :, :patches], 1, 2)
    grad_b_in = near[:, 0, :, rows]
    grad_t_out = near[:, 1, :, :patches]
    sums = vector_sum.value.reshape(layers, 16, width)
    me = lax.axis_index("fsdp")

    def owned(row):
        size = width // shards_count
        return lax.dynamic_slice_in_dim(sums[:, row], me * size, size, 1)

    grad_gain1, grad_shift1, grad_gain2, grad_shift2, grad_b_cout = [owned(row) for row in range(5)]
    size = hidden // shards_count
    grad_b_cin = lax.dynamic_slice(sums, (0, 8 + me // 2, (me % 2) * size), (layers, 1, size))[:, 0]
    bias_total = sums[:, 5, :patches]
    return (
        output, input_grad, grad_gain1, grad_shift1, grad_t_in, grad_b_in, grad_t_out, bias_total,
        grad_gain2, grad_shift2, grad_in, grad_b_cin, grad_out, grad_b_cout,
    )


def fits(mesh):
    return mesh.shape["dp"] == 4 and mesh.shape["fsdp"] == 8


def solution(mesh):
    in_specs = (
        P(("dp", "fsdp"), None, None),
        P(("dp", "fsdp")),
        P(("dp", "fsdp"), None, None),
        P(None, "fsdp"),
        P(None, "fsdp"),
        P(None, None, "fsdp"),
        P(None, "fsdp"),
        P(None, "fsdp", None),
        P(),
        P(None, "fsdp"),
        P(None, "fsdp"),
        P(None, "fsdp", None),
        P(None, "fsdp"),
        P(None, "fsdp", None),
        P(None, "fsdp"),
        P(("dp", "fsdp"), None, None),
    )
    out_specs = (
        P(("dp", "fsdp"), None, None),
        P(("dp", "fsdp"), None, None),
        P(None, "fsdp"),
        P(None, "fsdp"),
        P(None, None, "fsdp"),
        P(None, "fsdp"),
        P(None, "fsdp", None),
        P(),
        P(None, "fsdp"),
        P(None, "fsdp"),
        P(None, "fsdp", None),
        P(None, "fsdp"),
        P(None, "fsdp", None),
        P(None, "fsdp"),
    )
    program = blocked_shards if fits(mesh) else shards
    return jax.shard_map(program, mesh=mesh, in_specs=in_specs, out_specs=out_specs, check_vma=False)
```

```python
import functools
import math

import jax
import jax.numpy as jnp
from jax import lax
from jax.experimental import pallas as pl
from jax.experimental.pallas import tpu as pltpu
from jax.sharding import PartitionSpec as P

EPSILON = 1e-06
GELU_A = math.sqrt(2.0 / math.pi)
GELU_B = 0.044715 * GELU_A
IMAGES = 2
VMEM_BYTES = 60 * 2**20


def as_sent(shard):

    def short(part):
        return part.astype(jnp.bfloat16) if part.dtype == jnp.float32 else part

    return jax.tree.map(short, shard)


def layer_norm(values, gain, shift):
    center = values - jnp.mean(values, -1, keepdims=True)
    inv_std = lax.rsqrt(jnp.mean(center * center, -1, keepdims=True) + EPSILON)
    normed = center * inv_std
    return (normed * gain + shift, normed, inv_std)


def norm_back(grad_out, normed, inv_std, gain):
    grad_gain = jnp.sum(grad_out * normed, axis=(0, 1))
    grad_shift = jnp.sum(grad_out, axis=(0, 1))
    scaled = grad_out * gain
    grad_in = inv_std * (
        scaled
        - jnp.mean(scaled, -1, keepdims=True)
        - normed * jnp.mean(scaled * normed, -1, keepdims=True)
    )
    return (grad_in, grad_gain, grad_shift)


def gelu_back(pre_act, grad_out):
    return jax.vjp(jax.nn.gelu, pre_act)[1](grad_out)[0]


def fetch_forward(pieces):
    return (
        lax.all_gather(pieces[0], "fsdp", axis=0, tiled=True),
        lax.all_gather(pieces[1], "fsdp", axis=0, tiled=True),
        lax.all_gather(pieces[2], "fsdp", axis=1, tiled=True),
        lax.all_gather(pieces[3], "fsdp", axis=0, tiled=True),
        lax.all_gather(pieces[4], "fsdp", axis=0, tiled=True),
        lax.all_gather(pieces[5], "fsdp", axis=0, tiled=True),
        lax.all_gather(pieces[6], "fsdp", axis=0, tiled=True),
        lax.all_gather(pieces[7], "fsdp", axis=0, tiled=True),
        lax.all_gather(pieces[8], "fsdp", axis=0, tiled=True),
        lax.all_gather(pieces[9], "fsdp", axis=0, tiled=True),
        lax.all_gather(pieces[10], "fsdp", axis=0, tiled=True),
    )


def fetch_backward(pieces):
    return (
        lax.all_gather(pieces[0], "fsdp", axis=0, tiled=True),
        lax.all_gather(pieces[1], "fsdp", axis=0, tiled=True),
        lax.all_gather(pieces[2], "fsdp", axis=1, tiled=True),
        lax.all_gather(pieces[3], "fsdp", axis=0, tiled=True),
        lax.all_gather(pieces[4], "fsdp", axis=0, tiled=True),
        lax.all_gather(pieces[5], "fsdp", axis=0, tiled=True),
        lax.all_gather(pieces[6], "fsdp", axis=0, tiled=True),
        lax.all_gather(pieces[7], "fsdp", axis=0, tiled=True),
        lax.all_gather(pieces[8], "fsdp", axis=0, tiled=True),
        lax.all_gather(pieces[9], "fsdp", axis=0, tiled=True),
        lax.all_gather(pieces[10], "fsdp", axis=0, tiled=True),
    )


def shards(
    tokens,
    image_counts,
    skip_mask,
    norm1_gain,
    norm1_bias,
    token_in,
    token_in_bias,
    token_out,
    token_out_bias,
    norm2_gain,
    norm2_bias,
    channel_in,
    channel_in_bias,
    channel_out,
    channel_out_bias,
    cotangent,
):
    f32 = jnp.float32
    bf16 = jnp.bfloat16
    slots = tokens.shape[0]
    layers = norm1_gain.shape[0]
    live = (jnp.arange(slots, dtype=jnp.int32) < image_counts[0]).astype(f32)
    branch_scale = live[:, None, None] * skip_mask.astype(f32)

    def layer_pieces(index):
        return (
            norm1_gain[index],
            norm1_bias[index],
            token_in[index],
            token_in_bias[index],
            token_out[index],
            norm2_gain[index],
            norm2_bias[index],
            channel_in[index],
            channel_in_bias[index],
            channel_out[index],
            channel_out_bias[index],
        )

    values = tokens.astype(f32)
    saved = []
    kept_weights = []
    for index in range(layers):
        weights = fetch_forward(layer_pieces(index))
        kept_weights.append(weights)
        gain1, shift1, w_tin, b_tin, w_tout, gain2, shift2, w_cin, b_cin, w_cout, b_cout = weights
        tok_bias = token_out_bias[index].astype(f32)
        normed1, plain1, inv1 = layer_norm(values, gain1.astype(f32), shift1.astype(f32))
        normed1 = normed1.astype(bf16)
        pre_tok = jnp.einsum(
            "isd,sk->idk", normed1, w_tin, preferred_element_type=f32
        ) + b_tin.astype(f32)
        hidden1 = jax.nn.gelu(pre_tok).astype(bf16)
        branch = (
            jnp.einsum("idk,ks->isd", hidden1, w_tout, preferred_element_type=f32)
            + tok_bias[None, :, None]
        )
        middle = values + branch_scale[:, index, 0][:, None, None] * branch
        normed2, plain2, inv2 = layer_norm(middle, gain2.astype(f32), shift2.astype(f32))
        normed2 = normed2.astype(bf16)
        pre_chan = jnp.einsum(
            "isd,df->isf", normed2, w_cin, preferred_element_type=f32
        ) + b_cin.astype(f32)
        hidden2 = jax.nn.gelu(pre_chan).astype(bf16)
        branch = jnp.einsum(
            "isf,fd->isd", hidden2, w_cout, preferred_element_type=f32
        ) + b_cout.astype(f32)
        values = middle + branch_scale[:, index, 1][:, None, None] * branch
        saved.append(
            (normed1, plain1, inv1, pre_tok, hidden1, normed2, plain2, inv2, pre_chan, hidden2)
        )
    output = values.astype(bf16)
    grad = cotangent.astype(f32)
    local_grads = [None] * layers
    bias_grads = [None] * layers
    for index in reversed(range(layers)):
        weights = fetch_backward(layer_pieces(index))
        gain1, shift1, w_tin, b_tin, w_tout, gain2, shift2, w_cin, b_cin, w_cout, b_cout = weights
        normed1, plain1, inv1, pre_tok, hidden1, normed2, plain2, inv2, pre_chan, hidden2 = saved[
            index
        ]
        out_chan = branch_scale[:, index, 1][:, None, None] * grad
        grad_b_cout = jnp.sum(out_chan, axis=(0, 1))
        low_chan = out_chan.astype(bf16)
        grad_w_cout = jnp.einsum("isf,isd->fd", hidden2, low_chan, preferred_element_type=f32)
        back_hidden = jnp.einsum("isd,fd->isf", low_chan, w_cout, preferred_element_type=f32)
        pre_grad = gelu_back(pre_chan, back_hidden)
        grad_b_cin = jnp.sum(pre_grad, axis=(0, 1))
        low_pre = pre_grad.astype(bf16)
        grad_w_cin = jnp.einsum("isd,isf->df", normed2, low_pre, preferred_element_type=f32)
        back_norm = jnp.einsum("isf,df->isd", low_pre, w_cin, preferred_element_type=f32)
        norm_in, grad_gain2, grad_shift2 = norm_back(back_norm, plain2, inv2, gain2.astype(f32))
        grad_mid = grad + norm_in
        out_tok = branch_scale[:, index, 0][:, None, None] * grad_mid
        bias_grads[index] = jnp.sum(out_tok, axis=(0, 2))
        low_tok = out_tok.astype(bf16)
        grad_w_tout = jnp.einsum("idk,isd->ks", hidden1, low_tok, preferred_element_type=f32)
        back_hidden = jnp.einsum("isd,ks->idk", low_tok, w_tout, preferred_element_type=f32)
        pre_grad = gelu_back(pre_tok, back_hidden)
        grad_b_tin = jnp.sum(pre_grad, axis=(0, 1))
        low_pre = pre_grad.astype(bf16)
        grad_w_tin = jnp.einsum("isd,idk->sk", normed1, low_pre, preferred_element_type=f32)
        back_norm = jnp.einsum("idk,sk->isd", low_pre, w_tin, preferred_element_type=f32)
        norm_in, grad_gain1, grad_shift1 = norm_back(back_norm, plain1, inv1, gain1.astype(f32))
        grad = grad_mid + norm_in
        local = (
            grad_gain1,
            grad_shift1,
            grad_w_tin,
            grad_b_tin,
            grad_w_tout,
            grad_gain2,
            grad_shift2,
            grad_w_cin,
            grad_b_cin,
            grad_w_cout,
            grad_b_cout,
        )
        local_grads[index] = local
    token_bias_total = lax.psum(jnp.stack(bias_grads), ("dp", "fsdp"))
    joined = tuple(
        (
            jnp.stack([local_grads[index][position] for index in range(layers)])
            for position in range(11)
        )
    )
    owned = (
        lax.psum_scatter(joined[0], "fsdp", scatter_dimension=1, tiled=True),
        lax.psum_scatter(joined[1], "fsdp", scatter_dimension=1, tiled=True),
        lax.psum_scatter(joined[2], "fsdp", scatter_dimension=2, tiled=True),
        lax.psum_scatter(joined[3], "fsdp", scatter_dimension=1, tiled=True),
        lax.psum_scatter(joined[4], "fsdp", scatter_dimension=1, tiled=True),
        lax.psum_scatter(joined[5], "fsdp", scatter_dimension=1, tiled=True),
        lax.psum_scatter(joined[6], "fsdp", scatter_dimension=1, tiled=True),
        lax.psum_scatter(joined[7], "fsdp", scatter_dimension=1, tiled=True),
        lax.psum_scatter(joined[8], "fsdp", scatter_dimension=1, tiled=True),
        lax.psum_scatter(joined[9], "fsdp", scatter_dimension=1, tiled=True),
        lax.psum_scatter(joined[10], "fsdp", scatter_dimension=1, tiled=True),
    )
    results = jax.tree.map(lambda part: part.astype(jnp.float32), lax.psum(as_sent(owned), "dp"))
    return (
        output,
        grad,
        results[0],
        results[1],
        results[2],
        results[3],
        results[4],
        token_bias_total,
        results[5],
        results[6],
        results[7],
        results[8],
        results[9],
        results[10],
    )


def norm_parts(values):
    center = values - jnp.mean(values, -1, keepdims=True)
    inv_std = lax.rsqrt(jnp.mean(center * center, -1, keepdims=True) + EPSILON)
    return center * inv_std, inv_std


def norm_input_grad(grad, normed, inv_std):
    return inv_std * (
        grad
        - jnp.mean(grad, -1, keepdims=True)
        - normed * jnp.mean(grad * normed, -1, keepdims=True)
    )


def gelu_pair(value):
    square = value * value
    gate = 0.5 + 0.5 * jnp.tanh(value * (GELU_A + GELU_B * square))
    result = value * gate
    slope = gate + result * (1.0 - gate) * (2.0 * GELU_A + 6.0 * GELU_B * square)
    return result.astype(jnp.bfloat16), slope.astype(jnp.bfloat16)


def dot(left, right, left_dim, right_dim):
    return lax.dot_general(
        left, right, (((left_dim,), (right_dim,)), ((), ())), preferred_element_type=jnp.float32
    )


def chunks(size, count):
    return [slice(k * size // count, (k + 1) * size // count) for k in range(count)]


def position(copy):
    odd = copy & 1
    return 2 * odd + (odd ^ (copy >> 1))


def staggered(parts, product, finish):
    held = product(parts[0])
    for k, part in enumerate(parts):
        later = product(parts[k + 1]) if k + 1 < len(parts) else None
        finish(part, held)
        held = later


def clear(first, *refs):
    @pl.when(first)
    def _():
        for ref in refs:
            ref[...] = jnp.zeros_like(ref)


def unpack_small(place, own, other, *refs):
    vectors = refs[-1]
    z, c = place[0], place[1]
    lines, rows, _ = own.shape
    layers, extra, wide = vectors.shape[1:]
    keys = rows // layers
    for layer in range(layers):
        w_in, w_in_t, w_out, w_out_t, *rest = refs[10 * layer : 10 * layer + 10]
        base = layer * keys
        for source, side in ((own, c), (other, 1 - c)):
            for i in range(lines):
                shard = 2 * (i ^ z) + side
                start = pl.multiple_of(shard * keys, keys)
                w_in[pl.ds(start, keys)] = source[i, base : base + keys, :wide]
                w_out[pl.ds(start, keys)] = source[i, base : base + keys, wide : 2 * wide]
                vectors[shard, layer] = source[i, base : base + extra, 2 * wide :]
        w_in_t[...] = w_in[...].T
        w_out_t[...] = w_out[...].T
        held = [vectors[shard, layer].astype(jnp.float32) for shard in range(vectors.shape[0])]
        for row, target in enumerate(rest[:5]):
            size = target.shape[1] // len(held)
            target[...] = jnp.concatenate([part[row : row + 1, :size] for part in held], axis=1)
        biases = rest[5]
        size = biases.shape[1] // len(held)
        for shard, part in enumerate(held):
            whole = jnp.concatenate([part[5:6], part[6:7]], axis=1)
            biases[:, shard * size : (shard + 1) * size] = whole[:, :size]


def token_branch(values, scale, small, b_out, u_out, hidden_out, slope_out):
    gain1, shift1, w_in, w_out, gain2, shift2 = small
    rows, wide = values.shape[0], w_in.shape[1]
    normed, _ = norm_parts(values)
    u_out[:rows] = (normed * gain1[...] + shift1[...]).astype(jnp.bfloat16)
    below = lax.broadcasted_iota(jnp.int32, (wide - rows, values.shape[1]), 0)
    u_out[rows:] = jnp.where(below == 0, 1.0, 0.0).astype(jnp.bfloat16)
    hidden, slope = gelu_pair(dot(w_in[...], u_out[...], 1, 0))
    hidden_out[...] = hidden
    slope_out[...] = slope
    middle = values + scale * (dot(w_out[:rows], hidden, 1, 0) + b_out[0, :rows])
    normed, _ = norm_parts(middle)
    return middle, (normed * gain2[...] + shift2[...]).astype(jnp.bfloat16)


def token_forward(place, scale, x, b_out, *rest, layer):
    small, (u_out, hidden_out, slope_out, middle_out, v_out) = rest[:6], rest[6:]
    count, rows = x.shape[:2]
    for k in range(count):
        part = scale[count * pl.program_id(0) + k, 2 * layer]
        middle, v = token_branch(
            x[k].astype(jnp.float32), part, small, b_out, u_out.at[k], hidden_out.at[k], slope_out.at[k]
        )
        middle_out[k] = middle
        v_out[k * rows : (k + 1) * rows] = v


def token_grads(scale, grad, back_v, middle, x, u, hidden, slope, w_in, w_out, gain1, gain2, padded):
    rows, width = grad.shape
    normed, inv_std = norm_parts(middle)
    moved = back_v * normed
    sums = [jnp.sum(moved, 0, keepdims=True), jnp.sum(back_v, 0, keepdims=True)]
    grad_mid = grad + norm_input_grad(back_v * gain2[...], normed, inv_std)
    padded[:rows] = (scale * grad_mid).astype(jnp.bfloat16)
    low = padded[...]
    b_out = dot(jnp.ones((8, width), jnp.bfloat16), low, 1, 1)[:1]
    w_out_grad = dot(hidden, low, 1, 1)
    pre = (dot(w_out[...], low, 1, 0) * slope.astype(jnp.float32)).astype(jnp.bfloat16)
    w_in_grad = dot(pre, u, 1, 1)
    back = dot(w_in[:rows], pre, 1, 0)
    normed, inv_std = norm_parts(x)
    sums = [jnp.sum(back * normed, 0, keepdims=True), jnp.sum(back, 0, keepdims=True)] + sums
    return grad_mid + norm_input_grad(back * gain1[...], normed, inv_std), sums, b_out, w_in_grad, w_out_grad


def token_blocks(place, w_in_grad, w_out_grad, whole, put):
    z, c = place[0], place[1]
    keys = whole.shape[1] // 8
    for which, total in ((0, w_in_grad), (1, w_out_grad)):
        whole[which] = total[...].astype(jnp.bfloat16)
        for i in range(4):
            for side, core in ((0, c), (1, 1 - c)):
                start = pl.multiple_of((2 * (i ^ z) + core) * keys, keys)
                put(which, i, side, whole[which, pl.ds(start, keys)])


def token_backward(place, scale, grad, back_v, middle, x, u, hidden, slope, w_in, w_out, gain1, gain2, *rest):
    image = pl.program_id(0)
    g_cout, g_cin = rest[:2]
    last = len(rest) == 2 + 6 + 4
    if last:
        grad_out, mine_out, other_out, vector, low_out, above_grad = rest[2:8]
        layer = 1
    else:
        earlier, grad_out, mine_out, other_out, vector = rest[2:5], *rest[5:9]
        layer = 0
    padded, w_in_grad, w_out_grad, whole = rest[-4:]
    count, rows = x.shape[:2]
    first = image == 0
    clear(first, padded, vector, w_in_grad, w_out_grad)

    @pl.when(first)
    def _():
        vector[4:5] = g_cout[...]
        for j in range(g_cin.shape[0]):
            vector[8 + j : 9 + j] = g_cin[j]
        if not last:
            vector[16:] = earlier[2][...]

    if last:
        clear(first, above_grad)
    found = []
    for k in range(count):
        part = slice(k * rows, (k + 1) * rows)
        result, *sums = token_grads(
            scale[count * image + k, 2 * layer], grad[k].astype(jnp.float32), back_v[part], middle[k],
            x[k].astype(jnp.float32), u[k], hidden[k], slope[k], w_in, w_out, gain1, gain2, padded.at[k],
        )
        grad_out[k] = result
        if last:
            out = scale[count * image + k, 1] * result
            above_grad[...] += jnp.sum(out, 0, keepdims=True)
            low_out[part] = out.astype(jnp.bfloat16)
        found.append(sums)
    for k in range(4):
        vector[k : k + 1] += sum(sums[0][k] for sums in found)
    vector[5:6, : padded.shape[1]] += sum(sums[1] for sums in found)
    w_in_grad[...] += sum(sums[2] for sums in found)
    w_out_grad[...] += sum(sums[3] for sums in found)

    @pl.when(image == pl.num_programs(0) - 1)
    def _():
        targets = (mine_out, other_out)

        def put(which, i, side, part):
            targets[side][i, which] = part

        if not last:
            for side in range(2):
                targets[side][:, 2:] = earlier[side][...]
        token_blocks(place, w_in_grad, w_out_grad, whole, put)


def out_weight_grad(place, low, hidden, mine_out, other_out, turned, whole):
    @pl.when(pl.program_id(0) == 0)
    def _():
        turned[...] = low[...].T

    out_blocks(place, turned, hidden[0], mine_out, other_out, whole)


class Weight:
    def __init__(self, refs, which):
        self.which = which
        self.shards, self.parts = (refs[which], refs[2 + which]), (refs[4 : 4 + 4], refs[8:12])

    def blocks(self, copy, i):
        for side, (line, from_x, from_y, corner) in enumerate(self.parts):
            yield side, (line, from_x, from_y, corner)[copy].at[i - 1, self.which], 0


def fetch_in(place, layer, weight, target, sem):
    z, c, q = place[0], place[1], place[2]
    copies, _, columns = target.shape
    rows = weight.shards[0].shape[1]
    for copy in range(copies):
        j = copy ^ q

        def put(ref, i, side, first):
            start = pl.multiple_of((2 * (i ^ z) + (c ^ side)) * rows + first, 16)
            goal = target.at[j, pl.ds(start, ref.shape[0])]
            pltpu.make_async_copy(ref, goal, sem.at[j]).start()

        for side, shard in enumerate(weight.shards):
            put(shard.at[layer, :, pl.ds(pl.multiple_of(j * columns, columns), columns)], 0, side, 0)
        for i in range(1, copies):
            for side, ref, first in weight.blocks(copy, i):
                put(ref, i, side, first)


def fetch_out(place, layer, weight, target, sem):
    z, c, q = place[0], place[1], place[2]
    lines, part, _ = target.shape
    for i in range(lines):

        def put(ref, start):
            goal = target.at[i ^ z, pl.ds(pl.multiple_of(start, 16), ref.shape[0])]
            pltpu.make_async_copy(ref, goal, sem.at[i ^ z]).start()

        if i == 0:
            for side, shard in enumerate(weight.shards):
                put(shard.at[layer], (c ^ side) * (part // 2))
            continue
        for copy in range(4):
            for side, ref, first in weight.blocks(copy, i):
                put(ref, (c ^ side) * (part // 2) + (copy ^ q) * (part // 8) + first)


def arrive(weight, sem, step):
    pltpu.make_async_copy(weight.at[step], weight.at[step], sem.at[step]).wait()


def out_blocks(place, turned, hidden, mine_out, other_out, whole):
    c, q = place[1], place[2]
    whole[...] = dot(turned[...], hidden, 1, 0).astype(jnp.bfloat16)
    copies, _, rows, columns = mine_out.shape
    size = columns // 2
    for side, target in ((c, mine_out), (1 - c, other_out)):
        units = pl.ds(pl.multiple_of(side * size, 128), size)
        for j in range(copies):
            start = 2 * j * rows
            target[position(j ^ q), 0, :, :size] = whole[start : start + rows, units]
            target[position(j ^ q), 0, :, size:] = whole[start + rows : start + 2 * rows, units]


def first_forward(place, scale, v, middle, bias_in, bias_out, *rest):
    weight_in, weight_out = Weight(rest[:12], 0), Weight(rest[:12], 1)
    hidden_out, slope_out, x_out, w_in, w_out, hidden, total, sem_in, sem_out = rest[12:]
    step = pl.program_id(0)
    rows = middle.shape[1]

    @pl.when(step == 0)
    def _():
        fetch_in(place, 0, weight_in, w_in, sem_in)
        fetch_out(place, 0, weight_out, w_out, sem_out)
        total[...] = jnp.zeros_like(total)

    @pl.when(step < 4)
    def _():
        j = (step & 3) ^ place[2]
        arrive(w_in, sem_in, j)
        def product(part):
            return dot(v[part], w_in[j], 1, 0) + bias_in[...]

        def finish(part, found):
            value, slope = gelu_pair(found)
            hidden_out[0, part] = value
            hidden[j, part] = value
            slope_out[0, part] = slope

        staggered(chunks(v.shape[0], 4), product, finish)

    @pl.when(step >= 4)
    def _():
        j = (step & 3) ^ place[0]
        arrive(w_out, sem_out, j)
        total[...] += dot(hidden[j], w_out[j], 1, 0)

    @pl.when(step == 7)
    def _():
        for image in range(middle.shape[0]):
            branch = total[image * rows : (image + 1) * rows] + bias_out[...]
            x_out[image] = middle[image] + scale[image, 1] * branch


def last_hidden(place, scale, v, bias, grad, w_in, hidden_out, slope_out, blocks_out, low_out, bias_grad, hidden, turned):
    step = pl.program_id(0)

    @pl.when(step == 0)
    def _():
        rows = grad.shape[1]
        sums = 0.0
        for image in range(grad.shape[0]):
            out = scale[image, 3] * grad[image].astype(jnp.float32)
            sums = sums + jnp.sum(out, 0, keepdims=True)
            low_out[image * rows : (image + 1) * rows] = out.astype(jnp.bfloat16)
        bias_grad[...] = sums
        turned[...] = low_out[...].T

    @pl.when(step < 4)
    def _():
        def product(part):
            return dot(v[part], w_in[...], 1, 0) + bias[...]

        def finish(part, found):
            value, slope = gelu_pair(found)
            hidden_out[0, part] = value
            hidden[step & 3, part] = value
            slope_out[0, part] = slope

        staggered(chunks(v.shape[0], 4), product, finish)

    @pl.when(step >= 4)
    def _():
        found = dot(turned[...], hidden[step & 3], 1, 0).astype(jnp.bfloat16)
        size = blocks_out.shape[2]
        for k in range(blocks_out.shape[0]):
            blocks_out[k] = found[:, k * size : (k + 1) * size]


def last_out(place, scale, hidden, middle, bias, w_out, x_out, total):
    step = pl.program_id(0)

    @pl.when(step == 0)
    def _():
        total[...] = jnp.zeros_like(total)

    total[...] += dot(hidden[0], w_out[...], 1, 0)

    @pl.when(step == pl.num_programs(0) - 1)
    def _():
        for image in range(middle.shape[0]):
            rows = middle.shape[1]
            branch = total[image * rows : (image + 1) * rows] + bias[...]
            x_out[image] = (middle[image] + scale[image, 3] * branch).astype(x_out.dtype)


def last_backward(place, low, v, slope, w_out, w_in, in_out, back_out, bias_grad, turned, pre):
    @pl.when(pl.program_id(0) == 0)
    def _():
        turned[...] = v[...].T
        back_out[...] = jnp.zeros_like(back_out)

    sums = []

    def product(part):
        return dot(low[part], w_out[...], 1, 1)

    def finish(part, found):
        grad = found * slope[0, part].astype(jnp.float32)
        sums.append(jnp.sum(grad, 0, keepdims=True))
        pre[part] = grad.astype(jnp.bfloat16)

    staggered(chunks(low.shape[0], 2), product, finish)
    bias_grad[0] = sum(sums)
    for part in chunks(turned.shape[0], 3):
        in_out[part] = dot(turned[part], pre[...], 1, 0).astype(jnp.bfloat16)
    back_out[...] += dot(pre[...], w_in[...], 1, 1)


def channel_backward(place, low, v, slope, *rest, layer):
    mine, theirs, back_out, bias_grad, w_out, w_in, turned, pre, whole, sem_out, sem_in = rest[12:]
    z, c = place[0], place[1]
    step = pl.program_id(0)

    @pl.when(step == 0)
    def _():
        fetch_out(place, layer, Weight(rest[:12], 1), w_out, sem_out)
        fetch_in(place, layer, Weight(rest[:12], 0), w_in, sem_in)
        turned[...] = v[...].T
        back_out[...] = jnp.zeros_like(back_out)

    j = step ^ z
    arrive(w_out, sem_out, j)
    arrive(w_in, sem_in, j)
    sums = []

    def product(part):
        return dot(low[part], w_out[j], 1, 1)

    def finish(part, found):
        grad = found * slope[0, part].astype(jnp.float32)
        sums.append(jnp.sum(grad, 0, keepdims=True))
        pre[part] = grad.astype(jnp.bfloat16)

    staggered(chunks(low.shape[0], 2), product, finish)
    bias_grad[0] = sum(sums)
    for part in chunks(turned.shape[0], 3):
        whole[part] = dot(turned[part], pre[...], 1, 0).astype(jnp.bfloat16)
    lines = mine.shape[1]
    rows = whole.shape[0] // (2 * lines)
    for i in range(lines):
        for side, target in ((c, mine), (1 - c, theirs)):
            start = pl.multiple_of((2 * (i ^ z) + side) * rows, rows)
            target[0, i] = whole[pl.ds(start, rows)]
    back_out[...] += dot(pre[...], w_in[j], 1, 1)


def finish_last(place, grad_in, grad_out, in_out, out_out):
    in_out[0] = grad_in[...].astype(jnp.float32)
    out_out[0] = grad_out[0].astype(jnp.float32).T


def finish_first(place, *refs):
    parts_in, parts_out = refs[:4], refs[4:8]
    in_out, out_out, whole = refs[-3:]
    for j in range(4):
        columns = parts_in[j].shape[2]
        start = pl.multiple_of((j ^ place[2]) * columns, columns)
        in_out[0, :, pl.ds(start, columns)] = parts_in[j][0].astype(jnp.float32)
        rows, columns = parts_out[j].shape[1:]
        for half in range(2):
            start = pl.multiple_of((2 * (j ^ place[2]) + half) * rows, rows)
            part = parts_out[j][0, :, half * columns // 2 : (half + 1) * columns // 2]
            whole[pl.ds(start, rows)] = part.astype(jnp.float32)
    out_out[0] = whole[...].T


class Kernels:
    def __init__(self, place, slots, rows, width, inner, hidden, lines, block):
        self.place = place
        self.slots, self.rows, self.width = slots, rows, width
        self.inner, self.hidden = inner, hidden
        self.lines, self.block = lines, block
        self.part = hidden // 4
        self.wide = 256

    def run(self, body, steps, inputs, outputs, scratch, flops, aliases=None, **fixed):
        sizes = sum(a.size * a.dtype.itemsize for a, _, _ in inputs)
        sizes += sum(math.prod(o[0]) * jnp.dtype(o[1]).itemsize for o in outputs)

        def spec(block, index):
            if isinstance(block, tuple):
                return pl.BlockSpec(block, index)
            return pl.BlockSpec(memory_space=block)

        return pl.pallas_call(
            functools.partial(body, **fixed) if fixed else body,
            name=body.__name__,
            grid_spec=pltpu.PrefetchScalarGridSpec(
                num_scalar_prefetch=1,
                grid=(steps,),
                in_specs=[spec(block, index) for _, block, index in inputs],
                out_specs=[spec(o[2], o[3]) for o in outputs],
                scratch_shapes=scratch,
            ),
            out_shape=[jax.ShapeDtypeStruct(o[0], o[1]) for o in outputs],
            input_output_aliases=aliases or {},
            compiler_params=pltpu.CompilerParams(
                dimension_semantics=("arbitrary",), vmem_limit_bytes=VMEM_BYTES
            ),
            cost_estimate=pl.CostEstimate(flops=flops, bytes_accessed=sizes, transcendentals=0),
        )(self.place, *[a for a, _, _ in inputs])

    def image(self, array):
        return (array, (1,) + array.shape[1:], lambda i, s: (i, 0, 0))

    def fixed(self, array):
        zeros = (0,) * array.ndim
        return (array, array.shape, lambda i, s: zeros)

    def scalars(self, array):
        return (array, pltpu.SMEM, None)

    def in_hbm(self, arrays):
        return [(a, pltpu.HBM, None) for a in arrays]

    def fixed_out(self, shape, dtype):
        zeros = (0,) * len(shape)
        return (shape, dtype, shape, lambda i, s: zeros)

    def columns(self, array, count):
        return (array, (array.shape[0], array.shape[1] // count), lambda i, s: (0, i))

    def columns_out(self, rows, columns, count, dtype):
        return ((rows, columns), dtype, (rows, columns // count), lambda i, s: (0, i))

    def late(self, step, start):
        return jnp.clip(step - start, 0, 3)

    def images_out(self, rows, dtype):
        block = (IMAGES, rows, self.width)
        return ((self.slots, rows, self.width), dtype, block, lambda i, s: (i, 0, 0))

    def images(self, array):
        return (array, (IMAGES,) + array.shape[1:], lambda i, s: (i, 0, 0))

    def rows_out(self):
        shape = (self.slots * self.rows, self.width)
        return (shape, jnp.bfloat16, (IMAGES * self.rows, self.width), lambda i, s: (i, 0))

    def quarters(self, array, which, start=0):
        return (array, (1,) + array.shape[1:], lambda i, s: (self.late(i, start) ^ s[which], 0, 0))

    def quarters_out(self, which, start=0):
        rows = self.slots * self.rows
        block = (1, rows, self.part)
        return ((4,) + block[1:], jnp.bfloat16, block, lambda i, s: (self.late(i, start) ^ s[which], 0, 0))

    def row(self, array, which, start=0):
        return (array, (1, self.part), lambda i, s: (0, self.late(i, start) ^ s[which]))

    def out_blocks_out(self, start=0):
        block = (4, 1, self.block, self.width)
        shape = (4, self.lines) + block[2:]
        return (shape, jnp.bfloat16, block, lambda i, s: (0, self.late(i, start), 0, 0))

    def product(self):
        return 2 * self.slots * self.rows * self.width * self.hidden

    def unpack_small(self, own, other, layers, shards, extra):
        bf16, f32 = jnp.bfloat16, jnp.float32
        inner, wide, width = self.inner, self.wide, self.width
        outputs = [((inner, wide), bf16), ((wide, inner), bf16)] * 2
        outputs += [((1, width), f32)] * 5 + [((1, self.hidden), f32)]
        found = self.run(
            unpack_small,
            1,
            [self.fixed(own), self.fixed(other)],
            [self.fixed_out(*part) for part in outputs * layers],
            [pltpu.VMEM((shards, layers, extra, wide), bf16)],
            0,
        )
        return [list(found[10 * layer : 10 * layer + 10]) for layer in range(layers)]

    def token_product(self):
        return 2 * self.slots * self.wide * self.width * self.inner

    def b_out(self, array, layer):
        return (array, (1,) + array.shape[1:], lambda i, s: (layer, 0, 0))

    def token_outs(self):
        bf16 = jnp.bfloat16
        outs = [self.images_out(rows, bf16) for rows in (self.wide, self.inner, self.inner)]
        return outs + [self.images_out(self.rows, jnp.float32), self.rows_out()]

    def token_forward(self, scale, x, b_out, small, layer):
        return self.run(
            token_forward,
            self.slots // IMAGES,
            [self.scalars(scale), self.images(x), self.b_out(b_out, layer)] + [self.fixed(a) for a in small],
            self.token_outs(),
            [],
            2 * self.token_product(),
            layer=layer,
        )

    def first_forward(self, scale, v, middle, bias_in, bias_out, weights):
        bf16, f32 = jnp.bfloat16, jnp.float32
        rows = self.slots * self.rows
        return self.run(
            first_forward,
            8,
            [self.scalars(scale), self.fixed(v), self.fixed(middle), self.row(bias_in, 2), self.fixed(bias_out)]
            + self.in_hbm(weights),
            [self.quarters_out(2)] * 2 + [self.fixed_out((self.slots, self.rows, self.width), f32)],
            [
                self.weight(),
                self.weight(),
                pltpu.VMEM((4, rows, self.part), bf16),
                pltpu.VMEM((rows, self.width), f32),
                pltpu.SemaphoreType.DMA((4,)),
                pltpu.SemaphoreType.DMA((4,)),
            ],
            2 * self.product(),
        )

    def steps(self, array):
        return (array, (1,) + array.shape[1:], lambda i, s: (jnp.minimum(i, 3), 0, 0))

    def steps_out(self):
        block = (1, self.slots * self.rows, self.part)
        return ((4,) + block[1:], jnp.bfloat16, block, lambda i, s: (jnp.minimum(i, 3), 0, 0))

    def columns_in(self, array):
        return (array, (array.shape[0], self.part), lambda i, s: (0, jnp.minimum(i, 3)))

    def rows_in(self, array):
        return (array, (self.part, array.shape[1]), lambda i, s: (i, 0))

    def last_hidden(self, scale, v, bias, grad, w_in):
        bf16, f32 = jnp.bfloat16, jnp.float32
        rows = self.slots * self.rows
        block = (2, self.width, self.part // 2)
        return self.run(
            last_hidden,
            8,
            [self.scalars(scale), self.fixed(v), self.columns_in(bias), self.fixed(grad), self.columns_in(w_in)],
            [self.steps_out()] * 2
            + [((8,) + block[1:], bf16, block, lambda i, s: (jnp.maximum(i - 4, 0), 0, 0))]
            + [self.fixed_out((rows, self.width), bf16), self.fixed_out((1, self.width), f32)],
            [pltpu.VMEM((4, rows, self.part), bf16), pltpu.VMEM((self.width, rows), bf16)],
            2 * self.product(),
        )

    def last_out(self, scale, hidden, middle, bias, w_out):
        return self.run(
            last_out,
            4,
            [self.scalars(scale), self.steps(hidden), self.fixed(middle), self.fixed(bias), self.rows_in(w_out)],
            [self.fixed_out(middle.shape, jnp.bfloat16)],
            [pltpu.VMEM((self.slots * self.rows, self.width), jnp.float32)],
            self.product(),
        )[0]

    def last_backward(self, low, v, slope, w_out, w_in):
        bf16, f32 = jnp.bfloat16, jnp.float32
        rows = self.slots * self.rows
        return self.run(
            last_backward,
            4,
            [self.fixed(low), self.fixed(v), self.steps(slope), self.rows_in(w_out), self.columns_in(w_in)],
            [
                ((self.width, self.hidden), bf16, (self.width, self.part), lambda i, s: (0, i)),
                self.fixed_out((rows, self.width), f32),
                ((4, 1, self.part), f32, (1, 1, self.part), lambda i, s: (i, 0, 0)),
            ],
            [pltpu.VMEM((self.width, rows), bf16), pltpu.VMEM((rows, self.part), bf16)],
            3 * self.product(),
        )

    def token_backward(self, scale, grad, back, kept, small, g_cout, g_cin, keys, earlier=()):
        bf16, f32 = jnp.bfloat16, jnp.float32
        width = self.width
        middle, x, u, hidden, slope = kept
        inputs = [self.scalars(scale), self.images(grad)]
        inputs += [(back, (IMAGES * self.rows, width), lambda i, s: (i, 0))]
        inputs += [self.images(a) for a in (middle, x, u, hidden, slope)]
        inputs += [self.fixed(a) for a in tuple(small) + (g_cout, g_cin) + tuple(earlier)]
        outputs = [self.images_out(self.rows, f32)]
        outputs += [self.fixed_out((self.lines, 4 if earlier else 2, keys, self.wide), bf16)] * 2
        outputs += [self.fixed_out((32 if earlier else 16, width), f32)]
        if not earlier:
            outputs += [self.rows_out(), self.fixed_out((1, width), f32)]
        return self.run(
            token_backward,
            self.slots // IMAGES,
            inputs,
            outputs,
            [
                pltpu.VMEM((IMAGES, self.wide, width), bf16),
                pltpu.VMEM((self.inner, self.wide), f32),
                pltpu.VMEM((self.inner, self.wide), f32),
                pltpu.VMEM((2, self.inner, self.wide), bf16),
            ],
            4 * self.token_product(),
        )

    def out_weight_grad(self, low, hidden):
        rows = self.slots * self.rows
        return self.run(
            out_weight_grad,
            4,
            [self.fixed(low), self.quarters(hidden, 0)],
            [self.out_blocks_out()] * 2,
            [pltpu.VMEM((self.width, rows), jnp.bfloat16), pltpu.VMEM((self.width, self.part), jnp.bfloat16)],
            self.product(),
        )

    def weight(self):
        return pltpu.VMEM((4, self.width, self.part), jnp.bfloat16)

    def out_forward(self, scale, hidden, middle, bias, weights, layer, dtype):
        return self.run(
            out_forward,
            4,
            [self.scalars(scale), self.quarters(hidden, 0), self.fixed(middle), self.fixed(bias)]
            + self.in_hbm(weights),
            [self.fixed_out(middle.shape, dtype)],
            [
                self.weight(),
                pltpu.VMEM((self.slots * self.rows, self.width), jnp.float32),
                pltpu.SemaphoreType.DMA((4,)),
            ],
            self.product(),
            layer=layer,
        )[0]

    def channel_backward(self, low, v, slope, weights, layer):
        bf16, f32 = jnp.bfloat16, jnp.float32
        rows = self.slots * self.rows
        block = (1, self.lines, self.block, self.width)
        shape = (4, self.lines, self.block, self.width)
        blocks = (shape, bf16, block, lambda j, s: (position(j ^ s[0] ^ s[2]), 0, 0, 0))
        return self.run(
            channel_backward,
            4,
            [self.fixed(low), self.fixed(v), self.quarters(slope, 0)]
            + self.in_hbm(weights),
            [
                blocks,
                blocks,
                self.fixed_out((rows, self.width), f32),
                ((4, 1, self.part), f32, (1, 1, self.part), lambda i, s: (i ^ s[0], 0, 0)),
            ],
            [
                self.weight(),
                self.weight(),
                pltpu.VMEM((self.width, rows), bf16),
                pltpu.VMEM((rows, self.part), bf16),
                pltpu.VMEM((self.width, self.part), bf16),
                pltpu.SemaphoreType.DMA((4,)),
                pltpu.SemaphoreType.DMA((4,)),
            ],
            3 * self.product(),
            layer=layer,
        )

    def shard_outs(self, layer, layers):
        shapes = (layers, self.block, self.hidden), (layers, self.part // 2, self.width)
        return [(shape, jnp.float32, (1,) + shape[1:], lambda i, s: (layer, 0, 0)) for shape in shapes]

    def finish_last(self, grad_in, grad_out, layer, layers):
        inputs = [self.fixed(grad_in), self.fixed(grad_out)]
        return self.run(finish_last, 1, inputs, self.shard_outs(layer, layers), [], 0)

    def finish_first(self, parts_in, parts_out, layer, layers, earlier):
        def one(part):
            array, index = part
            return (array, (1,) + array.shape[1:], lambda i, s: (index, 0, 0))

        inputs = [one(part) for part in parts_in + parts_out]
        return self.run(
            finish_first,
            1,
            inputs + self.in_hbm(earlier),
            self.shard_outs(layer, layers),
            [pltpu.VMEM((self.width, self.part // 2), jnp.float32)],
            0,
            {1 + len(inputs): 0, 2 + len(inputs): 1},
        )


class Moves:
    def __init__(self):
        self.lines = lax.axis_size("fsdp") // 2
        self.copies = lax.axis_size("dp")
        me = lax.axis_index("fsdp")
        self.z, self.c, self.q = me // 2, me % 2, lax.axis_index("dp")

    def along(self, values, bits):
        return lax.ppermute(values, "fsdp", [(f, f ^ (2 * bits)) for f in range(2 * self.lines)])

    def core(self, values):
        return lax.ppermute(values, "fsdp", [(f, f ^ 1) for f in range(2 * self.lines)])

    def across(self, values, bits):
        return lax.ppermute(values, "dp", [(q, q ^ bits) for q in range(self.copies)])


class Held:
    def __init__(self, moves):
        self.moves, self.fresh = moves, []
        self.half = moves.lines // 2

    def bring(self, **arrays):
        for name, array in arrays.items():
            setattr(self, name, array)
            self.fresh.append(name)


def settle(held, *values):
    names = [(part, name) for part in held for name in part.fresh]
    arrays = tuple(getattr(part, name) for part, name in names)
    arrays = lax.optimization_barrier(tuple(values) + arrays)
    for (part, name), array in zip(names, arrays[len(values) :]):
        setattr(part, name, array)
    for part in held:
        part.fresh = []
    return arrays[: len(values)]


class Gather(Held):
    def __init__(self, moves, part):
        super().__init__(moves)
        self.part = part

    def direct(self):
        self.bring(**{"z%d" % i: self.moves.along(self.part, i) for i in range(1, self.moves.lines)})

    def join(self):
        self.line = jnp.stack([getattr(self, "z%d" % i) for i in range(1, self.moves.lines)])

    def first(self):
        self.bring(x=self.moves.across(self.line, 1), y=self.moves.across(self.line, 2))

    def second(self):
        self.bring(low=self.moves.across(self.y[:, :1], 1), high=self.moves.across(self.x[:, 1:], 2))

    def corner_core(self):
        self.corner = jnp.concatenate([self.low, self.high], 1)
        self.core("corner")

    def core(self, *names):
        self.bring(**{name + "_core": self.moves.core(getattr(self, name)) for name in names})

    def whole(self):
        names = ("line", "x", "y", "corner")
        return [getattr(self, name) for name in names] + [getattr(self, name + "_core") for name in names]


class Sum(Held):
    def __init__(self, moves, mine, other):
        super().__init__(moves)
        self.mine, self.theirs = mine, other
        self.low, self.high = slice(0, self.half), slice(self.half, None)

    def both(self, copies, part):
        return self.mine[copies, part] + self.got[copies, part]

    def core(self):
        self.bring(got=self.moves.core(self.theirs))

    def first(self):
        self.bring(
            from_x=self.moves.across(self.both(slice(2, 4), self.low), 1),
            from_y=self.moves.across(self.both(slice(1, 3), self.high), 2),
        )

    def second(self):
        self.bring(
            low2=self.moves.across(self.both(1, self.low) + self.from_x[0], 2),
            high1=self.moves.across(self.both(3, self.high) + self.from_y[1], 1),
        )

    def halves(self):
        low = self.both(0, self.low) + self.from_x[1] + self.low2
        high = self.both(0, self.high) + self.from_y[0] + self.high1
        return low, high

    def once(self):
        low, high = self.halves()
        self.block = low[0]
        blocks = [low[i] for i in range(1, self.half)] + [high[i] for i in range(self.half)]
        self.bring(**{"z%d" % (i + 1): self.moves.along(block, i + 1) for i, block in enumerate(blocks)})

    def far(self):
        self.block, high = self.halves()
        self.bring(z=self.moves.along(high, 2))

    def near(self):
        pair = self.block + self.z
        self.block = pair[0]
        self.bring(z1=self.moves.along(pair[1], 1))

    def total(self):
        total = self.block.astype(jnp.float32)
        for i in range(1, self.moves.lines):
            if hasattr(self, "z%d" % i):
                total = total + getattr(self, "z%d" % i).astype(jnp.float32)
        return total.astype(jnp.bfloat16)


class Share(Held):
    def __init__(self, moves, part, axis):
        super().__init__(moves)
        self.part, self.axis = part, axis

    def first(self):
        self.bring(near=self.moves.across(self.part, self.axis))

    def second(self):
        self.bring(far=self.moves.across(jnp.stack([self.part, self.near]), 3 - self.axis))

    def parts(self):
        near, far = (self.near[None], 0), (self.far, 0)
        return [(self.part[None], 0)] + ([near, far] if self.axis == 1 else [far, near]) + [(self.far, 1)]


class SumSmall(Held):
    def __init__(self, moves, mine, other):
        super().__init__(moves)
        self.value, self.theirs = mine, other

    def core(self):
        self.bring(got=self.moves.core(self.theirs))

    def across(self, bits):
        self.value = self.value + self.got
        self.bring(got=self.moves.across(self.value, bits))

    def along(self):
        self.value = self.value + self.got
        self.bring(**{"z%d" % i: self.moves.along(self.value[i], i) for i in range(1, self.moves.lines)})

    def total(self):
        parts = [self.value[0]] + [getattr(self, "z%d" % i) for i in range(1, self.moves.lines)]
        return sum(part.astype(jnp.float32) for part in parts)


class Copies(Held):
    def __init__(self, moves, *values):
        super().__init__(moves)
        self.values = list(values)

    def step(self, *axes):
        got = [self.moves.across(value, bits) for value, bits in zip(self.values, axes)]
        self.bring(got0=got[0], got1=got[1])

    def add(self):
        self.values = [self.values[0] + self.got0, self.values[1] + self.got1]


class SumAll(Held):
    def __init__(self, moves, value):
        super().__init__(moves)
        self.value = value
        self.steps = [(axis, 2**k) for axis in ("fsdp", "dp") for k in range((lax.axis_size(axis) - 1).bit_length())]

    def step(self):
        axis, bit = self.steps.pop(0)
        count = lax.axis_size(axis)
        got = lax.ppermute(self.value, axis, [(i, i ^ bit) for i in range(count)])
        self.bring(value=self.value + got)


def blocked_shards(
    tokens, image_counts, skip_mask, norm1_gain, norm1_bias, token_in, token_in_bias, token_out,
    token_out_bias, norm2_gain, norm2_bias, channel_in, channel_in_bias, channel_out,
    channel_out_bias, cotangent,
):
    f32, bf16 = jnp.float32, jnp.bfloat16
    slots, patches, width = tokens.shape
    layers, in_rows, hidden = channel_in.shape
    keys = token_out.shape[1]
    moves = Moves()
    shards_count = 2 * moves.lines
    inner = keys * shards_count
    rows = -(-patches // 16) * 16
    place = jnp.stack([moves.z, moves.c, moves.q]).astype(jnp.int32)
    kernels = Kernels(place, slots, rows, width, inner, hidden, moves.lines, in_rows)
    wide = kernels.wide

    live = (jnp.arange(slots, dtype=jnp.int32) < image_counts[0]).astype(f32)
    scale = live[:, None, None] * skip_mask.astype(f32)

    def padded(images):
        return jnp.pad(images, ((0, 0), (0, rows - patches), (0, 0)))

    def quarter(array, axis):
        size = array.shape[axis] // 4
        return lax.dynamic_slice_in_dim(array, moves.q * size, size, axis)

    def widen(array):
        return jnp.pad(array, ((0, 0), (0, 0), (0, wide - array.shape[2])))

    gap = jnp.zeros((layers, keys, rows - patches), bf16)
    with_bias = jnp.concatenate([jnp.swapaxes(token_in, 1, 2), gap, token_in_bias[:, :, None]], 2)
    vectors = jnp.stack([norm1_gain, norm1_bias, norm2_gain, norm2_bias, channel_out_bias], 1)
    biases = jnp.pad(channel_in_bias, ((0, 0), (0, 2 * wide - channel_in_bias.shape[1])))
    vectors = jnp.concatenate([widen(vectors), biases.reshape(layers, 2, wide)], 1)
    extra = 16
    vectors = jnp.pad(vectors, ((0, 0), (0, extra - vectors.shape[1]), (0, 0)))
    vectors = jnp.pad(vectors, ((0, 0), (0, keys - extra), (0, 0)))
    packs = jnp.concatenate([widen(with_bias), widen(token_out), vectors], 2).reshape(layers * keys, width)
    b_outs = jnp.pad(token_out_bias.astype(f32), ((0, 0), (0, wide - patches)))[:, :, None]
    scale = scale.reshape(slots, 2 * layers)

    first = Gather(moves, jnp.stack([quarter(channel_in[0], 1), quarter(channel_out[0], 0)]))
    small = Gather(moves, packs)
    shards_held = Held(moves)
    small.direct()
    first.direct()
    shards_held.bring(ins=moves.core(channel_in[0]), outs=moves.core(channel_out[0]))
    shard_in, shard_out = settle((first, small, shards_held), channel_in[1], channel_out[1])
    first.join()
    small.line = jnp.stack([small.part, small.z1, small.z2, small.z3])

    w_cin1 = lax.all_gather(shard_in, "fsdp", axis=0, tiled=True)
    w_cout1 = lax.all_gather(shard_out, "fsdp", axis=0, tiled=True)

    small.core("line")
    first.first()
    began, first.fresh = first.fresh, []
    first.core("line")
    (first.line,) = settle((first, small), first.line)
    first.fresh = began
    found = kernels.unpack_small(small.line, small.line_core, layers, shards_count, extra)
    x0 = padded(tokens)
    (w_in0, w_in_t0, w_out0, w_out_t0, gain1_0, shift1_0, gain2_0, shift2_0, b_cout0, b_cin0) = found[0]
    (w_in1, w_in_t1, w_out1, w_out_t1, gain1_1, shift1_1, gain2_1, shift2_1, b_cout1, b_cin1) = found[1]
    u0, h0, d0, mid0, v0 = kernels.token_forward(
        scale, x0, b_outs, (gain1_0, shift1_0, w_in0, w_out_t0, gain2_0, shift2_0), 0
    )
    (v0,) = settle((first,), v0)

    first.second()
    first.core("x", "y")
    (v0,) = settle((first,), v0)
    first.corner_core()
    (v0,) = settle((first,), v0)
    weights = [channel_in, channel_out, shards_held.ins[None], shards_held.outs[None]] + first.whole()
    hid0, slope0, x1 = kernels.first_forward(scale, v0, mid0, b_cin0, b_cout0, weights)
    u1, h1, d1, mid1, v1 = kernels.token_forward(
        scale, x1, b_outs, (gain1_1, shift1_1, w_in1, w_out_t1, gain2_1, shift2_1), 1
    )
    grad2 = padded(cotangent)
    hid1, slope1, blocks1, low1, g_cout1 = kernels.last_hidden(scale, v1, b_cin1, grad2, w_cin1)

    grad_cout1 = lax.psum_scatter(blocks1, "fsdp", scatter_dimension=0, tiled=True)
    grad_cin1, back, g_cin1 = kernels.last_backward(low1, v1, slope1, w_cout1, w_cin1)
    grad_cin1 = lax.psum_scatter(grad_cin1, "fsdp", scatter_dimension=0, tiled=True)
    grad1, *tokens1, vector1, low0, g_cout0 = kernels.token_backward(
        scale, grad2, back, (mid1, x1, u1, h1, d1), (w_in_t1, w_out1, gain1_1, gain2_1), g_cout1, g_cin1, keys
    )
    mine, theirs = kernels.out_weight_grad(low0, hid0)
    mine, theirs, grad1 = settle((), mine, theirs, grad1)

    sum_out0 = Sum(moves, mine, theirs)
    sum_out0.core()
    mine, theirs, back, g_cin0 = kernels.channel_backward(low0, v0, slope0, weights, 0)
    mine, theirs, back, grad_cout1 = settle((sum_out0,), mine, theirs, back, grad_cout1)

    sum_in0 = Sum(moves, mine, theirs)
    sum_in0.core()
    sum_out0.first()
    grad0, *tokens, vector = kernels.token_backward(
        scale, grad1, back, (mid0, x0, u0, h0, d0), (w_in_t0, w_out0, gain1_0, gain2_0), g_cout0, g_cin0, keys,
        (*tokens1, vector1),
    )
    hid1, grad0, *tokens, vector = settle((sum_in0, sum_out0), hid1, grad0, *tokens, vector)

    sum_tokens = SumSmall(moves, *tokens)
    sum_tokens.core()
    sum_in0.first()
    sum_out0.second()
    vector_sum = SumAll(moves, vector)
    vector_sum.step()
    output = kernels.last_out(scale, hid1, mid1, b_cout1, w_cout1)
    (output,) = settle((sum_in0, sum_out0, sum_tokens, vector_sum), output)

    sum_in0.second()
    sum_out0.once()
    sum_tokens.across(1)
    vector_sum.step()
    output = jnp.swapaxes(output[:, :patches], 0, 1)
    output, grad_cin1, grad_cout1 = settle(
        (sum_in0, sum_out0, sum_tokens, vector_sum), output, grad_cin1, grad_cout1
    )

    sum_in0.once()
    sum_tokens.across(2)
    vector_sum.step()
    share_out0 = Share(moves, sum_out0.total(), 2)
    share_out0.first()
    whole = Copies(moves, grad_cin1, grad_cout1)
    whole.step(1, 2)
    input_grad = jnp.swapaxes(grad0[:, :patches], 0, 1)
    (input_grad,) = settle((sum_in0, sum_tokens, share_out0, whole, vector_sum), input_grad)

    total = sum_in0.total()
    near = [moves.across(total, bits) for bits in (1, 2, 3)]
    share_out0.second()
    whole.add()
    whole.step(2, 1)
    vector_sum.step()
    near = settle((share_out0, whole, vector_sum), *near)
    sum_tokens.along()
    vector_sum.step()
    whole.add()
    finished = kernels.finish_last(*whole.values, 1, layers)
    parts = [(part[None], 0) for part in [total] + list(near)]
    grad_in, grad_out = kernels.finish_first(parts, share_out0.parts(), 0, layers, finished)
    output, input_grad = jnp.swapaxes(output, 0, 1), jnp.swapaxes(input_grad, 0, 1)
    near = sum_tokens.total()

    near = near.reshape(layers, 2, keys, wide)
    grad_t_in = jnp.swapaxes(near[:, 0, :, :patches], 1, 2)
    grad_b_in = near[:, 0, :, rows]
    grad_t_out = near[:, 1, :, :patches]
    sums = vector_sum.value.reshape(layers, 16, width)
    me = lax.axis_index("fsdp")

    def owned(row):
        size = width // shards_count
        return lax.dynamic_slice_in_dim(sums[:, row], me * size, size, 1)

    grad_gain1, grad_shift1, grad_gain2, grad_shift2, grad_b_cout = [owned(row) for row in range(5)]
    size = hidden // shards_count
    grad_b_cin = lax.dynamic_slice(sums, (0, 8 + me // 2, (me % 2) * size), (layers, 1, size))[:, 0]
    bias_total = sums[:, 5, :patches]
    return (
        output, input_grad, grad_gain1, grad_shift1, grad_t_in, grad_b_in, grad_t_out, bias_total,
        grad_gain2, grad_shift2, grad_in, grad_b_cin, grad_out, grad_b_cout,
    )


def fits(mesh):
    return mesh.shape["dp"] == 4 and mesh.shape["fsdp"] == 8


def solution(mesh):
    in_specs = (
        P(("dp", "fsdp"), None, None),
        P(("dp", "fsdp")),
        P(("dp", "fsdp"), None, None),
        P(None, "fsdp"),
        P(None, "fsdp"),
        P(None, None, "fsdp"),
        P(None, "fsdp"),
        P(None, "fsdp", None),
        P(),
        P(None, "fsdp"),
        P(None, "fsdp"),
        P(None, "fsdp", None),
        P(None, "fsdp"),
        P(None, "fsdp", None),
        P(None, "fsdp"),
        P(("dp", "fsdp"), None, None),
    )
    out_specs = (
        P(("dp", "fsdp"), None, None),
        P(("dp", "fsdp"), None, None),
        P(None, "fsdp"),
        P(None, "fsdp"),
        P(None, None, "fsdp"),
        P(None, "fsdp"),
        P(None, "fsdp", None),
        P(),
        P(None, "fsdp"),
        P(None, "fsdp"),
        P(None, "fsdp", None),
        P(None, "fsdp"),
        P(None, "fsdp", None),
        P(None, "fsdp"),
    )
    program = blocked_shards if fits(mesh) else shards
    return jax.shard_map(program, mesh=mesh, in_specs=in_specs, out_specs=out_specs, check_vma=False)
```

```python
import functools
import math

import jax
import jax.numpy as jnp
from jax import lax
from jax.experimental import pallas as pl
from jax.experimental.pallas import tpu as pltpu
from jax.sharding import PartitionSpec as P

EPSILON = 1e-06
GELU_A = math.sqrt(2.0 / math.pi)
GELU_B = 0.044715 * GELU_A
IMAGES = 2
VMEM_BYTES = 60 * 2**20


def as_sent(shard):

    def short(part):
        return part.astype(jnp.bfloat16) if part.dtype == jnp.float32 else part

    return jax.tree.map(short, shard)


def layer_norm(values, gain, shift):
    center = values - jnp.mean(values, -1, keepdims=True)
    inv_std = lax.rsqrt(jnp.mean(center * center, -1, keepdims=True) + EPSILON)
    normed = center * inv_std
    return (normed * gain + shift, normed, inv_std)


def norm_back(grad_out, normed, inv_std, gain):
    grad_gain = jnp.sum(grad_out * normed, axis=(0, 1))
    grad_shift = jnp.sum(grad_out, axis=(0, 1))
    scaled = grad_out * gain
    grad_in = inv_std * (
        scaled
        - jnp.mean(scaled, -1, keepdims=True)
        - normed * jnp.mean(scaled * normed, -1, keepdims=True)
    )
    return (grad_in, grad_gain, grad_shift)


def gelu_back(pre_act, grad_out):
    return jax.vjp(jax.nn.gelu, pre_act)[1](grad_out)[0]


def fetch_forward(pieces):
    return (
        lax.all_gather(pieces[0], "fsdp", axis=0, tiled=True),
        lax.all_gather(pieces[1], "fsdp", axis=0, tiled=True),
        lax.all_gather(pieces[2], "fsdp", axis=1, tiled=True),
        lax.all_gather(pieces[3], "fsdp", axis=0, tiled=True),
        lax.all_gather(pieces[4], "fsdp", axis=0, tiled=True),
        lax.all_gather(pieces[5], "fsdp", axis=0, tiled=True),
        lax.all_gather(pieces[6], "fsdp", axis=0, tiled=True),
        lax.all_gather(pieces[7], "fsdp", axis=0, tiled=True),
        lax.all_gather(pieces[8], "fsdp", axis=0, tiled=True),
        lax.all_gather(pieces[9], "fsdp", axis=0, tiled=True),
        lax.all_gather(pieces[10], "fsdp", axis=0, tiled=True),
    )


def fetch_backward(pieces):
    return (
        lax.all_gather(pieces[0], "fsdp", axis=0, tiled=True),
        lax.all_gather(pieces[1], "fsdp", axis=0, tiled=True),
        lax.all_gather(pieces[2], "fsdp", axis=1, tiled=True),
        lax.all_gather(pieces[3], "fsdp", axis=0, tiled=True),
        lax.all_gather(pieces[4], "fsdp", axis=0, tiled=True),
        lax.all_gather(pieces[5], "fsdp", axis=0, tiled=True),
        lax.all_gather(pieces[6], "fsdp", axis=0, tiled=True),
        lax.all_gather(pieces[7], "fsdp", axis=0, tiled=True),
        lax.all_gather(pieces[8], "fsdp", axis=0, tiled=True),
        lax.all_gather(pieces[9], "fsdp", axis=0, tiled=True),
        lax.all_gather(pieces[10], "fsdp", axis=0, tiled=True),
    )


def shards(
    tokens,
    image_counts,
    skip_mask,
    norm1_gain,
    norm1_bias,
    token_in,
    token_in_bias,
    token_out,
    token_out_bias,
    norm2_gain,
    norm2_bias,
    channel_in,
    channel_in_bias,
    channel_out,
    channel_out_bias,
    cotangent,
):
    f32 = jnp.float32
    bf16 = jnp.bfloat16
    slots = tokens.shape[0]
    layers = norm1_gain.shape[0]
    live = (jnp.arange(slots, dtype=jnp.int32) < image_counts[0]).astype(f32)
    branch_scale = live[:, None, None] * skip_mask.astype(f32)

    def layer_pieces(index):
        return (
            norm1_gain[index],
            norm1_bias[index],
            token_in[index],
            token_in_bias[index],
            token_out[index],
            norm2_gain[index],
            norm2_bias[index],
            channel_in[index],
            channel_in_bias[index],
            channel_out[index],
            channel_out_bias[index],
        )

    values = tokens.astype(f32)
    saved = []
    kept_weights = []
    for index in range(layers):
        weights = fetch_forward(layer_pieces(index))
        kept_weights.append(weights)
        gain1, shift1, w_tin, b_tin, w_tout, gain2, shift2, w_cin, b_cin, w_cout, b_cout = weights
        tok_bias = token_out_bias[index].astype(f32)
        normed1, plain1, inv1 = layer_norm(values, gain1.astype(f32), shift1.astype(f32))
        normed1 = normed1.astype(bf16)
        pre_tok = jnp.einsum(
            "isd,sk->idk", normed1, w_tin, preferred_element_type=f32
        ) + b_tin.astype(f32)
        hidden1 = jax.nn.gelu(pre_tok).astype(bf16)
        branch = (
            jnp.einsum("idk,ks->isd", hidden1, w_tout, preferred_element_type=f32)
            + tok_bias[None, :, None]
        )
        middle = values + branch_scale[:, index, 0][:, None, None] * branch
        normed2, plain2, inv2 = layer_norm(middle, gain2.astype(f32), shift2.astype(f32))
        normed2 = normed2.astype(bf16)
        pre_chan = jnp.einsum(
            "isd,df->isf", normed2, w_cin, preferred_element_type=f32
        ) + b_cin.astype(f32)
        hidden2 = jax.nn.gelu(pre_chan).astype(bf16)
        branch = jnp.einsum(
            "isf,fd->isd", hidden2, w_cout, preferred_element_type=f32
        ) + b_cout.astype(f32)
        values = middle + branch_scale[:, index, 1][:, None, None] * branch
        saved.append(
            (normed1, plain1, inv1, pre_tok, hidden1, normed2, plain2, inv2, pre_chan, hidden2)
        )
    output = values.astype(bf16)
    grad = cotangent.astype(f32)
    local_grads = [None] * layers
    bias_grads = [None] * layers
    for index in reversed(range(layers)):
        weights = fetch_backward(layer_pieces(index))
        gain1, shift1, w_tin, b_tin, w_tout, gain2, shift2, w_cin, b_cin, w_cout, b_cout = weights
        normed1, plain1, inv1, pre_tok, hidden1, normed2, plain2, inv2, pre_chan, hidden2 = saved[
            index
        ]
        out_chan = branch_scale[:, index, 1][:, None, None] * grad
        grad_b_cout = jnp.sum(out_chan, axis=(0, 1))
        low_chan = out_chan.astype(bf16)
        grad_w_cout = jnp.einsum("isf,isd->fd", hidden2, low_chan, preferred_element_type=f32)
        back_hidden = jnp.einsum("isd,fd->isf", low_chan, w_cout, preferred_element_type=f32)
        pre_grad = gelu_back(pre_chan, back_hidden)
        grad_b_cin = jnp.sum(pre_grad, axis=(0, 1))
        low_pre = pre_grad.astype(bf16)
        grad_w_cin = jnp.einsum("isd,isf->df", normed2, low_pre, preferred_element_type=f32)
        back_norm = jnp.einsum("isf,df->isd", low_pre, w_cin, preferred_element_type=f32)
        norm_in, grad_gain2, grad_shift2 = norm_back(back_norm, plain2, inv2, gain2.astype(f32))
        grad_mid = grad + norm_in
        out_tok = branch_scale[:, index, 0][:, None, None] * grad_mid
        bias_grads[index] = jnp.sum(out_tok, axis=(0, 2))
        low_tok = out_tok.astype(bf16)
        grad_w_tout = jnp.einsum("idk,isd->ks", hidden1, low_tok, preferred_element_type=f32)
        back_hidden = jnp.einsum("isd,ks->idk", low_tok, w_tout, preferred_element_type=f32)
        pre_grad = gelu_back(pre_tok, back_hidden)
        grad_b_tin = jnp.sum(pre_grad, axis=(0, 1))
        low_pre = pre_grad.astype(bf16)
        grad_w_tin = jnp.einsum("isd,idk->sk", normed1, low_pre, preferred_element_type=f32)
        back_norm = jnp.einsum("idk,sk->isd", low_pre, w_tin, preferred_element_type=f32)
        norm_in, grad_gain1, grad_shift1 = norm_back(back_norm, plain1, inv1, gain1.astype(f32))
        grad = grad_mid + norm_in
        local = (
            grad_gain1,
            grad_shift1,
            grad_w_tin,
            grad_b_tin,
            grad_w_tout,
            grad_gain2,
            grad_shift2,
            grad_w_cin,
            grad_b_cin,
            grad_w_cout,
            grad_b_cout,
        )
        local_grads[index] = local
    token_bias_total = lax.psum(jnp.stack(bias_grads), ("dp", "fsdp"))
    joined = tuple(
        (
            jnp.stack([local_grads[index][position] for index in range(layers)])
            for position in range(11)
        )
    )
    owned = (
        lax.psum_scatter(joined[0], "fsdp", scatter_dimension=1, tiled=True),
        lax.psum_scatter(joined[1], "fsdp", scatter_dimension=1, tiled=True),
        lax.psum_scatter(joined[2], "fsdp", scatter_dimension=2, tiled=True),
        lax.psum_scatter(joined[3], "fsdp", scatter_dimension=1, tiled=True),
        lax.psum_scatter(joined[4], "fsdp", scatter_dimension=1, tiled=True),
        lax.psum_scatter(joined[5], "fsdp", scatter_dimension=1, tiled=True),
        lax.psum_scatter(joined[6], "fsdp", scatter_dimension=1, tiled=True),
        lax.psum_scatter(joined[7], "fsdp", scatter_dimension=1, tiled=True),
        lax.psum_scatter(joined[8], "fsdp", scatter_dimension=1, tiled=True),
        lax.psum_scatter(joined[9], "fsdp", scatter_dimension=1, tiled=True),
        lax.psum_scatter(joined[10], "fsdp", scatter_dimension=1, tiled=True),
    )
    results = jax.tree.map(lambda part: part.astype(jnp.float32), lax.psum(as_sent(owned), "dp"))
    return (
        output,
        grad,
        results[0],
        results[1],
        results[2],
        results[3],
        results[4],
        token_bias_total,
        results[5],
        results[6],
        results[7],
        results[8],
        results[9],
        results[10],
    )


def norm_parts(values):
    center = values - jnp.mean(values, -1, keepdims=True)
    inv_std = lax.rsqrt(jnp.mean(center * center, -1, keepdims=True) + EPSILON)
    return center * inv_std, inv_std


def norm_input_grad(grad, normed, inv_std):
    return inv_std * (
        grad
        - jnp.mean(grad, -1, keepdims=True)
        - normed * jnp.mean(grad * normed, -1, keepdims=True)
    )


def gelu_pair(value):
    square = value * value
    gate = 0.5 + 0.5 * jnp.tanh(value * (GELU_A + GELU_B * square))
    result = value * gate
    slope = gate + result * (1.0 - gate) * (2.0 * GELU_A + 6.0 * GELU_B * square)
    return result.astype(jnp.bfloat16), slope.astype(jnp.bfloat16)


def dot(left, right, left_dim, right_dim):
    return lax.dot_general(
        left, right, (((left_dim,), (right_dim,)), ((), ())), preferred_element_type=jnp.float32
    )


def chunks(size, count):
    return [slice(k * size // count, (k + 1) * size // count) for k in range(count)]


def position(copy):
    odd = copy & 1
    return 2 * odd + (odd ^ (copy >> 1))


def staggered(parts, product, finish):
    held = product(parts[0])
    for k, part in enumerate(parts):
        later = product(parts[k + 1]) if k + 1 < len(parts) else None
        finish(part, held)
        held = later


def clear(first, *refs):
    @pl.when(first)
    def _():
        for ref in refs:
            ref[...] = jnp.zeros_like(ref)


def unpack_small(place, own, other, *refs):
    vectors = refs[-1]
    z, c = place[0], place[1]
    lines, rows, _ = own.shape
    layers, extra, wide = vectors.shape[1:]
    keys = rows // layers
    for layer in range(layers):
        w_in, w_in_t, w_out, w_out_t, *rest = refs[10 * layer : 10 * layer + 10]
        base = layer * keys
        for source, side in ((own, c), (other, 1 - c)):
            for i in range(lines):
                shard = 2 * (i ^ z) + side
                start = pl.multiple_of(shard * keys, keys)
                w_in[pl.ds(start, keys)] = source[i, base : base + keys, :wide]
                w_out[pl.ds(start, keys)] = source[i, base : base + keys, wide : 2 * wide]
                vectors[shard, layer] = source[i, base : base + extra, 2 * wide :]
        w_in_t[...] = w_in[...].T
        w_out_t[...] = w_out[...].T
        held = [vectors[shard, layer].astype(jnp.float32) for shard in range(vectors.shape[0])]
        for row, target in enumerate(rest[:5]):
            size = target.shape[1] // len(held)
            target[...] = jnp.concatenate([part[row : row + 1, :size] for part in held], axis=1)
        biases = rest[5]
        size = biases.shape[1] // len(held)
        for shard, part in enumerate(held):
            whole = jnp.concatenate([part[5:6], part[6:7]], axis=1)
            biases[:, shard * size : (shard + 1) * size] = whole[:, :size]


def token_branch(values, scale, small, b_out, u_out, hidden_out, slope_out):
    gain1, shift1, w_in, w_out, gain2, shift2 = small
    rows, wide = values.shape[0], w_in.shape[1]
    normed, _ = norm_parts(values)
    u_out[:rows] = (normed * gain1[...] + shift1[...]).astype(jnp.bfloat16)
    below = lax.broadcasted_iota(jnp.int32, (wide - rows, values.shape[1]), 0)
    u_out[rows:] = jnp.where(below == 0, 1.0, 0.0).astype(jnp.bfloat16)
    hidden, slope = gelu_pair(dot(w_in[...], u_out[...], 1, 0))
    hidden_out[...] = hidden
    slope_out[...] = slope
    middle = values + scale * (dot(w_out[:rows], hidden, 1, 0) + b_out[0, :rows])
    normed, _ = norm_parts(middle)
    return middle, (normed * gain2[...] + shift2[...]).astype(jnp.bfloat16)


def token_forward(place, scale, x, b_out, *rest, layer):
    small, (u_out, hidden_out, slope_out, middle_out, v_out) = rest[:6], rest[6:]
    count, rows = x.shape[:2]
    for k in range(count):
        part = scale[count * pl.program_id(0) + k, 2 * layer]
        middle, v = token_branch(
            x[k].astype(jnp.float32), part, small, b_out, u_out.at[k], hidden_out.at[k], slope_out.at[k]
        )
        middle_out[k] = middle
        v_out[k * rows : (k + 1) * rows] = v


def token_grads(scale, grad, back_v, middle, x, u, hidden, slope, w_in, w_out, gain1, gain2, padded):
    rows, width = grad.shape
    normed, inv_std = norm_parts(middle)
    moved = back_v * normed
    sums = [jnp.sum(moved, 0, keepdims=True), jnp.sum(back_v, 0, keepdims=True)]
    grad_mid = grad + norm_input_grad(back_v * gain2[...], normed, inv_std)
    padded[:rows] = (scale * grad_mid).astype(jnp.bfloat16)
    low = padded[...]
    b_out = dot(jnp.ones((8, width), jnp.bfloat16), low, 1, 1)[:1]
    w_out_grad = dot(hidden, low, 1, 1)
    pre = (dot(w_out[...], low, 1, 0) * slope.astype(jnp.float32)).astype(jnp.bfloat16)
    w_in_grad = dot(pre, u, 1, 1)
    back = dot(w_in[:rows], pre, 1, 0)
    normed, inv_std = norm_parts(x)
    sums = [jnp.sum(back * normed, 0, keepdims=True), jnp.sum(back, 0, keepdims=True)] + sums
    return grad_mid + norm_input_grad(back * gain1[...], normed, inv_std), sums, b_out, w_in_grad, w_out_grad


def token_blocks(place, w_in_grad, w_out_grad, whole, put):
    z, c = place[0], place[1]
    keys = whole.shape[1] // 8
    for which, total in ((0, w_in_grad), (1, w_out_grad)):
        whole[which] = total[...].astype(jnp.bfloat16)
        for i in range(4):
            for side, core in ((0, c), (1, 1 - c)):
                start = pl.multiple_of((2 * (i ^ z) + core) * keys, keys)
                put(which, i, side, whole[which, pl.ds(start, keys)])


def token_backward(place, scale, grad, back_v, middle, x, u, hidden, slope, w_in, w_out, gain1, gain2, *rest):
    image = pl.program_id(0)
    g_cout, g_cin = rest[:2]
    last = len(rest) == 2 + 6 + 4
    if last:
        grad_out, mine_out, other_out, vector, low_out, above_grad = rest[2:8]
        layer = 1
    else:
        earlier, grad_out, mine_out, other_out, vector = rest[2:5], *rest[5:9]
        layer = 0
    padded, w_in_grad, w_out_grad, whole = rest[-4:]
    count, rows = x.shape[:2]
    first = image == 0
    clear(first, padded, vector, w_in_grad, w_out_grad)

    @pl.when(first)
    def _():
        vector[4:5] = g_cout[...]
        for j in range(g_cin.shape[0]):
            vector[8 + j : 9 + j] = g_cin[j]
        if not last:
            vector[16:] = earlier[2][...]

    if last:
        clear(first, above_grad)
    found = []
    for k in range(count):
        part = slice(k * rows, (k + 1) * rows)
        result, *sums = token_grads(
            scale[count * image + k, 2 * layer], grad[k].astype(jnp.float32), back_v[part], middle[k],
            x[k].astype(jnp.float32), u[k], hidden[k], slope[k], w_in, w_out, gain1, gain2, padded.at[k],
        )
        grad_out[k] = result
        if last:
            out = scale[count * image + k, 1] * result
            above_grad[...] += jnp.sum(out, 0, keepdims=True)
            low_out[part] = out.astype(jnp.bfloat16)
        found.append(sums)
    for k in range(4):
        vector[k : k + 1] += sum(sums[0][k] for sums in found)
    vector[5:6, : padded.shape[1]] += sum(sums[1] for sums in found)
    w_in_grad[...] += sum(sums[2] for sums in found)
    w_out_grad[...] += sum(sums[3] for sums in found)

    @pl.when(image == pl.num_programs(0) - 1)
    def _():
        targets = (mine_out, other_out)

        def put(which, i, side, part):
            targets[side][i, which] = part

        if not last:
            for side in range(2):
                targets[side][:, 2:] = earlier[side][...]
        token_blocks(place, w_in_grad, w_out_grad, whole, put)


def out_weight_grad(place, low, hidden, mine_out, other_out, turned, whole):
    @pl.when(pl.program_id(0) == 0)
    def _():
        turned[...] = low[...].T

    out_blocks(place, turned, hidden[0], mine_out, other_out, whole)


class Weight:
    def __init__(self, refs, which):
        self.which = which
        self.shards, self.parts = (refs[which], refs[2 + which]), (refs[4 : 4 + 4], refs[8:12])

    def blocks(self, copy, i):
        for side, (line, from_x, from_y, corner) in enumerate(self.parts):
            yield side, (line, from_x, from_y, corner)[copy].at[i - 1, self.which], 0


def fetch_in(place, layer, weight, target, sem):
    z, c, q = place[0], place[1], place[2]
    copies, _, columns = target.shape
    rows = weight.shards[0].shape[1]
    for copy in range(copies):
        j = copy ^ q

        def put(ref, i, side, first):
            start = pl.multiple_of((2 * (i ^ z) + (c ^ side)) * rows + first, 16)
            goal = target.at[j, pl.ds(start, ref.shape[0])]
            pltpu.make_async_copy(ref, goal, sem.at[j]).start()

        for side, shard in enumerate(weight.shards):
            put(shard.at[layer, :, pl.ds(pl.multiple_of(j * columns, columns), columns)], 0, side, 0)
        for i in range(1, copies):
            for side, ref, first in weight.blocks(copy, i):
                put(ref, i, side, first)


def fetch_out(place, layer, weight, target, sem):
    z, c, q = place[0], place[1], place[2]
    lines, part, _ = target.shape
    for i in range(lines):

        def put(ref, start):
            goal = target.at[i ^ z, pl.ds(pl.multiple_of(start, 16), ref.shape[0])]
            pltpu.make_async_copy(ref, goal, sem.at[i ^ z]).start()

        if i == 0:
            for side, shard in enumerate(weight.shards):
                put(shard.at[layer], (c ^ side) * (part // 2))
            continue
        for copy in range(4):
            for side, ref, first in weight.blocks(copy, i):
                put(ref, (c ^ side) * (part // 2) + (copy ^ q) * (part // 8) + first)


def arrive(weight, sem, step):
    pltpu.make_async_copy(weight.at[step], weight.at[step], sem.at[step]).wait()


def out_blocks(place, turned, hidden, mine_out, other_out, whole):
    c, q = place[1], place[2]
    whole[...] = dot(turned[...], hidden, 1, 0).astype(jnp.bfloat16)
    copies, _, rows, columns = mine_out.shape
    size = columns // 2
    for side, target in ((c, mine_out), (1 - c, other_out)):
        units = pl.ds(pl.multiple_of(side * size, 128), size)
        for j in range(copies):
            start = 2 * j * rows
            target[position(j ^ q), 0, :, :size] = whole[start : start + rows, units]
            target[position(j ^ q), 0, :, size:] = whole[start + rows : start + 2 * rows, units]


def first_forward(place, scale, v, middle, bias_in, bias_out, *rest):
    weight_in, weight_out = Weight(rest[:12], 0), Weight(rest[:12], 1)
    hidden_out, slope_out, x_out, w_in, w_out, hidden, total, sem_in, sem_out = rest[12:]
    step = pl.program_id(0)
    rows = middle.shape[1]

    @pl.when(step == 0)
    def _():
        fetch_in(place, 0, weight_in, w_in, sem_in)
        fetch_out(place, 0, weight_out, w_out, sem_out)
        total[...] = jnp.zeros_like(total)

    @pl.when(step < 4)
    def _():
        j = (step & 3) ^ place[2]
        arrive(w_in, sem_in, j)
        def product(part):
            return dot(v[part], w_in[j], 1, 0) + bias_in[...]

        def finish(part, found):
            value, slope = gelu_pair(found)
            hidden_out[0, part] = value
            hidden[j, part] = value
            slope_out[0, part] = slope

        staggered(chunks(v.shape[0], 4), product, finish)

    @pl.when(step >= 4)
    def _():
        j = (step & 3) ^ place[0]
        arrive(w_out, sem_out, j)
        total[...] += dot(hidden[j], w_out[j], 1, 0)

    @pl.when(step == 7)
    def _():
        for image in range(middle.shape[0]):
            branch = total[image * rows : (image + 1) * rows] + bias_out[...]
            x_out[image] = middle[image] + scale[image, 1] * branch


def last_hidden(place, scale, v, bias, grad, w_in, hidden_out, slope_out, blocks_out, low_out, bias_grad, hidden, turned):
    step = pl.program_id(0)

    @pl.when(step == 0)
    def _():
        rows = grad.shape[1]
        sums = 0.0
        for image in range(grad.shape[0]):
            out = scale[image, 3] * grad[image].astype(jnp.float32)
            sums = sums + jnp.sum(out, 0, keepdims=True)
            low_out[image * rows : (image + 1) * rows] = out.astype(jnp.bfloat16)
        bias_grad[...] = sums
        turned[...] = low_out[...].T

    @pl.when(step < 4)
    def _():
        def product(part):
            return dot(v[part], w_in[...], 1, 0) + bias[...]

        def finish(part, found):
            value, slope = gelu_pair(found)
            hidden_out[0, part] = value
            hidden[step & 3, part] = value
            slope_out[0, part] = slope

        staggered(chunks(v.shape[0], 4), product, finish)

    @pl.when(step >= 4)
    def _():
        found = dot(turned[...], hidden[step & 3], 1, 0).astype(jnp.bfloat16)
        size = blocks_out.shape[2]
        for k in range(blocks_out.shape[0]):
            blocks_out[k] = found[:, k * size : (k + 1) * size]


def last_out(place, scale, hidden, middle, bias, w_out, x_out, total):
    step = pl.program_id(0)

    @pl.when(step == 0)
    def _():
        total[...] = jnp.zeros_like(total)

    total[...] += dot(hidden[0], w_out[...], 1, 0)

    @pl.when(step == pl.num_programs(0) - 1)
    def _():
        for image in range(middle.shape[0]):
            rows = middle.shape[1]
            branch = total[image * rows : (image + 1) * rows] + bias[...]
            x_out[image] = (middle[image] + scale[image, 3] * branch).astype(x_out.dtype)


def last_backward(place, low, v, slope, w_out, w_in, in_out, back_out, bias_grad, turned, pre):
    @pl.when(pl.program_id(0) == 0)
    def _():
        turned[...] = v[...].T
        back_out[...] = jnp.zeros_like(back_out)

    sums = []

    def product(part):
        return dot(low[part], w_out[...], 1, 1)

    def finish(part, found):
        grad = found * slope[0, part].astype(jnp.float32)
        sums.append(jnp.sum(grad, 0, keepdims=True))
        pre[part] = grad.astype(jnp.bfloat16)

    staggered(chunks(low.shape[0], 2), product, finish)
    bias_grad[0] = sum(sums)
    for part in chunks(turned.shape[0], 3):
        in_out[part] = dot(turned[part], pre[...], 1, 0).astype(jnp.bfloat16)
    back_out[...] += dot(pre[...], w_in[...], 1, 1)


def channel_backward(place, low, v, slope, *rest, layer):
    mine, theirs, back_out, bias_grad, w_out, w_in, turned, pre, whole, sem_out, sem_in = rest[12:]
    z, c = place[0], place[1]
    step = pl.program_id(0)

    @pl.when(step == 0)
    def _():
        fetch_out(place, layer, Weight(rest[:12], 1), w_out, sem_out)
        fetch_in(place, layer, Weight(rest[:12], 0), w_in, sem_in)
        turned[...] = v[...].T
        back_out[...] = jnp.zeros_like(back_out)

    j = step ^ z
    arrive(w_out, sem_out, j)
    arrive(w_in, sem_in, j)
    sums = []

    def product(part):
        return dot(low[part], w_out[j], 1, 1)

    def finish(part, found):
        grad = found * slope[0, part].astype(jnp.float32)
        sums.append(jnp.sum(grad, 0, keepdims=True))
        pre[part] = grad.astype(jnp.bfloat16)

    staggered(chunks(low.shape[0], 2), product, finish)
    bias_grad[0] = sum(sums)
    for part in chunks(turned.shape[0], 3):
        whole[part] = dot(turned[part], pre[...], 1, 0).astype(jnp.bfloat16)
    lines = mine.shape[1]
    rows = whole.shape[0] // (2 * lines)
    for i in range(lines):
        for side, target in ((c, mine), (1 - c, theirs)):
            start = pl.multiple_of((2 * (i ^ z) + side) * rows, rows)
            target[0, i] = whole[pl.ds(start, rows)]
    back_out[...] += dot(pre[...], w_in[j], 1, 1)


def finish_last(place, grad_in, got_in, grad_out, got_out, in_out, out_out):
    in_out[0] = grad_in[...].astype(jnp.float32) + got_in[...].astype(jnp.float32)
    out_out[0] = (grad_out[0].astype(jnp.float32) + got_out[0].astype(jnp.float32)).T


def finish_first(place, *refs):
    parts_in, parts_out = refs[:4], refs[4:8]
    in_out, out_out, whole = refs[-3:]
    for j in range(4):
        columns = parts_in[j].shape[2]
        start = pl.multiple_of((j ^ place[2]) * columns, columns)
        in_out[0, :, pl.ds(start, columns)] = parts_in[j][0].astype(jnp.float32)
        rows, columns = parts_out[j].shape[1:]
        for half in range(2):
            start = pl.multiple_of((2 * (j ^ place[2]) + half) * rows, rows)
            part = parts_out[j][0, :, half * columns // 2 : (half + 1) * columns // 2]
            whole[pl.ds(start, rows)] = part.astype(jnp.float32)
    out_out[0] = whole[...].T


class Kernels:
    def __init__(self, place, slots, rows, width, inner, hidden, lines, block):
        self.place = place
        self.slots, self.rows, self.width = slots, rows, width
        self.inner, self.hidden = inner, hidden
        self.lines, self.block = lines, block
        self.part = hidden // 4
        self.wide = 256

    def run(self, body, steps, inputs, outputs, scratch, flops, aliases=None, **fixed):
        sizes = sum(a.size * a.dtype.itemsize for a, _, _ in inputs)
        sizes += sum(math.prod(o[0]) * jnp.dtype(o[1]).itemsize for o in outputs)

        def spec(block, index):
            if isinstance(block, tuple):
                return pl.BlockSpec(block, index)
            return pl.BlockSpec(memory_space=block)

        return pl.pallas_call(
            functools.partial(body, **fixed) if fixed else body,
            name=body.__name__,
            grid_spec=pltpu.PrefetchScalarGridSpec(
                num_scalar_prefetch=1,
                grid=(steps,),
                in_specs=[spec(block, index) for _, block, index in inputs],
                out_specs=[spec(o[2], o[3]) for o in outputs],
                scratch_shapes=scratch,
            ),
            out_shape=[jax.ShapeDtypeStruct(o[0], o[1]) for o in outputs],
            input_output_aliases=aliases or {},
            compiler_params=pltpu.CompilerParams(
                dimension_semantics=("arbitrary",), vmem_limit_bytes=VMEM_BYTES
            ),
            cost_estimate=pl.CostEstimate(flops=flops, bytes_accessed=sizes, transcendentals=0),
        )(self.place, *[a for a, _, _ in inputs])

    def image(self, array):
        return (array, (1,) + array.shape[1:], lambda i, s: (i, 0, 0))

    def fixed(self, array):
        zeros = (0,) * array.ndim
        return (array, array.shape, lambda i, s: zeros)

    def scalars(self, array):
        return (array, pltpu.SMEM, None)

    def in_hbm(self, arrays):
        return [(a, pltpu.HBM, None) for a in arrays]

    def fixed_out(self, shape, dtype):
        zeros = (0,) * len(shape)
        return (shape, dtype, shape, lambda i, s: zeros)

    def columns(self, array, count):
        return (array, (array.shape[0], array.shape[1] // count), lambda i, s: (0, i))

    def columns_out(self, rows, columns, count, dtype):
        return ((rows, columns), dtype, (rows, columns // count), lambda i, s: (0, i))

    def late(self, step, start):
        return jnp.clip(step - start, 0, 3)

    def images_out(self, rows, dtype):
        block = (IMAGES, rows, self.width)
        return ((self.slots, rows, self.width), dtype, block, lambda i, s: (i, 0, 0))

    def images(self, array):
        return (array, (IMAGES,) + array.shape[1:], lambda i, s: (i, 0, 0))

    def rows_out(self):
        shape = (self.slots * self.rows, self.width)
        return (shape, jnp.bfloat16, (IMAGES * self.rows, self.width), lambda i, s: (i, 0))

    def quarters(self, array, which, start=0):
        return (array, (1,) + array.shape[1:], lambda i, s: (self.late(i, start) ^ s[which], 0, 0))

    def quarters_out(self, which, start=0):
        rows = self.slots * self.rows
        block = (1, rows, self.part)
        return ((4,) + block[1:], jnp.bfloat16, block, lambda i, s: (self.late(i, start) ^ s[which], 0, 0))

    def row(self, array, which, start=0):
        return (array, (1, self.part), lambda i, s: (0, self.late(i, start) ^ s[which]))

    def out_blocks_out(self, start=0):
        block = (4, 1, self.block, self.width)
        shape = (4, self.lines) + block[2:]
        return (shape, jnp.bfloat16, block, lambda i, s: (0, self.late(i, start), 0, 0))

    def product(self):
        return 2 * self.slots * self.rows * self.width * self.hidden

    def unpack_small(self, own, other, layers, shards, extra):
        bf16, f32 = jnp.bfloat16, jnp.float32
        inner, wide, width = self.inner, self.wide, self.width
        outputs = [((inner, wide), bf16), ((wide, inner), bf16)] * 2
        outputs += [((1, width), f32)] * 5 + [((1, self.hidden), f32)]
        found = self.run(
            unpack_small,
            1,
            [self.fixed(own), self.fixed(other)],
            [self.fixed_out(*part) for part in outputs * layers],
            [pltpu.VMEM((shards, layers, extra, wide), bf16)],
            0,
        )
        return [list(found[10 * layer : 10 * layer + 10]) for layer in range(layers)]

    def token_product(self):
        return 2 * self.slots * self.wide * self.width * self.inner

    def b_out(self, array, layer):
        return (array, (1,) + array.shape[1:], lambda i, s: (layer, 0, 0))

    def token_outs(self):
        bf16 = jnp.bfloat16
        outs = [self.images_out(rows, bf16) for rows in (self.wide, self.inner, self.inner)]
        return outs + [self.images_out(self.rows, jnp.float32), self.rows_out()]

    def token_forward(self, scale, x, b_out, small, layer):
        return self.run(
            token_forward,
            self.slots // IMAGES,
            [self.scalars(scale), self.images(x), self.b_out(b_out, layer)] + [self.fixed(a) for a in small],
            self.token_outs(),
            [],
            2 * self.token_product(),
            layer=layer,
        )

    def first_forward(self, scale, v, middle, bias_in, bias_out, weights):
        bf16, f32 = jnp.bfloat16, jnp.float32
        rows = self.slots * self.rows
        return self.run(
            first_forward,
            8,
            [self.scalars(scale), self.fixed(v), self.fixed(middle), self.row(bias_in, 2), self.fixed(bias_out)]
            + self.in_hbm(weights),
            [self.quarters_out(2)] * 2 + [self.fixed_out((self.slots, self.rows, self.width), f32)],
            [
                self.weight(),
                self.weight(),
                pltpu.VMEM((4, rows, self.part), bf16),
                pltpu.VMEM((rows, self.width), f32),
                pltpu.SemaphoreType.DMA((4,)),
                pltpu.SemaphoreType.DMA((4,)),
            ],
            2 * self.product(),
        )

    def steps(self, array):
        return (array, (1,) + array.shape[1:], lambda i, s: (jnp.minimum(i, 3), 0, 0))

    def steps_out(self):
        block = (1, self.slots * self.rows, self.part)
        return ((4,) + block[1:], jnp.bfloat16, block, lambda i, s: (jnp.minimum(i, 3), 0, 0))

    def columns_in(self, array):
        return (array, (array.shape[0], self.part), lambda i, s: (0, jnp.minimum(i, 3)))

    def rows_in(self, array):
        return (array, (self.part, array.shape[1]), lambda i, s: (i, 0))

    def last_hidden(self, scale, v, bias, grad, w_in):
        bf16, f32 = jnp.bfloat16, jnp.float32
        rows = self.slots * self.rows
        block = (2, self.width, self.part // 2)
        return self.run(
            last_hidden,
            8,
            [self.scalars(scale), self.fixed(v), self.columns_in(bias), self.fixed(grad), self.columns_in(w_in)],
            [self.steps_out()] * 2
            + [((8,) + block[1:], bf16, block, lambda i, s: (jnp.maximum(i - 4, 0), 0, 0))]
            + [self.fixed_out((rows, self.width), bf16), self.fixed_out((1, self.width), f32)],
            [pltpu.VMEM((4, rows, self.part), bf16), pltpu.VMEM((self.width, rows), bf16)],
            2 * self.product(),
        )

    def last_out(self, scale, hidden, middle, bias, w_out):
        return self.run(
            last_out,
            4,
            [self.scalars(scale), self.steps(hidden), self.fixed(middle), self.fixed(bias), self.rows_in(w_out)],
            [self.fixed_out(middle.shape, jnp.bfloat16)],
            [pltpu.VMEM((self.slots * self.rows, self.width), jnp.float32)],
            self.product(),
        )[0]

    def last_backward(self, low, v, slope, w_out, w_in):
        bf16, f32 = jnp.bfloat16, jnp.float32
        rows = self.slots * self.rows
        return self.run(
            last_backward,
            4,
            [self.fixed(low), self.fixed(v), self.steps(slope), self.rows_in(w_out), self.columns_in(w_in)],
            [
                ((self.width, self.hidden), bf16, (self.width, self.part), lambda i, s: (0, i)),
                self.fixed_out((rows, self.width), f32),
                ((4, 1, self.part), f32, (1, 1, self.part), lambda i, s: (i, 0, 0)),
            ],
            [pltpu.VMEM((self.width, rows), bf16), pltpu.VMEM((rows, self.part), bf16)],
            3 * self.product(),
        )

    def token_backward(self, scale, grad, back, kept, small, g_cout, g_cin, keys, earlier=()):
        bf16, f32 = jnp.bfloat16, jnp.float32
        width = self.width
        middle, x, u, hidden, slope = kept
        inputs = [self.scalars(scale), self.images(grad)]
        inputs += [(back, (IMAGES * self.rows, width), lambda i, s: (i, 0))]
        inputs += [self.images(a) for a in (middle, x, u, hidden, slope)]
        inputs += [self.fixed(a) for a in tuple(small) + (g_cout, g_cin) + tuple(earlier)]
        outputs = [self.images_out(self.rows, f32)]
        outputs += [self.fixed_out((self.lines, 4 if earlier else 2, keys, self.wide), bf16)] * 2
        outputs += [self.fixed_out((32 if earlier else 16, width), f32)]
        if not earlier:
            outputs += [self.rows_out(), self.fixed_out((1, width), f32)]
        return self.run(
            token_backward,
            self.slots // IMAGES,
            inputs,
            outputs,
            [
                pltpu.VMEM((IMAGES, self.wide, width), bf16),
                pltpu.VMEM((self.inner, self.wide), f32),
                pltpu.VMEM((self.inner, self.wide), f32),
                pltpu.VMEM((2, self.inner, self.wide), bf16),
            ],
            4 * self.token_product(),
        )

    def out_weight_grad(self, low, hidden):
        rows = self.slots * self.rows
        return self.run(
            out_weight_grad,
            4,
            [self.fixed(low), self.quarters(hidden, 0)],
            [self.out_blocks_out()] * 2,
            [pltpu.VMEM((self.width, rows), jnp.bfloat16), pltpu.VMEM((self.width, self.part), jnp.bfloat16)],
            self.product(),
        )

    def weight(self):
        return pltpu.VMEM((4, self.width, self.part), jnp.bfloat16)

    def out_forward(self, scale, hidden, middle, bias, weights, layer, dtype):
        return self.run(
            out_forward,
            4,
            [self.scalars(scale), self.quarters(hidden, 0), self.fixed(middle), self.fixed(bias)]
            + self.in_hbm(weights),
            [self.fixed_out(middle.shape, dtype)],
            [
                self.weight(),
                pltpu.VMEM((self.slots * self.rows, self.width), jnp.float32),
                pltpu.SemaphoreType.DMA((4,)),
            ],
            self.product(),
            layer=layer,
        )[0]

    def channel_backward(self, low, v, slope, weights, layer):
        bf16, f32 = jnp.bfloat16, jnp.float32
        rows = self.slots * self.rows
        block = (1, self.lines, self.block, self.width)
        shape = (4, self.lines, self.block, self.width)
        blocks = (shape, bf16, block, lambda j, s: (position(j ^ s[0] ^ s[2]), 0, 0, 0))
        return self.run(
            channel_backward,
            4,
            [self.fixed(low), self.fixed(v), self.quarters(slope, 0)]
            + self.in_hbm(weights),
            [
                blocks,
                blocks,
                self.fixed_out((rows, self.width), f32),
                ((4, 1, self.part), f32, (1, 1, self.part), lambda i, s: (i ^ s[0], 0, 0)),
            ],
            [
                self.weight(),
                self.weight(),
                pltpu.VMEM((self.width, rows), bf16),
                pltpu.VMEM((rows, self.part), bf16),
                pltpu.VMEM((self.width, self.part), bf16),
                pltpu.SemaphoreType.DMA((4,)),
                pltpu.SemaphoreType.DMA((4,)),
            ],
            3 * self.product(),
            layer=layer,
        )

    def shard_outs(self, layer, layers):
        shapes = (layers, self.block, self.hidden), (layers, self.part // 2, self.width)
        return [(shape, jnp.float32, (1,) + shape[1:], lambda i, s: (layer, 0, 0)) for shape in shapes]

    def finish_last(self, whole, layer, layers):
        inputs = [self.fixed(a) for a in (whole.values[0], whole.got0, whole.values[1], whole.got1)]
        return self.run(finish_last, 1, inputs, self.shard_outs(layer, layers), [], 0)

    def finish_first(self, parts_in, parts_out, layer, layers, earlier):
        def one(part):
            array, index = part
            return (array, (1,) + array.shape[1:], lambda i, s: (index, 0, 0))

        inputs = [one(part) for part in parts_in + parts_out]
        return self.run(
            finish_first,
            1,
            inputs + self.in_hbm(earlier),
            self.shard_outs(layer, layers),
            [pltpu.VMEM((self.width, self.part // 2), jnp.float32)],
            0,
            {1 + len(inputs): 0, 2 + len(inputs): 1},
        )


class Moves:
    def __init__(self):
        self.lines = lax.axis_size("fsdp") // 2
        self.copies = lax.axis_size("dp")
        me = lax.axis_index("fsdp")
        self.z, self.c, self.q = me // 2, me % 2, lax.axis_index("dp")

    def along(self, values, bits):
        return lax.ppermute(values, "fsdp", [(f, f ^ (2 * bits)) for f in range(2 * self.lines)])

    def core(self, values):
        return lax.ppermute(values, "fsdp", [(f, f ^ 1) for f in range(2 * self.lines)])

    def across(self, values, bits):
        return lax.ppermute(values, "dp", [(q, q ^ bits) for q in range(self.copies)])


class Held:
    def __init__(self, moves):
        self.moves, self.fresh = moves, []
        self.half = moves.lines // 2

    def bring(self, **arrays):
        for name, array in arrays.items():
            setattr(self, name, array)
            self.fresh.append(name)


def settle(held, *values):
    names = [(part, name) for part in held for name in part.fresh]
    arrays = tuple(getattr(part, name) for part, name in names)
    arrays = lax.optimization_barrier(tuple(values) + arrays)
    for (part, name), array in zip(names, arrays[len(values) :]):
        setattr(part, name, array)
    for part in held:
        part.fresh = []
    return arrays[: len(values)]


class Gather(Held):
    def __init__(self, moves, part):
        super().__init__(moves)
        self.part = part

    def direct(self):
        self.bring(**{"z%d" % i: self.moves.along(self.part, i) for i in range(1, self.moves.lines)})

    def join(self):
        self.line = jnp.stack([getattr(self, "z%d" % i) for i in range(1, self.moves.lines)])

    def first(self):
        self.bring(x=self.moves.across(self.line, 1), y=self.moves.across(self.line, 2))

    def second(self):
        self.bring(low=self.moves.across(self.y[:, :1], 1), high=self.moves.across(self.x[:, 1:], 2))

    def corner_core(self):
        self.corner = jnp.concatenate([self.low, self.high], 1)
        self.core("corner")

    def core(self, *names):
        self.bring(**{name + "_core": self.moves.core(getattr(self, name)) for name in names})

    def whole(self):
        names = ("line", "x", "y", "corner")
        return [getattr(self, name) for name in names] + [getattr(self, name + "_core") for name in names]


class Sum(Held):
    def __init__(self, moves, mine, other):
        super().__init__(moves)
        self.mine, self.theirs = mine, other
        self.low, self.high = slice(0, self.half), slice(self.half, None)

    def both(self, copies, part):
        return self.mine[copies, part] + self.got[copies, part]

    def core(self):
        self.bring(got=self.moves.core(self.theirs))

    def first(self):
        self.bring(
            from_x=self.moves.across(self.both(slice(2, 4), self.low), 1),
            from_y=self.moves.across(self.both(slice(1, 3), self.high), 2),
        )

    def second(self):
        self.bring(
            low2=self.moves.across(self.both(1, self.low) + self.from_x[0], 2),
            high1=self.moves.across(self.both(3, self.high) + self.from_y[1], 1),
        )

    def halves(self):
        low = self.both(0, self.low) + self.from_x[1] + self.low2
        high = self.both(0, self.high) + self.from_y[0] + self.high1
        return low, high

    def once(self):
        low, high = self.halves()
        self.block = low[0]
        blocks = [low[i] for i in range(1, self.half)] + [high[i] for i in range(self.half)]
        self.bring(**{"z%d" % (i + 1): self.moves.along(block, i + 1) for i, block in enumerate(blocks)})

    def far(self):
        self.block, high = self.halves()
        self.bring(z=self.moves.along(high, 2))

    def near(self):
        pair = self.block + self.z
        self.block = pair[0]
        self.bring(z1=self.moves.along(pair[1], 1))

    def total(self):
        total = self.block.astype(jnp.float32)
        for i in range(1, self.moves.lines):
            if hasattr(self, "z%d" % i):
                total = total + getattr(self, "z%d" % i).astype(jnp.float32)
        return total.astype(jnp.bfloat16)


class Share(Held):
    def __init__(self, moves, part, axis):
        super().__init__(moves)
        self.part, self.axis = part, axis

    def first(self):
        self.bring(near=self.moves.across(self.part, self.axis))

    def second(self):
        self.bring(far=self.moves.across(jnp.stack([self.part, self.near]), 3 - self.axis))

    def parts(self):
        near, far = (self.near[None], 0), (self.far, 0)
        return [(self.part[None], 0)] + ([near, far] if self.axis == 1 else [far, near]) + [(self.far, 1)]


class SumSmall(Held):
    def __init__(self, moves, mine, other):
        super().__init__(moves)
        self.mine, self.theirs = mine, other

    def core(self):
        self.bring(got=self.moves.core(self.theirs))

    def along(self):
        both = self.mine + self.got
        self.value = both[0]
        self.bring(**{"z%d" % i: self.moves.along(both[i], i) for i in range(1, self.moves.lines)})

    def across(self, bits):
        if bits == 1:
            parts = [self.value] + [getattr(self, "z%d" % i) for i in range(1, self.moves.lines)]
            self.value = sum(part.astype(jnp.float32) for part in parts).astype(jnp.bfloat16)
        else:
            self.value = self.value + self.got
        self.bring(got=self.moves.across(self.value, bits))

    def total(self):
        return self.value.astype(jnp.float32) + self.got.astype(jnp.float32)


class Copies(Held):
    def __init__(self, moves, *values):
        super().__init__(moves)
        self.values = list(values)

    def step(self, *axes):
        got = [self.moves.across(value, bits) for value, bits in zip(self.values, axes)]
        self.bring(got0=got[0], got1=got[1])

    def add(self):
        self.values = [self.values[0] + self.got0, self.values[1] + self.got1]


class SumAll(Held):
    def __init__(self, moves, value):
        super().__init__(moves)
        self.value, self.bit = value, 1

    def step(self):
        count = 2 * self.moves.lines
        got = lax.ppermute(self.value, "fsdp", [(i, i ^ self.bit) for i in range(count)])
        self.bit *= 2
        self.bring(value=self.value + got)

    def copies(self):
        self.bring(**{"q%d" % bits: self.moves.across(self.value, bits) for bits in (1, 2, 3)})

    def total(self):
        return (self.value + self.q1) + (self.q2 + self.q3)


def blocked_shards(
    tokens, image_counts, skip_mask, norm1_gain, norm1_bias, token_in, token_in_bias, token_out,
    token_out_bias, norm2_gain, norm2_bias, channel_in, channel_in_bias, channel_out,
    channel_out_bias, cotangent,
):
    f32, bf16 = jnp.float32, jnp.bfloat16
    slots, patches, width = tokens.shape
    layers, in_rows, hidden = channel_in.shape
    keys = token_out.shape[1]
    moves = Moves()
    shards_count = 2 * moves.lines
    inner = keys * shards_count
    rows = -(-patches // 16) * 16
    place = jnp.stack([moves.z, moves.c, moves.q]).astype(jnp.int32)
    kernels = Kernels(place, slots, rows, width, inner, hidden, moves.lines, in_rows)
    wide = kernels.wide

    live = (jnp.arange(slots, dtype=jnp.int32) < image_counts[0]).astype(f32)
    scale = live[:, None, None] * skip_mask.astype(f32)

    def padded(images):
        return jnp.pad(images, ((0, 0), (0, rows - patches), (0, 0)))

    def quarter(array, axis):
        size = array.shape[axis] // 4
        return lax.dynamic_slice_in_dim(array, moves.q * size, size, axis)

    def widen(array):
        return jnp.pad(array, ((0, 0), (0, 0), (0, wide - array.shape[2])))

    gap = jnp.zeros((layers, keys, rows - patches), bf16)
    with_bias = jnp.concatenate([jnp.swapaxes(token_in, 1, 2), gap, token_in_bias[:, :, None]], 2)
    vectors = jnp.stack([norm1_gain, norm1_bias, norm2_gain, norm2_bias, channel_out_bias], 1)
    biases = jnp.pad(channel_in_bias, ((0, 0), (0, 2 * wide - channel_in_bias.shape[1])))
    vectors = jnp.concatenate([widen(vectors), biases.reshape(layers, 2, wide)], 1)
    extra = 16
    vectors = jnp.pad(vectors, ((0, 0), (0, extra - vectors.shape[1]), (0, 0)))
    vectors = jnp.pad(vectors, ((0, 0), (0, keys - extra), (0, 0)))
    packs = jnp.concatenate([widen(with_bias), widen(token_out), vectors], 2).reshape(layers * keys, width)
    b_outs = jnp.pad(token_out_bias.astype(f32), ((0, 0), (0, wide - patches)))[:, :, None]
    scale = scale.reshape(slots, 2 * layers)

    first = Gather(moves, jnp.stack([quarter(channel_in[0], 1), quarter(channel_out[0], 0)]))
    small = Gather(moves, packs)
    shards_held = Held(moves)
    small.direct()
    first.direct()
    shards_held.bring(ins=moves.core(channel_in[0]), outs=moves.core(channel_out[0]))
    shard_in, shard_out = settle((first, small, shards_held), channel_in[1], channel_out[1])
    first.join()
    small.line = jnp.stack([small.part, small.z1, small.z2, small.z3])

    w_cin1 = lax.all_gather(shard_in, "fsdp", axis=0, tiled=True)
    w_cout1 = lax.all_gather(shard_out, "fsdp", axis=0, tiled=True)

    small.core("line")
    first.first()
    began, first.fresh = first.fresh, []
    first.core("line")
    (first.line,) = settle((first, small), first.line)
    first.fresh = began
    found = kernels.unpack_small(small.line, small.line_core, layers, shards_count, extra)
    x0 = padded(tokens)
    (w_in0, w_in_t0, w_out0, w_out_t0, gain1_0, shift1_0, gain2_0, shift2_0, b_cout0, b_cin0) = found[0]
    (w_in1, w_in_t1, w_out1, w_out_t1, gain1_1, shift1_1, gain2_1, shift2_1, b_cout1, b_cin1) = found[1]
    u0, h0, d0, mid0, v0 = kernels.token_forward(
        scale, x0, b_outs, (gain1_0, shift1_0, w_in0, w_out_t0, gain2_0, shift2_0), 0
    )
    (v0,) = settle((first,), v0)

    first.second()
    first.core("x", "y")
    (v0,) = settle((first,), v0)
    first.corner_core()
    (v0,) = settle((first,), v0)
    weights = [channel_in, channel_out, shards_held.ins[None], shards_held.outs[None]] + first.whole()
    hid0, slope0, x1 = kernels.first_forward(scale, v0, mid0, b_cin0, b_cout0, weights)
    u1, h1, d1, mid1, v1 = kernels.token_forward(
        scale, x1, b_outs, (gain1_1, shift1_1, w_in1, w_out_t1, gain2_1, shift2_1), 1
    )
    grad2 = padded(cotangent)
    hid1, slope1, blocks1, low1, g_cout1 = kernels.last_hidden(scale, v1, b_cin1, grad2, w_cin1)

    grad_cout1 = lax.psum_scatter(blocks1, "fsdp", scatter_dimension=0, tiled=True)
    grad_cin1, back, g_cin1 = kernels.last_backward(low1, v1, slope1, w_cout1, w_cin1)
    grad_cin1 = lax.psum_scatter(grad_cin1, "fsdp", scatter_dimension=0, tiled=True)
    grad1, *tokens1, vector1, low0, g_cout0 = kernels.token_backward(
        scale, grad2, back, (mid1, x1, u1, h1, d1), (w_in_t1, w_out1, gain1_1, gain2_1), g_cout1, g_cin1, keys
    )
    mine, theirs = kernels.out_weight_grad(low0, hid0)
    mine, theirs, grad1 = settle((), mine, theirs, grad1)

    sum_out0 = Sum(moves, mine, theirs)
    sum_out0.core()
    mine, theirs, back, g_cin0 = kernels.channel_backward(low0, v0, slope0, weights, 0)
    mine, theirs, back, grad_cout1 = settle((sum_out0,), mine, theirs, back, grad_cout1)

    sum_in0 = Sum(moves, mine, theirs)
    sum_in0.core()
    sum_out0.first()
    grad0, *tokens, vector = kernels.token_backward(
        scale, grad1, back, (mid0, x0, u0, h0, d0), (w_in_t0, w_out0, gain1_0, gain2_0), g_cout0, g_cin0, keys,
        (*tokens1, vector1),
    )
    hid1, grad0, *tokens, vector = settle((sum_in0, sum_out0), hid1, grad0, *tokens, vector)

    sum_tokens = SumSmall(moves, *tokens)
    sum_tokens.core()
    sum_in0.first()
    sum_out0.second()
    vector_sum = SumAll(moves, vector)
    vector_sum.step()
    output = kernels.last_out(scale, hid1, mid1, b_cout1, w_cout1)
    output, grad_cin1, grad_cout1 = settle(
        (sum_in0, sum_out0, sum_tokens, vector_sum), output, grad_cin1, grad_cout1
    )

    sum_in0.second()
    sum_out0.once()
    sum_tokens.along()
    vector_sum.step()
    whole = Copies(moves, grad_cin1, grad_cout1)
    whole.step(1, 2)
    output = jnp.swapaxes(output[:, :patches], 0, 1)
    (output,) = settle((sum_in0, sum_out0, sum_tokens, whole, vector_sum), output)

    sum_in0.once()
    sum_tokens.across(1)
    vector_sum.step()
    share_out0 = Share(moves, sum_out0.total(), 2)
    share_out0.first()
    whole.add()
    whole.step(2, 1)
    input_grad = jnp.swapaxes(grad0[:, :patches], 0, 1)
    (input_grad,) = settle((sum_in0, sum_tokens, share_out0, whole, vector_sum), input_grad)

    total = sum_in0.total()
    near = [moves.across(total, bits) for bits in (1, 2, 3)]
    share_out0.second()
    sum_tokens.across(2)
    vector_sum.copies()
    finished = kernels.finish_last(whole, 1, layers)
    near = settle((share_out0, sum_tokens, vector_sum), *near)
    parts = [(part[None], 0) for part in [total] + list(near)]
    grad_in, grad_out = kernels.finish_first(parts, share_out0.parts(), 0, layers, finished)
    output, input_grad = jnp.swapaxes(output, 0, 1), jnp.swapaxes(input_grad, 0, 1)
    near = sum_tokens.total()

    near = near.reshape(layers, 2, keys, wide)
    grad_t_in = jnp.swapaxes(near[:, 0, :, :patches], 1, 2)
    grad_b_in = near[:, 0, :, rows]
    grad_t_out = near[:, 1, :, :patches]
    sums = vector_sum.total().reshape(layers, 16, width)
    me = lax.axis_index("fsdp")

    def owned(row):
        size = width // shards_count
        return lax.dynamic_slice_in_dim(sums[:, row], me * size, size, 1)

    grad_gain1, grad_shift1, grad_gain2, grad_shift2, grad_b_cout = [owned(row) for row in range(5)]
    size = hidden // shards_count
    grad_b_cin = lax.dynamic_slice(sums, (0, 8 + me // 2, (me % 2) * size), (layers, 1, size))[:, 0]
    bias_total = sums[:, 5, :patches]
    return (
        output, input_grad, grad_gain1, grad_shift1, grad_t_in, grad_b_in, grad_t_out, bias_total,
        grad_gain2, grad_shift2, grad_in, grad_b_cin, grad_out, grad_b_cout,
    )


def fits(mesh):
    return mesh.shape["dp"] == 4 and mesh.shape["fsdp"] == 8


def solution(mesh):
    in_specs = (
        P(("dp", "fsdp"), None, None),
        P(("dp", "fsdp")),
        P(("dp", "fsdp"), None, None),
        P(None, "fsdp"),
        P(None, "fsdp"),
        P(None, None, "fsdp"),
        P(None, "fsdp"),
        P(None, "fsdp", None),
        P(),
        P(None, "fsdp"),
        P(None, "fsdp"),
        P(None, "fsdp", None),
        P(None, "fsdp"),
        P(None, "fsdp", None),
        P(None, "fsdp"),
        P(("dp", "fsdp"), None, None),
    )
    out_specs = (
        P(("dp", "fsdp"), None, None),
        P(("dp", "fsdp"), None, None),
        P(None, "fsdp"),
        P(None, "fsdp"),
        P(None, None, "fsdp"),
        P(None, "fsdp"),
        P(None, "fsdp", None),
        P(),
        P(None, "fsdp"),
        P(None, "fsdp"),
        P(None, "fsdp", None),
        P(None, "fsdp"),
        P(None, "fsdp", None),
        P(None, "fsdp"),
    )
    program = blocked_shards if fits(mesh) else shards
    return jax.shard_map(program, mesh=mesh, in_specs=in_specs, out_specs=out_specs, check_vma=False)
```

```python
import functools
import math

import jax
import jax.numpy as jnp
from jax import lax
from jax.experimental import pallas as pl
from jax.experimental.layout import Layout, with_layout_constraint
from jax.experimental.pallas import tpu as pltpu
from jax.sharding import PartitionSpec as P

EPSILON = 1e-06
GELU_A = math.sqrt(2.0 / math.pi)
GELU_B = 0.044715 * GELU_A
ROWS_FIRST = Layout(major_to_minor=(1, 0, 2))
IMAGES = 2
VMEM_BYTES = 60 * 2**20


def as_sent(shard):

    def short(part):
        return part.astype(jnp.bfloat16) if part.dtype == jnp.float32 else part

    return jax.tree.map(short, shard)


def layer_norm(values, gain, shift):
    center = values - jnp.mean(values, -1, keepdims=True)
    inv_std = lax.rsqrt(jnp.mean(center * center, -1, keepdims=True) + EPSILON)
    normed = center * inv_std
    return (normed * gain + shift, normed, inv_std)


def norm_back(grad_out, normed, inv_std, gain):
    grad_gain = jnp.sum(grad_out * normed, axis=(0, 1))
    grad_shift = jnp.sum(grad_out, axis=(0, 1))
    scaled = grad_out * gain
    grad_in = inv_std * (
        scaled
        - jnp.mean(scaled, -1, keepdims=True)
        - normed * jnp.mean(scaled * normed, -1, keepdims=True)
    )
    return (grad_in, grad_gain, grad_shift)


def gelu_back(pre_act, grad_out):
    return jax.vjp(jax.nn.gelu, pre_act)[1](grad_out)[0]


def fetch_forward(pieces):
    return (
        lax.all_gather(pieces[0], "fsdp", axis=0, tiled=True),
        lax.all_gather(pieces[1], "fsdp", axis=0, tiled=True),
        lax.all_gather(pieces[2], "fsdp", axis=1, tiled=True),
        lax.all_gather(pieces[3], "fsdp", axis=0, tiled=True),
        lax.all_gather(pieces[4], "fsdp", axis=0, tiled=True),
        lax.all_gather(pieces[5], "fsdp", axis=0, tiled=True),
        lax.all_gather(pieces[6], "fsdp", axis=0, tiled=True),
        lax.all_gather(pieces[7], "fsdp", axis=0, tiled=True),
        lax.all_gather(pieces[8], "fsdp", axis=0, tiled=True),
        lax.all_gather(pieces[9], "fsdp", axis=0, tiled=True),
        lax.all_gather(pieces[10], "fsdp", axis=0, tiled=True),
    )


def fetch_backward(pieces):
    return (
        lax.all_gather(pieces[0], "fsdp", axis=0, tiled=True),
        lax.all_gather(pieces[1], "fsdp", axis=0, tiled=True),
        lax.all_gather(pieces[2], "fsdp", axis=1, tiled=True),
        lax.all_gather(pieces[3], "fsdp", axis=0, tiled=True),
        lax.all_gather(pieces[4], "fsdp", axis=0, tiled=True),
        lax.all_gather(pieces[5], "fsdp", axis=0, tiled=True),
        lax.all_gather(pieces[6], "fsdp", axis=0, tiled=True),
        lax.all_gather(pieces[7], "fsdp", axis=0, tiled=True),
        lax.all_gather(pieces[8], "fsdp", axis=0, tiled=True),
        lax.all_gather(pieces[9], "fsdp", axis=0, tiled=True),
        lax.all_gather(pieces[10], "fsdp", axis=0, tiled=True),
    )


def shards(
    tokens,
    image_counts,
    skip_mask,
    norm1_gain,
    norm1_bias,
    token_in,
    token_in_bias,
    token_out,
    token_out_bias,
    norm2_gain,
    norm2_bias,
    channel_in,
    channel_in_bias,
    channel_out,
    channel_out_bias,
    cotangent,
):
    f32 = jnp.float32
    bf16 = jnp.bfloat16
    slots = tokens.shape[0]
    layers = norm1_gain.shape[0]
    live = (jnp.arange(slots, dtype=jnp.int32) < image_counts[0]).astype(f32)
    branch_scale = live[:, None, None] * skip_mask.astype(f32)

    def layer_pieces(index):
        return (
            norm1_gain[index],
            norm1_bias[index],
            token_in[index],
            token_in_bias[index],
            token_out[index],
            norm2_gain[index],
            norm2_bias[index],
            channel_in[index],
            channel_in_bias[index],
            channel_out[index],
            channel_out_bias[index],
        )

    values = tokens.astype(f32)
    saved = []
    kept_weights = []
    for index in range(layers):
        weights = fetch_forward(layer_pieces(index))
        kept_weights.append(weights)
        gain1, shift1, w_tin, b_tin, w_tout, gain2, shift2, w_cin, b_cin, w_cout, b_cout = weights
        tok_bias = token_out_bias[index].astype(f32)
        normed1, plain1, inv1 = layer_norm(values, gain1.astype(f32), shift1.astype(f32))
        normed1 = normed1.astype(bf16)
        pre_tok = jnp.einsum(
            "isd,sk->idk", normed1, w_tin, preferred_element_type=f32
        ) + b_tin.astype(f32)
        hidden1 = jax.nn.gelu(pre_tok).astype(bf16)
        branch = (
            jnp.einsum("idk,ks->isd", hidden1, w_tout, preferred_element_type=f32)
            + tok_bias[None, :, None]
        )
        middle = values + branch_scale[:, index, 0][:, None, None] * branch
        normed2, plain2, inv2 = layer_norm(middle, gain2.astype(f32), shift2.astype(f32))
        normed2 = normed2.astype(bf16)
        pre_chan = jnp.einsum(
            "isd,df->isf", normed2, w_cin, preferred_element_type=f32
        ) + b_cin.astype(f32)
        hidden2 = jax.nn.gelu(pre_chan).astype(bf16)
        branch = jnp.einsum(
            "isf,fd->isd", hidden2, w_cout, preferred_element_type=f32
        ) + b_cout.astype(f32)
        values = middle + branch_scale[:, index, 1][:, None, None] * branch
        saved.append(
            (normed1, plain1, inv1, pre_tok, hidden1, normed2, plain2, inv2, pre_chan, hidden2)
        )
    output = values.astype(bf16)
    grad = cotangent.astype(f32)
    local_grads = [None] * layers
    bias_grads = [None] * layers
    for index in reversed(range(layers)):
        weights = fetch_backward(layer_pieces(index))
        gain1, shift1, w_tin, b_tin, w_tout, gain2, shift2, w_cin, b_cin, w_cout, b_cout = weights
        normed1, plain1, inv1, pre_tok, hidden1, normed2, plain2, inv2, pre_chan, hidden2 = saved[
            index
        ]
        out_chan = branch_scale[:, index, 1][:, None, None] * grad
        grad_b_cout = jnp.sum(out_chan, axis=(0, 1))
        low_chan = out_chan.astype(bf16)
        grad_w_cout = jnp.einsum("isf,isd->fd", hidden2, low_chan, preferred_element_type=f32)
        back_hidden = jnp.einsum("isd,fd->isf", low_chan, w_cout, preferred_element_type=f32)
        pre_grad = gelu_back(pre_chan, back_hidden)
        grad_b_cin = jnp.sum(pre_grad, axis=(0, 1))
        low_pre = pre_grad.astype(bf16)
        grad_w_cin = jnp.einsum("isd,isf->df", normed2, low_pre, preferred_element_type=f32)
        back_norm = jnp.einsum("isf,df->isd", low_pre, w_cin, preferred_element_type=f32)
        norm_in, grad_gain2, grad_shift2 = norm_back(back_norm, plain2, inv2, gain2.astype(f32))
        grad_mid = grad + norm_in
        out_tok = branch_scale[:, index, 0][:, None, None] * grad_mid
        bias_grads[index] = jnp.sum(out_tok, axis=(0, 2))
        low_tok = out_tok.astype(bf16)
        grad_w_tout = jnp.einsum("idk,isd->ks", hidden1, low_tok, preferred_element_type=f32)
        back_hidden = jnp.einsum("isd,ks->idk", low_tok, w_tout, preferred_element_type=f32)
        pre_grad = gelu_back(pre_tok, back_hidden)
        grad_b_tin = jnp.sum(pre_grad, axis=(0, 1))
        low_pre = pre_grad.astype(bf16)
        grad_w_tin = jnp.einsum("isd,idk->sk", normed1, low_pre, preferred_element_type=f32)
        back_norm = jnp.einsum("idk,sk->isd", low_pre, w_tin, preferred_element_type=f32)
        norm_in, grad_gain1, grad_shift1 = norm_back(back_norm, plain1, inv1, gain1.astype(f32))
        grad = grad_mid + norm_in
        local = (
            grad_gain1,
            grad_shift1,
            grad_w_tin,
            grad_b_tin,
            grad_w_tout,
            grad_gain2,
            grad_shift2,
            grad_w_cin,
            grad_b_cin,
            grad_w_cout,
            grad_b_cout,
        )
        local_grads[index] = local
    token_bias_total = lax.psum(jnp.stack(bias_grads), ("dp", "fsdp"))
    joined = tuple(
        (
            jnp.stack([local_grads[index][position] for index in range(layers)])
            for position in range(11)
        )
    )
    owned = (
        lax.psum_scatter(joined[0], "fsdp", scatter_dimension=1, tiled=True),
        lax.psum_scatter(joined[1], "fsdp", scatter_dimension=1, tiled=True),
        lax.psum_scatter(joined[2], "fsdp", scatter_dimension=2, tiled=True),
        lax.psum_scatter(joined[3], "fsdp", scatter_dimension=1, tiled=True),
        lax.psum_scatter(joined[4], "fsdp", scatter_dimension=1, tiled=True),
        lax.psum_scatter(joined[5], "fsdp", scatter_dimension=1, tiled=True),
        lax.psum_scatter(joined[6], "fsdp", scatter_dimension=1, tiled=True),
        lax.psum_scatter(joined[7], "fsdp", scatter_dimension=1, tiled=True),
        lax.psum_scatter(joined[8], "fsdp", scatter_dimension=1, tiled=True),
        lax.psum_scatter(joined[9], "fsdp", scatter_dimension=1, tiled=True),
        lax.psum_scatter(joined[10], "fsdp", scatter_dimension=1, tiled=True),
    )
    results = jax.tree.map(lambda part: part.astype(jnp.float32), lax.psum(as_sent(owned), "dp"))
    return (
        output,
        grad,
        results[0],
        results[1],
        results[2],
        results[3],
        results[4],
        token_bias_total,
        results[5],
        results[6],
        results[7],
        results[8],
        results[9],
        results[10],
    )


def norm_parts(values):
    center = values - jnp.mean(values, -1, keepdims=True)
    inv_std = lax.rsqrt(jnp.mean(center * center, -1, keepdims=True) + EPSILON)
    return center * inv_std, inv_std


def norm_input_grad(grad, normed, inv_std):
    return inv_std * (
        grad
        - jnp.mean(grad, -1, keepdims=True)
        - normed * jnp.mean(grad * normed, -1, keepdims=True)
    )


def gelu_pair(value):
    square = value * value
    gate = 0.5 + 0.5 * jnp.tanh(value * (GELU_A + GELU_B * square))
    result = value * gate
    slope = gate + result * (1.0 - gate) * (2.0 * GELU_A + 6.0 * GELU_B * square)
    return result.astype(jnp.bfloat16), slope.astype(jnp.bfloat16)


def dot(left, right, left_dim, right_dim):
    return lax.dot_general(
        left, right, (((left_dim,), (right_dim,)), ((), ())), preferred_element_type=jnp.float32
    )


def chunks(size, count):
    return [slice(k * size // count, (k + 1) * size // count) for k in range(count)]


def position(copy):
    odd = copy & 1
    return 2 * odd + (odd ^ (copy >> 1))


def staggered(parts, product, finish):
    held = product(parts[0])
    for k, part in enumerate(parts):
        later = product(parts[k + 1]) if k + 1 < len(parts) else None
        finish(part, held)
        held = later


def clear(first, *refs):
    @pl.when(first)
    def _():
        for ref in refs:
            ref[...] = jnp.zeros_like(ref)


def unpack_small(place, own, other, *refs):
    vectors = refs[-1]
    z, c = place[0], place[1]
    lines, rows, _ = own.shape
    layers, extra, wide = vectors.shape[1:]
    keys = rows // layers
    for layer in range(layers):
        w_in, w_in_t, w_out, w_out_t, *rest = refs[10 * layer : 10 * layer + 10]
        base = layer * keys
        for source, side in ((own, c), (other, 1 - c)):
            for i in range(lines):
                shard = 2 * (i ^ z) + side
                start = pl.multiple_of(shard * keys, keys)
                w_in[pl.ds(start, keys)] = source[i, base : base + keys, :wide]
                w_out[pl.ds(start, keys)] = source[i, base : base + keys, wide : 2 * wide]
                vectors[shard, layer] = source[i, base : base + extra, 2 * wide :]
        w_in_t[...] = w_in[...].T
        w_out_t[...] = w_out[...].T
        held = [vectors[shard, layer].astype(jnp.float32) for shard in range(vectors.shape[0])]
        for row, target in enumerate(rest[:5]):
            size = target.shape[1] // len(held)
            target[...] = jnp.concatenate([part[row : row + 1, :size] for part in held], axis=1)
        biases = rest[5]
        size = biases.shape[1] // len(held)
        for shard, part in enumerate(held):
            whole = jnp.concatenate([part[5:6], part[6:7]], axis=1)
            biases[:, shard * size : (shard + 1) * size] = whole[:, :size]


def token_branch(values, scale, small, b_out, u_out, hidden_out, slope_out):
    gain1, shift1, w_in, w_out, gain2, shift2 = small
    rows, wide = values.shape[0], w_in.shape[1]
    normed, _ = norm_parts(values)
    u_out[:rows] = (normed * gain1[...] + shift1[...]).astype(jnp.bfloat16)
    below = lax.broadcasted_iota(jnp.int32, (wide - rows, values.shape[1]), 0)
    u_out[rows:] = jnp.where(below == 0, 1.0, 0.0).astype(jnp.bfloat16)
    hidden, slope = gelu_pair(dot(w_in[...], u_out[...], 1, 0))
    hidden_out[...] = hidden
    slope_out[...] = slope
    middle = values + scale * (dot(w_out[:rows], hidden, 1, 0) + b_out[0, :rows])
    normed, _ = norm_parts(middle)
    return middle, (normed * gain2[...] + shift2[...]).astype(jnp.bfloat16)


def token_forward(place, scale, x, b_out, *rest, layer):
    small, (u_out, hidden_out, slope_out, middle_out, v_out) = rest[:6], rest[6:]
    count, rows = x.shape[:2]
    for k in range(count):
        part = scale[count * pl.program_id(0) + k, 2 * layer]
        middle, v = token_branch(
            x[k].astype(jnp.float32), part, small, b_out, u_out.at[k], hidden_out.at[k], slope_out.at[k]
        )
        middle_out[k] = middle
        v_out[k * rows : (k + 1) * rows] = v


def token_grads(scale, grad, back_v, middle, x, u, hidden, slope, w_in, w_out, gain1, gain2, padded):
    rows, width = grad.shape
    normed, inv_std = norm_parts(middle)
    moved = back_v * normed
    sums = [jnp.sum(moved, 0, keepdims=True), jnp.sum(back_v, 0, keepdims=True)]
    grad_mid = grad + norm_input_grad(back_v * gain2[...], normed, inv_std)
    padded[:rows] = (scale * grad_mid).astype(jnp.bfloat16)
    low = padded[...]
    b_out = dot(jnp.ones((8, width), jnp.bfloat16), low, 1, 1)[:1]
    w_out_grad = dot(hidden, low, 1, 1)
    pre = (dot(w_out[...], low, 1, 0) * slope.astype(jnp.float32)).astype(jnp.bfloat16)
    w_in_grad = dot(pre, u, 1, 1)
    back = dot(w_in[:rows], pre, 1, 0)
    normed, inv_std = norm_parts(x)
    sums = [jnp.sum(back * normed, 0, keepdims=True), jnp.sum(back, 0, keepdims=True)] + sums
    return grad_mid + norm_input_grad(back * gain1[...], normed, inv_std), sums, b_out, w_in_grad, w_out_grad


def token_blocks(place, w_in_grad, w_out_grad, whole, put):
    z, c = place[0], place[1]
    keys = whole.shape[1] // 8
    for which, total in ((0, w_in_grad), (1, w_out_grad)):
        whole[which] = total[...].astype(jnp.bfloat16)
        for i in range(4):
            for side, core in ((0, c), (1, 1 - c)):
                start = pl.multiple_of((2 * (i ^ z) + core) * keys, keys)
                put(which, i, side, whole[which, pl.ds(start, keys)])


def token_backward(place, scale, grad, back_v, middle, x, u, hidden, slope, w_in, w_out, gain1, gain2, *rest):
    image = pl.program_id(0)
    g_cout, g_cin = rest[:2]
    last = len(rest) == 2 + 6 + 4
    if last:
        grad_out, mine_out, other_out, vector, low_out, above_grad = rest[2:8]
        layer = 1
    else:
        earlier, grad_out, mine_out, other_out, vector = rest[2:5], *rest[5:9]
        layer = 0
    padded, w_in_grad, w_out_grad, whole = rest[-4:]
    count, rows = x.shape[:2]
    first = image == 0
    clear(first, padded, vector, w_in_grad, w_out_grad)

    @pl.when(first)
    def _():
        vector[4:5] = g_cout[...]
        for j in range(g_cin.shape[0]):
            vector[8 + j : 9 + j] = g_cin[j]
        if not last:
            vector[16:] = earlier[2][...]

    if last:
        clear(first, above_grad)
    found = []
    for k in range(count):
        part = slice(k * rows, (k + 1) * rows)
        result, *sums = token_grads(
            scale[count * image + k, 2 * layer], grad[k].astype(jnp.float32), back_v[part], middle[k],
            x[k].astype(jnp.float32), u[k], hidden[k], slope[k], w_in, w_out, gain1, gain2, padded.at[k],
        )
        grad_out[k] = result
        if last:
            out = scale[count * image + k, 1] * result
            above_grad[...] += jnp.sum(out, 0, keepdims=True)
            low_out[part] = out.astype(jnp.bfloat16)
        found.append(sums)
    for k in range(4):
        vector[k : k + 1] += sum(sums[0][k] for sums in found)
    vector[5:6, : padded.shape[1]] += sum(sums[1] for sums in found)
    w_in_grad[...] += sum(sums[2] for sums in found)
    w_out_grad[...] += sum(sums[3] for sums in found)

    @pl.when(image == pl.num_programs(0) - 1)
    def _():
        targets = (mine_out, other_out)

        def put(which, i, side, part):
            targets[side][i, which] = part

        if not last:
            for side in range(2):
                targets[side][:, 2:] = earlier[side][...]
        token_blocks(place, w_in_grad, w_out_grad, whole, put)


def out_weight_grad(place, low, hidden, mine_out, other_out, turned, whole):
    @pl.when(pl.program_id(0) == 0)
    def _():
        turned[...] = low[...].T

    out_blocks(place, turned, hidden[0], mine_out, other_out, whole)


class Weight:
    def __init__(self, refs, which):
        self.which = which
        self.shards, self.parts = (refs[which], refs[2 + which]), (refs[4:9], refs[9:14])

    def blocks(self, copy, i):
        for side, (line, from_x, from_y, low, high) in enumerate(self.parts):
            if copy < 3:
                yield side, (line, from_x, from_y)[copy].at[i - 1, self.which], 0
            else:
                yield side, (low, high)[self.which].at[i - 1, 0], 0


def fetch_in(place, layer, weight, target, sem):
    z, c, q = place[0], place[1], place[2]
    copies, _, columns = target.shape
    rows = weight.shards[0].shape[1]
    for copy in range(copies):
        j = copy ^ q

        def put(ref, i, side, first):
            start = pl.multiple_of((2 * (i ^ z) + (c ^ side)) * rows + first, 16)
            goal = target.at[j, pl.ds(start, ref.shape[0])]
            pltpu.make_async_copy(ref, goal, sem.at[j]).start()

        for side, shard in enumerate(weight.shards):
            put(shard.at[layer, :, pl.ds(pl.multiple_of(j * columns, columns), columns)], 0, side, 0)
        for i in range(1, copies):
            for side, ref, first in weight.blocks(copy, i):
                put(ref, i, side, first)


def fetch_out(place, layer, weight, target, sem):
    z, c, q = place[0], place[1], place[2]
    lines, part, _ = target.shape
    for i in range(lines):

        def put(ref, start):
            goal = target.at[i ^ z, pl.ds(pl.multiple_of(start, 16), ref.shape[0])]
            pltpu.make_async_copy(ref, goal, sem.at[i ^ z]).start()

        if i == 0:
            for side, shard in enumerate(weight.shards):
                put(shard.at[layer], (c ^ side) * (part // 2))
            continue
        for copy in range(4):
            for side, ref, first in weight.blocks(copy, i):
                put(ref, (c ^ side) * (part // 2) + (copy ^ q) * (part // 8) + first)


def arrive(weight, sem, step):
    pltpu.make_async_copy(weight.at[step], weight.at[step], sem.at[step]).wait()


def out_blocks(place, turned, hidden, mine_out, other_out, whole):
    c, q = place[1], place[2]
    whole[...] = dot(turned[...], hidden, 1, 0).astype(jnp.bfloat16)
    copies, _, rows, columns = mine_out.shape
    size = columns // 2
    for side, target in ((c, mine_out), (1 - c, other_out)):
        units = pl.ds(pl.multiple_of(side * size, 128), size)
        for j in range(copies):
            start = 2 * j * rows
            target[position(j ^ q), 0, :, :size] = whole[start : start + rows, units]
            target[position(j ^ q), 0, :, size:] = whole[start + rows : start + 2 * rows, units]


def first_forward(place, scale, v, middle, bias_in, bias_out, *rest):
    weight_in, weight_out = Weight(rest[:14], 0), Weight(rest[:14], 1)
    hidden_out, slope_out, x_out, w_in, w_out, hidden, sem_in, sem_out = rest[14:]
    step = pl.program_id(0)

    @pl.when(step == 0)
    def _():
        fetch_in(place, 0, weight_in, w_in, sem_in)
        fetch_out(place, 0, weight_out, w_out, sem_out)

    @pl.when(step < 4)
    def _():
        j = (step & 3) ^ place[2]
        arrive(w_in, sem_in, j)
        def product(part):
            return dot(v[part], w_in[j], 1, 0) + bias_in[...]

        def finish(part, found):
            value, slope = gelu_pair(found)
            hidden_out[0, part] = value
            hidden[j, part] = value
            slope_out[0, part] = slope

        staggered(chunks(v.shape[0], 4), product, finish)

    @pl.when(step == 4)
    def _():
        for j in range(4):
            arrive(w_out, sem_out, j)
        for image, part in enumerate(chunks(v.shape[0], middle.shape[0])):
            branch = bias_out[...] + sum(dot(hidden[j, part], w_out[j], 1, 0) for j in range(4))
            x_out[image] = middle[image] + scale[image, 1] * branch


def last_hidden(place, scale, v, bias, grad, w_in, hidden_out, slope_out, blocks_out, low_out, bias_grad, hidden, turned):
    step = pl.program_id(0)

    @pl.when(step == 0)
    def _():
        rows = grad.shape[1]
        sums = 0.0
        for image in range(grad.shape[0]):
            out = scale[image, 3] * grad[image].astype(jnp.float32)
            sums = sums + jnp.sum(out, 0, keepdims=True)
            low_out[image * rows : (image + 1) * rows] = out.astype(jnp.bfloat16)
        bias_grad[...] = sums
        turned[...] = low_out[...].T

    @pl.when(step < 4)
    def _():
        def product(part):
            return dot(v[part], w_in[...], 1, 0) + bias[...]

        def finish(part, found):
            value, slope = gelu_pair(found)
            hidden_out[0, part] = value
            hidden[step & 3, part] = value
            slope_out[0, part] = slope

        staggered(chunks(v.shape[0], 4), product, finish)

    @pl.when(step >= 4)
    def _():
        found = dot(turned[...], hidden[step & 3], 1, 0).astype(jnp.bfloat16)
        size = blocks_out.shape[2]
        for k in range(blocks_out.shape[0]):
            blocks_out[k] = found[:, k * size : (k + 1) * size]


def last_out(place, scale, hidden, middle, bias, w_out, x_out, total):
    step = pl.program_id(0)

    @pl.when(step == 0)
    def _():
        total[...] = jnp.zeros_like(total)

    total[...] += dot(hidden[0], w_out[...], 1, 0)

    @pl.when(step == pl.num_programs(0) - 1)
    def _():
        for image in range(middle.shape[0]):
            rows = middle.shape[1]
            branch = total[image * rows : (image + 1) * rows] + bias[...]
            x_out[image] = (middle[image] + scale[image, 3] * branch).astype(x_out.dtype)


def last_backward(place, low, v, slope, w_out, w_in, in_out, back_out, bias_grad, turned, pre):
    @pl.when(pl.program_id(0) == 0)
    def _():
        turned[...] = v[...].T
        back_out[...] = jnp.zeros_like(back_out)

    sums = []

    def product(part):
        return dot(low[part], w_out[...], 1, 1)

    def finish(part, found):
        grad = found * slope[0, part].astype(jnp.float32)
        sums.append(jnp.sum(grad, 0, keepdims=True))
        pre[part] = grad.astype(jnp.bfloat16)

    staggered(chunks(low.shape[0], 2), product, finish)
    bias_grad[0] = sum(sums)
    for part in chunks(turned.shape[0], 3):
        in_out[part] = dot(turned[part], pre[...], 1, 0).astype(jnp.bfloat16)
    back_out[...] += dot(pre[...], w_in[...], 1, 1)


def channel_backward(place, low, v, slope, *rest, layer):
    mine, theirs, back_out, bias_grad, w_out, w_in, turned, pre, whole, sem_out, sem_in = rest[14:]
    z, c = place[0], place[1]
    step = pl.program_id(0)

    @pl.when(step == 0)
    def _():
        fetch_out(place, layer, Weight(rest[:14], 1), w_out, sem_out)
        fetch_in(place, layer, Weight(rest[:14], 0), w_in, sem_in)
        turned[...] = v[...].T
        back_out[...] = jnp.zeros_like(back_out)

    j = step ^ z
    arrive(w_out, sem_out, j)
    arrive(w_in, sem_in, j)
    sums = []

    def product(part):
        return dot(low[part], w_out[j], 1, 1)

    def finish(part, found):
        grad = found * slope[0, part].astype(jnp.float32)
        sums.append(jnp.sum(grad, 0, keepdims=True))
        pre[part] = grad.astype(jnp.bfloat16)

    staggered(chunks(low.shape[0], 2), product, finish)
    bias_grad[0] = sum(sums)
    for part in chunks(turned.shape[0], 3):
        whole[part] = dot(turned[part], pre[...], 1, 0).astype(jnp.bfloat16)
    lines = mine.shape[1]
    rows = whole.shape[0] // (2 * lines)
    for i in range(lines):
        for side, target in ((c, mine), (1 - c, theirs)):
            start = pl.multiple_of((2 * (i ^ z) + side) * rows, rows)
            target[0, i] = whole[pl.ds(start, rows)]
    back_out[...] += dot(pre[...], w_in[j], 1, 1)


def finish_last(place, grad_in, got_in, grad_out, got_out, in_out, out_out):
    in_out[0] = grad_in[...].astype(jnp.float32) + got_in[...].astype(jnp.float32)
    out_out[0] = (grad_out[0].astype(jnp.float32) + got_out[0].astype(jnp.float32)).T


def finish_first(place, *refs):
    parts_in, parts_out = refs[:4], refs[4:8]
    in_out, out_out, whole = refs[-3:]
    for j in range(4):
        columns = parts_in[j].shape[2]
        start = pl.multiple_of((j ^ place[2]) * columns, columns)
        in_out[0, :, pl.ds(start, columns)] = parts_in[j][0].astype(jnp.float32)
        rows, columns = parts_out[j].shape[1:]
        for half in range(2):
            start = pl.multiple_of((2 * (j ^ place[2]) + half) * rows, rows)
            part = parts_out[j][0, :, half * columns // 2 : (half + 1) * columns // 2]
            whole[pl.ds(start, rows)] = part.astype(jnp.float32)
    out_out[0] = whole[...].T


class Kernels:
    def __init__(self, place, slots, rows, width, inner, hidden, lines, block):
        self.place = place
        self.slots, self.rows, self.width = slots, rows, width
        self.inner, self.hidden = inner, hidden
        self.lines, self.block = lines, block
        self.part = hidden // 4
        self.wide = 256

    def run(self, body, steps, inputs, outputs, scratch, flops, aliases=None, **fixed):
        sizes = sum(a.size * a.dtype.itemsize for a, _, _ in inputs)
        sizes += sum(math.prod(o[0]) * jnp.dtype(o[1]).itemsize for o in outputs)

        def spec(block, index):
            if isinstance(block, tuple):
                return pl.BlockSpec(block, index)
            return pl.BlockSpec(memory_space=block)

        return pl.pallas_call(
            functools.partial(body, **fixed) if fixed else body,
            name=body.__name__,
            grid_spec=pltpu.PrefetchScalarGridSpec(
                num_scalar_prefetch=1,
                grid=(steps,),
                in_specs=[spec(block, index) for _, block, index in inputs],
                out_specs=[spec(o[2], o[3]) for o in outputs],
                scratch_shapes=scratch,
            ),
            out_shape=[jax.ShapeDtypeStruct(o[0], o[1]) for o in outputs],
            input_output_aliases=aliases or {},
            compiler_params=pltpu.CompilerParams(
                dimension_semantics=("arbitrary",), vmem_limit_bytes=VMEM_BYTES
            ),
            cost_estimate=pl.CostEstimate(flops=flops, bytes_accessed=sizes, transcendentals=0),
        )(self.place, *[a for a, _, _ in inputs])

    def image(self, array):
        return (array, (1,) + array.shape[1:], lambda i, s: (i, 0, 0))

    def fixed(self, array):
        zeros = (0,) * array.ndim
        return (array, array.shape, lambda i, s: zeros)

    def scalars(self, array):
        return (array, pltpu.SMEM, None)

    def in_hbm(self, arrays):
        return [(a, pltpu.HBM, None) for a in arrays]

    def fixed_out(self, shape, dtype):
        zeros = (0,) * len(shape)
        return (shape, dtype, shape, lambda i, s: zeros)

    def columns(self, array, count):
        return (array, (array.shape[0], array.shape[1] // count), lambda i, s: (0, i))

    def columns_out(self, rows, columns, count, dtype):
        return ((rows, columns), dtype, (rows, columns // count), lambda i, s: (0, i))

    def late(self, step, start):
        return jnp.clip(step - start, 0, 3)

    def images_out(self, rows, dtype):
        block = (IMAGES, rows, self.width)
        return ((self.slots, rows, self.width), dtype, block, lambda i, s: (i, 0, 0))

    def images(self, array):
        return (array, (IMAGES,) + array.shape[1:], lambda i, s: (i, 0, 0))

    def rows_out(self):
        shape = (self.slots * self.rows, self.width)
        return (shape, jnp.bfloat16, (IMAGES * self.rows, self.width), lambda i, s: (i, 0))

    def quarters(self, array, which, start=0):
        return (array, (1,) + array.shape[1:], lambda i, s: (self.late(i, start) ^ s[which], 0, 0))

    def quarters_out(self, which, start=0):
        rows = self.slots * self.rows
        block = (1, rows, self.part)
        return ((4,) + block[1:], jnp.bfloat16, block, lambda i, s: (self.late(i, start) ^ s[which], 0, 0))

    def row(self, array, which, start=0):
        return (array, (1, self.part), lambda i, s: (0, self.late(i, start) ^ s[which]))

    def out_blocks_out(self, start=0):
        block = (4, 1, self.block, self.width)
        shape = (4, self.lines) + block[2:]
        return (shape, jnp.bfloat16, block, lambda i, s: (0, self.late(i, start), 0, 0))

    def product(self):
        return 2 * self.slots * self.rows * self.width * self.hidden

    def unpack_small(self, own, other, layers, shards, extra):
        bf16, f32 = jnp.bfloat16, jnp.float32
        inner, wide, width = self.inner, self.wide, self.width
        outputs = [((inner, wide), bf16), ((wide, inner), bf16)] * 2
        outputs += [((1, width), f32)] * 5 + [((1, self.hidden), f32)]
        found = self.run(
            unpack_small,
            1,
            [self.fixed(own), self.fixed(other)],
            [self.fixed_out(*part) for part in outputs * layers],
            [pltpu.VMEM((shards, layers, extra, wide), bf16)],
            0,
        )
        return [list(found[10 * layer : 10 * layer + 10]) for layer in range(layers)]

    def token_product(self):
        return 2 * self.slots * self.wide * self.width * self.inner

    def b_out(self, array, layer):
        return (array, (1,) + array.shape[1:], lambda i, s: (layer, 0, 0))

    def token_outs(self):
        bf16 = jnp.bfloat16
        outs = [self.images_out(rows, bf16) for rows in (self.wide, self.inner, self.inner)]
        return outs + [self.images_out(self.rows, jnp.float32), self.rows_out()]

    def token_forward(self, scale, x, b_out, small, layer):
        return self.run(
            token_forward,
            self.slots // IMAGES,
            [self.scalars(scale), self.images(x), self.b_out(b_out, layer)] + [self.fixed(a) for a in small],
            self.token_outs(),
            [],
            2 * self.token_product(),
            layer=layer,
        )

    def first_forward(self, scale, v, middle, bias_in, bias_out, weights):
        bf16, f32 = jnp.bfloat16, jnp.float32
        rows = self.slots * self.rows
        return self.run(
            first_forward,
            5,
            [self.scalars(scale), self.fixed(v), self.fixed(middle), self.row(bias_in, 2), self.fixed(bias_out)]
            + self.in_hbm(weights),
            [self.quarters_out(2)] * 2 + [self.fixed_out((self.slots, self.rows, self.width), f32)],
            [
                self.weight(),
                self.weight(),
                pltpu.VMEM((4, rows, self.part), bf16),
                pltpu.SemaphoreType.DMA((4,)),
                pltpu.SemaphoreType.DMA((4,)),
            ],
            2 * self.product(),
        )

    def steps(self, array):
        return (array, (1,) + array.shape[1:], lambda i, s: (jnp.minimum(i, 3), 0, 0))

    def steps_out(self):
        block = (1, self.slots * self.rows, self.part)
        return ((4,) + block[1:], jnp.bfloat16, block, lambda i, s: (jnp.minimum(i, 3), 0, 0))

    def columns_in(self, array):
        return (array, (array.shape[0], self.part), lambda i, s: (0, jnp.minimum(i, 3)))

    def rows_in(self, array):
        return (array, (self.part, array.shape[1]), lambda i, s: (i, 0))

    def last_hidden(self, scale, v, bias, grad, w_in):
        bf16, f32 = jnp.bfloat16, jnp.float32
        rows = self.slots * self.rows
        block = (2, self.width, self.part // 2)
        return self.run(
            last_hidden,
            8,
            [self.scalars(scale), self.fixed(v), self.columns_in(bias), self.fixed(grad), self.columns_in(w_in)],
            [self.steps_out()] * 2
            + [((8,) + block[1:], bf16, block, lambda i, s: (jnp.maximum(i - 4, 0), 0, 0))]
            + [self.fixed_out((rows, self.width), bf16), self.fixed_out((1, self.width), f32)],
            [pltpu.VMEM((4, rows, self.part), bf16), pltpu.VMEM((self.width, rows), bf16)],
            2 * self.product(),
        )

    def last_out(self, scale, hidden, middle, bias, w_out):
        return self.run(
            last_out,
            4,
            [self.scalars(scale), self.steps(hidden), self.fixed(middle), self.fixed(bias), self.rows_in(w_out)],
            [self.fixed_out(middle.shape, jnp.bfloat16)],
            [pltpu.VMEM((self.slots * self.rows, self.width), jnp.float32)],
            self.product(),
        )[0]

    def last_backward(self, low, v, slope, w_out, w_in):
        bf16, f32 = jnp.bfloat16, jnp.float32
        rows = self.slots * self.rows
        return self.run(
            last_backward,
            4,
            [self.fixed(low), self.fixed(v), self.steps(slope), self.rows_in(w_out), self.columns_in(w_in)],
            [
                ((self.width, self.hidden), bf16, (self.width, self.part), lambda i, s: (0, i)),
                self.fixed_out((rows, self.width), f32),
                ((4, 1, self.part), f32, (1, 1, self.part), lambda i, s: (i, 0, 0)),
            ],
            [pltpu.VMEM((self.width, rows), bf16), pltpu.VMEM((rows, self.part), bf16)],
            3 * self.product(),
        )

    def token_backward(self, scale, grad, back, kept, small, g_cout, g_cin, keys, earlier=()):
        bf16, f32 = jnp.bfloat16, jnp.float32
        width = self.width
        middle, x, u, hidden, slope = kept
        inputs = [self.scalars(scale), self.images(grad)]
        inputs += [(back, (IMAGES * self.rows, width), lambda i, s: (i, 0))]
        inputs += [self.images(a) for a in (middle, x, u, hidden, slope)]
        inputs += [self.fixed(a) for a in tuple(small) + (g_cout, g_cin) + tuple(earlier)]
        outputs = [self.images_out(self.rows, f32)]
        outputs += [self.fixed_out((self.lines, 4 if earlier else 2, keys, self.wide), bf16)] * 2
        outputs += [self.fixed_out((32 if earlier else 16, width), f32)]
        if not earlier:
            outputs += [self.rows_out(), self.fixed_out((1, width), f32)]
        return self.run(
            token_backward,
            self.slots // IMAGES,
            inputs,
            outputs,
            [
                pltpu.VMEM((IMAGES, self.wide, width), bf16),
                pltpu.VMEM((self.inner, self.wide), f32),
                pltpu.VMEM((self.inner, self.wide), f32),
                pltpu.VMEM((2, self.inner, self.wide), bf16),
            ],
            4 * self.token_product(),
        )

    def out_weight_grad(self, low, hidden):
        rows = self.slots * self.rows
        return self.run(
            out_weight_grad,
            4,
            [self.fixed(low), self.quarters(hidden, 0)],
            [self.out_blocks_out()] * 2,
            [pltpu.VMEM((self.width, rows), jnp.bfloat16), pltpu.VMEM((self.width, self.part), jnp.bfloat16)],
            self.product(),
        )

    def weight(self):
        return pltpu.VMEM((4, self.width, self.part), jnp.bfloat16)

    def out_forward(self, scale, hidden, middle, bias, weights, layer, dtype):
        return self.run(
            out_forward,
            4,
            [self.scalars(scale), self.quarters(hidden, 0), self.fixed(middle), self.fixed(bias)]
            + self.in_hbm(weights),
            [self.fixed_out(middle.shape, dtype)],
            [
                self.weight(),
                pltpu.VMEM((self.slots * self.rows, self.width), jnp.float32),
                pltpu.SemaphoreType.DMA((4,)),
            ],
            self.product(),
            layer=layer,
        )[0]

    def channel_backward(self, low, v, slope, weights, layer):
        bf16, f32 = jnp.bfloat16, jnp.float32
        rows = self.slots * self.rows
        block = (1, self.lines, self.block, self.width)
        shape = (4, self.lines, self.block, self.width)
        blocks = (shape, bf16, block, lambda j, s: (position(j ^ s[0] ^ s[2]), 0, 0, 0))
        return self.run(
            channel_backward,
            4,
            [self.fixed(low), self.fixed(v), self.quarters(slope, 0)]
            + self.in_hbm(weights),
            [
                blocks,
                blocks,
                self.fixed_out((rows, self.width), f32),
                ((4, 1, self.part), f32, (1, 1, self.part), lambda i, s: (i ^ s[0], 0, 0)),
            ],
            [
                self.weight(),
                self.weight(),
                pltpu.VMEM((self.width, rows), bf16),
                pltpu.VMEM((rows, self.part), bf16),
                pltpu.VMEM((self.width, self.part), bf16),
                pltpu.SemaphoreType.DMA((4,)),
                pltpu.SemaphoreType.DMA((4,)),
            ],
            3 * self.product(),
            layer=layer,
        )

    def shard_outs(self, layer, layers):
        shapes = (layers, self.block, self.hidden), (layers, self.part // 2, self.width)
        return [(shape, jnp.float32, (1,) + shape[1:], lambda i, s: (layer, 0, 0)) for shape in shapes]

    def finish_last(self, whole, layer, layers):
        inputs = [self.fixed(a) for a in (whole.values[0], whole.got0, whole.values[1], whole.got1)]
        return self.run(finish_last, 1, inputs, self.shard_outs(layer, layers), [], 0)

    def finish_first(self, parts_in, parts_out, layer, layers, earlier):
        def one(part):
            array, index = part
            return (array, (1,) + array.shape[1:], lambda i, s: (index, 0, 0))

        inputs = [one(part) for part in parts_in + parts_out]
        return self.run(
            finish_first,
            1,
            inputs + self.in_hbm(earlier),
            self.shard_outs(layer, layers),
            [pltpu.VMEM((self.width, self.part // 2), jnp.float32)],
            0,
            {1 + len(inputs): 0, 2 + len(inputs): 1},
        )


class Moves:
    def __init__(self):
        self.lines = lax.axis_size("fsdp") // 2
        self.copies = lax.axis_size("dp")
        me = lax.axis_index("fsdp")
        self.z, self.c, self.q = me // 2, me % 2, lax.axis_index("dp")

    def along(self, values, bits):
        return lax.ppermute(values, "fsdp", [(f, f ^ (2 * bits)) for f in range(2 * self.lines)])

    def core(self, values):
        return lax.ppermute(values, "fsdp", [(f, f ^ 1) for f in range(2 * self.lines)])

    def across(self, values, bits):
        return lax.ppermute(values, "dp", [(q, q ^ bits) for q in range(self.copies)])


class Held:
    def __init__(self, moves):
        self.moves, self.fresh = moves, []
        self.half = moves.lines // 2

    def bring(self, **arrays):
        for name, array in arrays.items():
            setattr(self, name, array)
            self.fresh.append(name)


def settle(held, *values):
    names = [(part, name) for part in held for name in part.fresh]
    arrays = tuple(getattr(part, name) for part, name in names)
    arrays = lax.optimization_barrier(tuple(values) + arrays)
    for (part, name), array in zip(names, arrays[len(values) :]):
        setattr(part, name, array)
    for part in held:
        part.fresh = []
    return arrays[: len(values)]


class Gather(Held):
    def __init__(self, moves, part):
        super().__init__(moves)
        self.part = part

    def direct(self):
        self.bring(**{"z%d" % i: self.moves.along(self.part, i) for i in range(1, self.moves.lines)})

    def join(self):
        self.line = jnp.stack([getattr(self, "z%d" % i) for i in range(1, self.moves.lines)])

    def first(self):
        self.bring(x=self.moves.across(self.line, 1), y=self.moves.across(self.line, 2))

    def second(self):
        self.bring(low=self.moves.across(self.y[:, :1], 1), high=self.moves.across(self.x[:, 1:], 2))

    def core(self, *names):
        self.bring(**{name + "_core": self.moves.core(getattr(self, name)) for name in names})

    def whole(self):
        names = ("line", "x", "y", "low", "high")
        return [getattr(self, name) for name in names] + [getattr(self, name + "_core") for name in names]


class Sum(Held):
    def __init__(self, moves, mine, other):
        super().__init__(moves)
        self.mine, self.theirs = mine, other
        self.low, self.high = slice(0, self.half), slice(self.half, None)

    def both(self, copies, part):
        return self.mine[copies, part] + self.got[copies, part]

    def core(self):
        self.bring(got=self.moves.core(self.theirs))

    def first(self):
        self.bring(
            from_x=self.moves.across(self.both(slice(2, 4), self.low), 1),
            from_y=self.moves.across(self.both(slice(1, 3), self.high), 2),
        )

    def second(self):
        self.bring(
            low2=self.moves.across(self.both(1, self.low) + self.from_x[0], 2),
            high1=self.moves.across(self.both(3, self.high) + self.from_y[1], 1),
        )

    def halves(self):
        low = self.both(0, self.low) + self.from_x[1] + self.low2
        high = self.both(0, self.high) + self.from_y[0] + self.high1
        return low, high

    def once(self):
        low, high = self.halves()
        self.block = low[0]
        blocks = [low[i] for i in range(1, self.half)] + [high[i] for i in range(self.half)]
        self.bring(**{"z%d" % (i + 1): self.moves.along(block, i + 1) for i, block in enumerate(blocks)})

    def far(self):
        self.block, high = self.halves()
        self.bring(z=self.moves.along(high, 2))

    def near(self):
        pair = self.block + self.z
        self.block = pair[0]
        self.bring(z1=self.moves.along(pair[1], 1))

    def total(self):
        total = self.block.astype(jnp.float32)
        for i in range(1, self.moves.lines):
            if hasattr(self, "z%d" % i):
                total = total + getattr(self, "z%d" % i).astype(jnp.float32)
        return total.astype(jnp.bfloat16)


class Share(Held):
    def __init__(self, moves, part, axis):
        super().__init__(moves)
        self.part, self.axis = part, axis

    def first(self):
        self.bring(near=self.moves.across(self.part, self.axis))

    def second(self):
        self.bring(far=self.moves.across(jnp.stack([self.part, self.near]), 3 - self.axis))

    def parts(self):
        near, far = (self.near[None], 0), (self.far, 0)
        return [(self.part[None], 0)] + ([near, far] if self.axis == 1 else [far, near]) + [(self.far, 1)]


class SumSmall(Held):
    def __init__(self, moves, mine, other):
        super().__init__(moves)
        self.mine, self.theirs = mine, other

    def core(self):
        self.bring(got=self.moves.core(self.theirs))

    def along(self):
        both = self.mine + self.got
        self.value = both[0]
        self.bring(**{"z%d" % i: self.moves.along(both[i], i) for i in range(1, self.moves.lines)})

    def across(self, bits):
        if bits == 1:
            parts = [self.value] + [getattr(self, "z%d" % i) for i in range(1, self.moves.lines)]
            self.value = sum(part.astype(jnp.float32) for part in parts).astype(jnp.bfloat16)
        else:
            self.value = self.value + self.got
        self.bring(got=self.moves.across(self.value, bits))

    def total(self):
        return self.value.astype(jnp.float32) + self.got.astype(jnp.float32)


class Copies(Held):
    def __init__(self, moves, *values):
        super().__init__(moves)
        self.values = list(values)

    def step(self, *axes):
        got = [self.moves.across(value, bits) for value, bits in zip(self.values, axes)]
        self.bring(got0=got[0], got1=got[1])

    def add(self):
        self.values = [self.values[0] + self.got0, self.values[1] + self.got1]


class SumAll(Held):
    def __init__(self, moves, value):
        super().__init__(moves)
        self.value, self.bit = value, 1

    def step(self):
        count = 2 * self.moves.lines
        got = lax.ppermute(self.value, "fsdp", [(i, i ^ self.bit) for i in range(count)])
        self.bit *= 2
        self.bring(value=self.value + got)

    def copies(self):
        self.bring(**{"q%d" % bits: self.moves.across(self.value, bits) for bits in (1, 2, 3)})

    def total(self):
        return (self.value + self.q1) + (self.q2 + self.q3)


def blocked_shards(
    tokens, image_counts, skip_mask, norm1_gain, norm1_bias, token_in, token_in_bias, token_out,
    token_out_bias, norm2_gain, norm2_bias, channel_in, channel_in_bias, channel_out,
    channel_out_bias, cotangent,
):
    f32, bf16 = jnp.float32, jnp.bfloat16
    slots, patches, width = tokens.shape
    layers, in_rows, hidden = channel_in.shape
    keys = token_out.shape[1]
    moves = Moves()
    shards_count = 2 * moves.lines
    inner = keys * shards_count
    rows = -(-patches // 16) * 16
    place = jnp.stack([moves.z, moves.c, moves.q]).astype(jnp.int32)
    kernels = Kernels(place, slots, rows, width, inner, hidden, moves.lines, in_rows)
    wide = kernels.wide

    live = (jnp.arange(slots, dtype=jnp.int32) < image_counts[0]).astype(f32)
    scale = live[:, None, None] * skip_mask.astype(f32)

    def padded(images):
        return jnp.pad(images, ((0, 0), (0, rows - patches), (0, 0)))

    def quarter(array, axis):
        size = array.shape[axis] // 4
        return lax.dynamic_slice_in_dim(array, moves.q * size, size, axis)

    def widen(array):
        return jnp.pad(array, ((0, 0), (0, 0), (0, wide - array.shape[2])))

    gap = jnp.zeros((layers, keys, rows - patches), bf16)
    with_bias = jnp.concatenate([jnp.swapaxes(token_in, 1, 2), gap, token_in_bias[:, :, None]], 2)
    vectors = jnp.stack([norm1_gain, norm1_bias, norm2_gain, norm2_bias, channel_out_bias], 1)
    biases = jnp.pad(channel_in_bias, ((0, 0), (0, 2 * wide - channel_in_bias.shape[1])))
    vectors = jnp.concatenate([widen(vectors), biases.reshape(layers, 2, wide)], 1)
    extra = 16
    vectors = jnp.pad(vectors, ((0, 0), (0, extra - vectors.shape[1]), (0, 0)))
    vectors = jnp.pad(vectors, ((0, 0), (0, keys - extra), (0, 0)))
    packs = jnp.concatenate([widen(with_bias), widen(token_out), vectors], 2).reshape(layers * keys, width)
    b_outs = jnp.pad(token_out_bias.astype(f32), ((0, 0), (0, wide - patches)))[:, :, None]
    scale = scale.reshape(slots, 2 * layers)

    first = Gather(moves, jnp.stack([quarter(channel_in[0], 1), quarter(channel_out[0], 0)]))
    small = Gather(moves, packs)
    shards_held = Held(moves)
    small.direct()
    first.direct()
    shards_held.bring(ins=moves.core(channel_in[0]), outs=moves.core(channel_out[0]))
    shard_in, shard_out = settle((first, small, shards_held), channel_in[1], channel_out[1])
    first.join()
    small.line = jnp.stack([small.part, small.z1, small.z2, small.z3])

    w_cin1 = lax.all_gather(shard_in, "fsdp", axis=0, tiled=True)
    w_cout1 = lax.all_gather(shard_out, "fsdp", axis=0, tiled=True)

    small.core("line")
    first.first()
    began, first.fresh = first.fresh, []
    first.core("line")
    (first.line,) = settle((first, small), first.line)
    first.fresh = began
    found = kernels.unpack_small(small.line, small.line_core, layers, shards_count, extra)
    x0 = padded(tokens)
    (w_in0, w_in_t0, w_out0, w_out_t0, gain1_0, shift1_0, gain2_0, shift2_0, b_cout0, b_cin0) = found[0]
    (w_in1, w_in_t1, w_out1, w_out_t1, gain1_1, shift1_1, gain2_1, shift2_1, b_cout1, b_cin1) = found[1]
    u0, h0, d0, mid0, v0 = kernels.token_forward(
        scale, x0, b_outs, (gain1_0, shift1_0, w_in0, w_out_t0, gain2_0, shift2_0), 0
    )
    (v0,) = settle((first,), v0)

    first.second()
    first.core("x", "y")
    (v0,) = settle((first,), v0)
    first.core("low", "high")
    (v0,) = settle((first,), v0)
    weights = [channel_in, channel_out, shards_held.ins[None], shards_held.outs[None]] + first.whole()
    hid0, slope0, x1 = kernels.first_forward(scale, v0, mid0, b_cin0, b_cout0, weights)
    u1, h1, d1, mid1, v1 = kernels.token_forward(
        scale, x1, b_outs, (gain1_1, shift1_1, w_in1, w_out_t1, gain2_1, shift2_1), 1
    )
    grad2 = padded(cotangent)
    hid1, slope1, blocks1, low1, g_cout1 = kernels.last_hidden(scale, v1, b_cin1, grad2, w_cin1)

    grad_cout1 = lax.psum_scatter(blocks1, "fsdp", scatter_dimension=0, tiled=True)
    grad_cin1, back, g_cin1 = kernels.last_backward(low1, v1, slope1, w_cout1, w_cin1)
    grad_cin1 = lax.psum_scatter(grad_cin1, "fsdp", scatter_dimension=0, tiled=True)
    grad1, *tokens1, vector1, low0, g_cout0 = kernels.token_backward(
        scale, grad2, back, (mid1, x1, u1, h1, d1), (w_in_t1, w_out1, gain1_1, gain2_1), g_cout1, g_cin1, keys
    )
    mine, theirs = kernels.out_weight_grad(low0, hid0)
    mine, theirs, grad1 = settle((), mine, theirs, grad1)

    sum_out0 = Sum(moves, mine, theirs)
    sum_out0.core()
    mine, theirs, back, g_cin0 = kernels.channel_backward(low0, v0, slope0, weights, 0)
    mine, theirs, back, grad_cout1 = settle((sum_out0,), mine, theirs, back, grad_cout1)

    sum_in0 = Sum(moves, mine, theirs)
    sum_in0.core()
    sum_out0.first()
    grad0, *tokens, vector = kernels.token_backward(
        scale, grad1, back, (mid0, x0, u0, h0, d0), (w_in_t0, w_out0, gain1_0, gain2_0), g_cout0, g_cin0, keys,
        (*tokens1, vector1),
    )
    hid1, grad0, *tokens, vector = settle((sum_in0, sum_out0), hid1, grad0, *tokens, vector)

    sum_tokens = SumSmall(moves, *tokens)
    sum_tokens.core()
    sum_in0.first()
    sum_out0.second()
    vector_sum = SumAll(moves, vector)
    vector_sum.step()
    output = kernels.last_out(scale, hid1, mid1, b_cout1, w_cout1)
    output, grad_cin1, grad_cout1 = settle(
        (sum_in0, sum_out0, sum_tokens, vector_sum), output, grad_cin1, grad_cout1
    )

    sum_in0.second()
    sum_out0.once()
    sum_tokens.along()
    vector_sum.step()
    whole = Copies(moves, grad_cin1, grad_cout1)
    whole.step(1, 2)
    output = with_layout_constraint(output[:, :patches], ROWS_FIRST)
    (output,) = settle((sum_in0, sum_out0, sum_tokens, whole, vector_sum), output)

    sum_in0.once()
    sum_tokens.across(1)
    vector_sum.step()
    share_out0 = Share(moves, sum_out0.total(), 2)
    share_out0.first()
    whole.add()
    whole.step(2, 1)
    input_grad = with_layout_constraint(grad0[:, :patches], ROWS_FIRST)
    (input_grad,) = settle((sum_in0, sum_tokens, share_out0, whole, vector_sum), input_grad)

    total = sum_in0.total()
    near = [moves.across(total, bits) for bits in (1, 2, 3)]
    share_out0.second()
    sum_tokens.across(2)
    vector_sum.copies()
    finished = kernels.finish_last(whole, 1, layers)
    near = settle((share_out0, sum_tokens, vector_sum), *near)
    parts = [(part[None], 0) for part in [total] + list(near)]
    grad_in, grad_out = kernels.finish_first(parts, share_out0.parts(), 0, layers, finished)
    near = sum_tokens.total()

    near = near.reshape(layers, 2, keys, wide)
    grad_t_in = jnp.swapaxes(near[:, 0, :, :patches], 1, 2)
    grad_b_in = near[:, 0, :, rows]
    grad_t_out = near[:, 1, :, :patches]
    sums = vector_sum.total().reshape(layers, 16, width)
    me = lax.axis_index("fsdp")

    def owned(row):
        size = width // shards_count
        return lax.dynamic_slice_in_dim(sums[:, row], me * size, size, 1)

    grad_gain1, grad_shift1, grad_gain2, grad_shift2, grad_b_cout = [owned(row) for row in range(5)]
    size = hidden // shards_count
    grad_b_cin = lax.dynamic_slice(sums, (0, 8 + me // 2, (me % 2) * size), (layers, 1, size))[:, 0]
    bias_total = sums[:, 5, :patches]
    return (
        output, input_grad, grad_gain1, grad_shift1, grad_t_in, grad_b_in, grad_t_out, bias_total,
        grad_gain2, grad_shift2, grad_in, grad_b_cin, grad_out, grad_b_cout,
    )


def fits(mesh):
    return mesh.shape["dp"] == 4 and mesh.shape["fsdp"] == 8


def solution(mesh):
    in_specs = (
        P(("dp", "fsdp"), None, None),
        P(("dp", "fsdp")),
        P(("dp", "fsdp"), None, None),
        P(None, "fsdp"),
        P(None, "fsdp"),
        P(None, None, "fsdp"),
        P(None, "fsdp"),
        P(None, "fsdp", None),
        P(),
        P(None, "fsdp"),
        P(None, "fsdp"),
        P(None, "fsdp", None),
        P(None, "fsdp"),
        P(None, "fsdp", None),
        P(None, "fsdp"),
        P(("dp", "fsdp"), None, None),
    )
    out_specs = (
        P(("dp", "fsdp"), None, None),
        P(("dp", "fsdp"), None, None),
        P(None, "fsdp"),
        P(None, "fsdp"),
        P(None, None, "fsdp"),
        P(None, "fsdp"),
        P(None, "fsdp", None),
        P(),
        P(None, "fsdp"),
        P(None, "fsdp"),
        P(None, "fsdp", None),
        P(None, "fsdp"),
        P(None, "fsdp", None),
        P(None, "fsdp"),
    )
    program = blocked_shards if fits(mesh) else shards
    return jax.shard_map(program, mesh=mesh, in_specs=in_specs, out_specs=out_specs, check_vma=False)
```

```python
import functools
import math

import jax
import jax.numpy as jnp
from jax import lax
from jax.experimental import pallas as pl
from jax.experimental.layout import Layout, with_layout_constraint
from jax.experimental.pallas import tpu as pltpu
from jax.sharding import PartitionSpec as P

EPSILON = 1e-06
GELU_A = math.sqrt(2.0 / math.pi)
GELU_B = 0.044715 * GELU_A
ROWS_FIRST = Layout(major_to_minor=(1, 0, 2))
IMAGES = 2
VMEM_BYTES = 60 * 2**20


def as_sent(shard):

    def short(part):
        return part.astype(jnp.bfloat16) if part.dtype == jnp.float32 else part

    return jax.tree.map(short, shard)


def layer_norm(values, gain, shift):
    center = values - jnp.mean(values, -1, keepdims=True)
    inv_std = lax.rsqrt(jnp.mean(center * center, -1, keepdims=True) + EPSILON)
    normed = center * inv_std
    return (normed * gain + shift, normed, inv_std)


def norm_back(grad_out, normed, inv_std, gain):
    grad_gain = jnp.sum(grad_out * normed, axis=(0, 1))
    grad_shift = jnp.sum(grad_out, axis=(0, 1))
    scaled = grad_out * gain
    grad_in = inv_std * (
        scaled
        - jnp.mean(scaled, -1, keepdims=True)
        - normed * jnp.mean(scaled * normed, -1, keepdims=True)
    )
    return (grad_in, grad_gain, grad_shift)


def gelu_back(pre_act, grad_out):
    return jax.vjp(jax.nn.gelu, pre_act)[1](grad_out)[0]


def fetch_forward(pieces):
    return (
        lax.all_gather(pieces[0], "fsdp", axis=0, tiled=True),
        lax.all_gather(pieces[1], "fsdp", axis=0, tiled=True),
        lax.all_gather(pieces[2], "fsdp", axis=1, tiled=True),
        lax.all_gather(pieces[3], "fsdp", axis=0, tiled=True),
        lax.all_gather(pieces[4], "fsdp", axis=0, tiled=True),
        lax.all_gather(pieces[5], "fsdp", axis=0, tiled=True),
        lax.all_gather(pieces[6], "fsdp", axis=0, tiled=True),
        lax.all_gather(pieces[7], "fsdp", axis=0, tiled=True),
        lax.all_gather(pieces[8], "fsdp", axis=0, tiled=True),
        lax.all_gather(pieces[9], "fsdp", axis=0, tiled=True),
        lax.all_gather(pieces[10], "fsdp", axis=0, tiled=True),
    )


def fetch_backward(pieces):
    return (
        lax.all_gather(pieces[0], "fsdp", axis=0, tiled=True),
        lax.all_gather(pieces[1], "fsdp", axis=0, tiled=True),
        lax.all_gather(pieces[2], "fsdp", axis=1, tiled=True),
        lax.all_gather(pieces[3], "fsdp", axis=0, tiled=True),
        lax.all_gather(pieces[4], "fsdp", axis=0, tiled=True),
        lax.all_gather(pieces[5], "fsdp", axis=0, tiled=True),
        lax.all_gather(pieces[6], "fsdp", axis=0, tiled=True),
        lax.all_gather(pieces[7], "fsdp", axis=0, tiled=True),
        lax.all_gather(pieces[8], "fsdp", axis=0, tiled=True),
        lax.all_gather(pieces[9], "fsdp", axis=0, tiled=True),
        lax.all_gather(pieces[10], "fsdp", axis=0, tiled=True),
    )


def shards(
    tokens,
    image_counts,
    skip_mask,
    norm1_gain,
    norm1_bias,
    token_in,
    token_in_bias,
    token_out,
    token_out_bias,
    norm2_gain,
    norm2_bias,
    channel_in,
    channel_in_bias,
    channel_out,
    channel_out_bias,
    cotangent,
):
    f32 = jnp.float32
    bf16 = jnp.bfloat16
    slots = tokens.shape[0]
    layers = norm1_gain.shape[0]
    live = (jnp.arange(slots, dtype=jnp.int32) < image_counts[0]).astype(f32)
    branch_scale = live[:, None, None] * skip_mask.astype(f32)

    def layer_pieces(index):
        return (
            norm1_gain[index],
            norm1_bias[index],
            token_in[index],
            token_in_bias[index],
            token_out[index],
            norm2_gain[index],
            norm2_bias[index],
            channel_in[index],
            channel_in_bias[index],
            channel_out[index],
            channel_out_bias[index],
        )

    values = tokens.astype(f32)
    saved = []
    kept_weights = []
    for index in range(layers):
        weights = fetch_forward(layer_pieces(index))
        kept_weights.append(weights)
        gain1, shift1, w_tin, b_tin, w_tout, gain2, shift2, w_cin, b_cin, w_cout, b_cout = weights
        tok_bias = token_out_bias[index].astype(f32)
        normed1, plain1, inv1 = layer_norm(values, gain1.astype(f32), shift1.astype(f32))
        normed1 = normed1.astype(bf16)
        pre_tok = jnp.einsum(
            "isd,sk->idk", normed1, w_tin, preferred_element_type=f32
        ) + b_tin.astype(f32)
        hidden1 = jax.nn.gelu(pre_tok).astype(bf16)
        branch = (
            jnp.einsum("idk,ks->isd", hidden1, w_tout, preferred_element_type=f32)
            + tok_bias[None, :, None]
        )
        middle = values + branch_scale[:, index, 0][:, None, None] * branch
        normed2, plain2, inv2 = layer_norm(middle, gain2.astype(f32), shift2.astype(f32))
        normed2 = normed2.astype(bf16)
        pre_chan = jnp.einsum(
            "isd,df->isf", normed2, w_cin, preferred_element_type=f32
        ) + b_cin.astype(f32)
        hidden2 = jax.nn.gelu(pre_chan).astype(bf16)
        branch = jnp.einsum(
            "isf,fd->isd", hidden2, w_cout, preferred_element_type=f32
        ) + b_cout.astype(f32)
        values = middle + branch_scale[:, index, 1][:, None, None] * branch
        saved.append(
            (normed1, plain1, inv1, pre_tok, hidden1, normed2, plain2, inv2, pre_chan, hidden2)
        )
    output = values.astype(bf16)
    grad = cotangent.astype(f32)
    local_grads = [None] * layers
    bias_grads = [None] * layers
    for index in reversed(range(layers)):
        weights = fetch_backward(layer_pieces(index))
        gain1, shift1, w_tin, b_tin, w_tout, gain2, shift2, w_cin, b_cin, w_cout, b_cout = weights
        normed1, plain1, inv1, pre_tok, hidden1, normed2, plain2, inv2, pre_chan, hidden2 = saved[
            index
        ]
        out_chan = branch_scale[:, index, 1][:, None, None] * grad
        grad_b_cout = jnp.sum(out_chan, axis=(0, 1))
        low_chan = out_chan.astype(bf16)
        grad_w_cout = jnp.einsum("isf,isd->fd", hidden2, low_chan, preferred_element_type=f32)
        back_hidden = jnp.einsum("isd,fd->isf", low_chan, w_cout, preferred_element_type=f32)
        pre_grad = gelu_back(pre_chan, back_hidden)
        grad_b_cin = jnp.sum(pre_grad, axis=(0, 1))
        low_pre = pre_grad.astype(bf16)
        grad_w_cin = jnp.einsum("isd,isf->df", normed2, low_pre, preferred_element_type=f32)
        back_norm = jnp.einsum("isf,df->isd", low_pre, w_cin, preferred_element_type=f32)
        norm_in, grad_gain2, grad_shift2 = norm_back(back_norm, plain2, inv2, gain2.astype(f32))
        grad_mid = grad + norm_in
        out_tok = branch_scale[:, index, 0][:, None, None] * grad_mid
        bias_grads[index] = jnp.sum(out_tok, axis=(0, 2))
        low_tok = out_tok.astype(bf16)
        grad_w_tout = jnp.einsum("idk,isd->ks", hidden1, low_tok, preferred_element_type=f32)
        back_hidden = jnp.einsum("isd,ks->idk", low_tok, w_tout, preferred_element_type=f32)
        pre_grad = gelu_back(pre_tok, back_hidden)
        grad_b_tin = jnp.sum(pre_grad, axis=(0, 1))
        low_pre = pre_grad.astype(bf16)
        grad_w_tin = jnp.einsum("isd,idk->sk", normed1, low_pre, preferred_element_type=f32)
        back_norm = jnp.einsum("idk,sk->isd", low_pre, w_tin, preferred_element_type=f32)
        norm_in, grad_gain1, grad_shift1 = norm_back(back_norm, plain1, inv1, gain1.astype(f32))
        grad = grad_mid + norm_in
        local = (
            grad_gain1,
            grad_shift1,
            grad_w_tin,
            grad_b_tin,
            grad_w_tout,
            grad_gain2,
            grad_shift2,
            grad_w_cin,
            grad_b_cin,
            grad_w_cout,
            grad_b_cout,
        )
        local_grads[index] = local
    token_bias_total = lax.psum(jnp.stack(bias_grads), ("dp", "fsdp"))
    joined = tuple(
        (
            jnp.stack([local_grads[index][position] for index in range(layers)])
            for position in range(11)
        )
    )
    owned = (
        lax.psum_scatter(joined[0], "fsdp", scatter_dimension=1, tiled=True),
        lax.psum_scatter(joined[1], "fsdp", scatter_dimension=1, tiled=True),
        lax.psum_scatter(joined[2], "fsdp", scatter_dimension=2, tiled=True),
        lax.psum_scatter(joined[3], "fsdp", scatter_dimension=1, tiled=True),
        lax.psum_scatter(joined[4], "fsdp", scatter_dimension=1, tiled=True),
        lax.psum_scatter(joined[5], "fsdp", scatter_dimension=1, tiled=True),
        lax.psum_scatter(joined[6], "fsdp", scatter_dimension=1, tiled=True),
        lax.psum_scatter(joined[7], "fsdp", scatter_dimension=1, tiled=True),
        lax.psum_scatter(joined[8], "fsdp", scatter_dimension=1, tiled=True),
        lax.psum_scatter(joined[9], "fsdp", scatter_dimension=1, tiled=True),
        lax.psum_scatter(joined[10], "fsdp", scatter_dimension=1, tiled=True),
    )
    results = jax.tree.map(lambda part: part.astype(jnp.float32), lax.psum(as_sent(owned), "dp"))
    return (
        output,
        grad,
        results[0],
        results[1],
        results[2],
        results[3],
        results[4],
        token_bias_total,
        results[5],
        results[6],
        results[7],
        results[8],
        results[9],
        results[10],
    )


def norm_parts(values):
    center = values - jnp.mean(values, -1, keepdims=True)
    inv_std = lax.rsqrt(jnp.mean(center * center, -1, keepdims=True) + EPSILON)
    return center * inv_std, inv_std


def norm_input_grad(grad, normed, inv_std):
    return inv_std * (
        grad
        - jnp.mean(grad, -1, keepdims=True)
        - normed * jnp.mean(grad * normed, -1, keepdims=True)
    )


def gelu_pair(value):
    square = value * value
    gate = 0.5 + 0.5 * jnp.tanh(value * (GELU_A + GELU_B * square))
    result = value * gate
    slope = gate + result * (1.0 - gate) * (2.0 * GELU_A + 6.0 * GELU_B * square)
    return result.astype(jnp.bfloat16), slope.astype(jnp.bfloat16)


def dot(left, right, left_dim, right_dim):
    return lax.dot_general(
        left, right, (((left_dim,), (right_dim,)), ((), ())), preferred_element_type=jnp.float32
    )


def chunks(size, count):
    return [slice(k * size // count, (k + 1) * size // count) for k in range(count)]


def position(copy):
    odd = copy & 1
    return 2 * odd + (odd ^ (copy >> 1))


def staggered(parts, product, finish):
    held = product(parts[0])
    for k, part in enumerate(parts):
        later = product(parts[k + 1]) if k + 1 < len(parts) else None
        finish(part, held)
        held = later


def clear(first, *refs):
    @pl.when(first)
    def _():
        for ref in refs:
            ref[...] = jnp.zeros_like(ref)


def unpack_small(place, own, other, *refs):
    vectors = refs[-1]
    z, c = place[0], place[1]
    lines, rows, _ = own.shape
    layers, extra, wide = vectors.shape[1:]
    keys = rows // layers
    for layer in range(layers):
        w_in, w_in_t, w_out, w_out_t, *rest = refs[10 * layer : 10 * layer + 10]
        base = layer * keys
        for source, side in ((own, c), (other, 1 - c)):
            for i in range(lines):
                shard = 2 * (i ^ z) + side
                start = pl.multiple_of(shard * keys, keys)
                w_in[pl.ds(start, keys)] = source[i, base : base + keys, :wide]
                w_out[pl.ds(start, keys)] = source[i, base : base + keys, wide : 2 * wide]
                vectors[shard, layer] = source[i, base : base + extra, 2 * wide :]
        w_in_t[...] = w_in[...].T
        w_out_t[...] = w_out[...].T
        held = [vectors[shard, layer].astype(jnp.float32) for shard in range(vectors.shape[0])]
        for row, target in enumerate(rest[:5]):
            size = target.shape[1] // len(held)
            target[...] = jnp.concatenate([part[row : row + 1, :size] for part in held], axis=1)
        biases = rest[5]
        size = biases.shape[1] // len(held)
        for shard, part in enumerate(held):
            whole = jnp.concatenate([part[5:6], part[6:7]], axis=1)
            biases[:, shard * size : (shard + 1) * size] = whole[:, :size]


def token_branch(values, scale, small, b_out, u_out, hidden_out, slope_out):
    gain1, shift1, w_in, w_out, gain2, shift2 = small
    rows, wide = values.shape[0], w_in.shape[1]
    normed, _ = norm_parts(values)
    u_out[:rows] = (normed * gain1[...] + shift1[...]).astype(jnp.bfloat16)
    below = lax.broadcasted_iota(jnp.int32, (wide - rows, values.shape[1]), 0)
    u_out[rows:] = jnp.where(below == 0, 1.0, 0.0).astype(jnp.bfloat16)
    hidden, slope = gelu_pair(dot(w_in[...], u_out[...], 1, 0))
    hidden_out[...] = hidden
    slope_out[...] = slope
    middle = values + scale * (dot(w_out[:rows], hidden, 1, 0) + b_out[0, :rows])
    normed, _ = norm_parts(middle)
    return middle, (normed * gain2[...] + shift2[...]).astype(jnp.bfloat16)


def token_forward(place, scale, x, b_out, *rest, layer):
    small, (u_out, hidden_out, slope_out, middle_out, v_out) = rest[:6], rest[6:]
    count, rows = x.shape[:2]
    for k in range(count):
        part = scale[count * pl.program_id(0) + k, 2 * layer]
        middle, v = token_branch(
            x[k].astype(jnp.float32), part, small, b_out, u_out.at[k], hidden_out.at[k], slope_out.at[k]
        )
        middle_out[k] = middle
        v_out[k * rows : (k + 1) * rows] = v


def token_grads(scale, grad, back_v, middle, x, u, hidden, slope, w_in, w_out, gain1, gain2, padded):
    rows, width = grad.shape
    normed, inv_std = norm_parts(middle)
    moved = back_v * normed
    sums = [jnp.sum(moved, 0, keepdims=True), jnp.sum(back_v, 0, keepdims=True)]
    grad_mid = grad + norm_input_grad(back_v * gain2[...], normed, inv_std)
    padded[:rows] = (scale * grad_mid).astype(jnp.bfloat16)
    low = padded[...]
    b_out = dot(jnp.ones((8, width), jnp.bfloat16), low, 1, 1)[:1]
    w_out_grad = dot(hidden, low, 1, 1)
    pre = (dot(w_out[...], low, 1, 0) * slope.astype(jnp.float32)).astype(jnp.bfloat16)
    w_in_grad = dot(pre, u, 1, 1)
    back = dot(w_in[:rows], pre, 1, 0)
    normed, inv_std = norm_parts(x)
    sums = [jnp.sum(back * normed, 0, keepdims=True), jnp.sum(back, 0, keepdims=True)] + sums
    return grad_mid + norm_input_grad(back * gain1[...], normed, inv_std), sums, b_out, w_in_grad, w_out_grad


def token_blocks(place, w_in_grad, w_out_grad, whole, put):
    z, c = place[0], place[1]
    keys = whole.shape[1] // 8
    for which, total in ((0, w_in_grad), (1, w_out_grad)):
        whole[which] = total[...].astype(jnp.bfloat16)
        for i in range(4):
            for side, core in ((0, c), (1, 1 - c)):
                start = pl.multiple_of((2 * (i ^ z) + core) * keys, keys)
                put(which, i, side, whole[which, pl.ds(start, keys)])


def token_backward(place, scale, grad, back_v, middle, x, u, hidden, slope, w_in, w_out, gain1, gain2, *rest):
    image = pl.program_id(0)
    g_cout, g_cin = rest[:2]
    last = len(rest) == 2 + 6 + 4
    if last:
        grad_out, mine_out, other_out, vector, low_out, above_grad = rest[2:8]
        layer = 1
    else:
        earlier, grad_out, mine_out, other_out, vector = rest[2:5], *rest[5:9]
        layer = 0
    padded, w_in_grad, w_out_grad, whole = rest[-4:]
    count, rows = x.shape[:2]
    first = image == 0
    clear(first, padded, vector, w_in_grad, w_out_grad)

    @pl.when(first)
    def _():
        vector[4:5] = g_cout[...]
        for j in range(g_cin.shape[0]):
            vector[8 + j : 9 + j] = g_cin[j]
        if not last:
            vector[16:] = earlier[2][...]

    if last:
        clear(first, above_grad)
    found = []
    for k in range(count):
        part = slice(k * rows, (k + 1) * rows)
        result, *sums = token_grads(
            scale[count * image + k, 2 * layer], grad[k].astype(jnp.float32), back_v[part], middle[k],
            x[k].astype(jnp.float32), u[k], hidden[k], slope[k], w_in, w_out, gain1, gain2, padded.at[k],
        )
        grad_out[k] = result
        if last:
            out = scale[count * image + k, 1] * result
            above_grad[...] += jnp.sum(out, 0, keepdims=True)
            low_out[part] = out.astype(jnp.bfloat16)
        found.append(sums)
    for k in range(4):
        vector[k : k + 1] += sum(sums[0][k] for sums in found)
    vector[5:6, : padded.shape[1]] += sum(sums[1] for sums in found)
    w_in_grad[...] += sum(sums[2] for sums in found)
    w_out_grad[...] += sum(sums[3] for sums in found)

    @pl.when(image == pl.num_programs(0) - 1)
    def _():
        targets = (mine_out, other_out)

        def put(which, i, side, part):
            targets[side][i, which] = part

        if not last:
            for side in range(2):
                targets[side][:, 2:] = earlier[side][...]
        token_blocks(place, w_in_grad, w_out_grad, whole, put)


def out_weight_grad(place, low, hidden, mine_out, other_out, turned, whole):
    @pl.when(pl.program_id(0) == 0)
    def _():
        turned[...] = low[...].T

    out_blocks(place, turned, hidden[0], mine_out, other_out, whole)


class Weight:
    def __init__(self, refs, which):
        self.which = which
        self.shards, self.parts = (refs[which], refs[2 + which]), (refs[4:9], refs[9:14])

    def blocks(self, copy, i):
        for side, (line, from_x, from_y, low, high) in enumerate(self.parts):
            if copy < 3:
                yield side, (line, from_x, from_y)[copy].at[i - 1, self.which], 0
            else:
                yield side, (low, high)[self.which].at[i - 1, 0], 0


def fetch_in(place, layer, weight, target, sem):
    z, c, q = place[0], place[1], place[2]
    copies, _, columns = target.shape
    rows = weight.shards[0].shape[1]
    for copy in range(copies):
        j = copy ^ q

        def put(ref, i, side, first):
            start = pl.multiple_of((2 * (i ^ z) + (c ^ side)) * rows + first, 16)
            goal = target.at[j, pl.ds(start, ref.shape[0])]
            pltpu.make_async_copy(ref, goal, sem.at[j]).start()

        for side, shard in enumerate(weight.shards):
            put(shard.at[layer, :, pl.ds(pl.multiple_of(j * columns, columns), columns)], 0, side, 0)
        for i in range(1, copies):
            for side, ref, first in weight.blocks(copy, i):
                put(ref, i, side, first)


def fetch_out(place, layer, weight, target, sem):
    z, c, q = place[0], place[1], place[2]
    lines, part, _ = target.shape
    for i in range(lines):

        def put(ref, start):
            goal = target.at[i ^ z, pl.ds(pl.multiple_of(start, 16), ref.shape[0])]
            pltpu.make_async_copy(ref, goal, sem.at[i ^ z]).start()

        if i == 0:
            for side, shard in enumerate(weight.shards):
                put(shard.at[layer], (c ^ side) * (part // 2))
            continue
        for copy in range(4):
            for side, ref, first in weight.blocks(copy, i):
                put(ref, (c ^ side) * (part // 2) + (copy ^ q) * (part // 8) + first)


def arrive(weight, sem, step):
    pltpu.make_async_copy(weight.at[step], weight.at[step], sem.at[step]).wait()


def out_blocks(place, turned, hidden, mine_out, other_out, whole):
    c, q = place[1], place[2]
    whole[...] = dot(turned[...], hidden, 1, 0).astype(jnp.bfloat16)
    copies, _, rows, columns = mine_out.shape
    size = columns // 2
    for side, target in ((c, mine_out), (1 - c, other_out)):
        units = pl.ds(pl.multiple_of(side * size, 128), size)
        for j in range(copies):
            start = 2 * j * rows
            target[position(j ^ q), 0, :, :size] = whole[start : start + rows, units]
            target[position(j ^ q), 0, :, size:] = whole[start + rows : start + 2 * rows, units]


def first_forward(place, scale, v, middle, bias_in, bias_out, *rest):
    weight_in, weight_out = Weight(rest[:14], 0), Weight(rest[:14], 1)
    hidden_out, slope_out, x_out, w_in, w_out, hidden, sem_in, sem_out = rest[14:]
    step = pl.program_id(0)

    @pl.when(step == 0)
    def _():
        fetch_in(place, 0, weight_in, w_in, sem_in)
        fetch_out(place, 0, weight_out, w_out, sem_out)

    @pl.when(step < 4)
    def _():
        j = (step & 3) ^ place[2]
        arrive(w_in, sem_in, j)
        def product(part):
            return dot(v[part], w_in[j], 1, 0) + bias_in[...]

        def finish(part, found):
            value, slope = gelu_pair(found)
            hidden_out[0, part] = value
            hidden[j, part] = value
            slope_out[0, part] = slope

        staggered(chunks(v.shape[0], 4), product, finish)

    @pl.when(step == 4)
    def _():
        for j in range(4):
            arrive(w_out, sem_out, j)
        for image, part in enumerate(chunks(v.shape[0], middle.shape[0])):
            branch = bias_out[...] + sum(dot(hidden[j, part], w_out[j], 1, 0) for j in range(4))
            x_out[image] = middle[image] + scale[image, 1] * branch


def last_hidden(place, scale, v, bias, grad, w_in, hidden_out, slope_out, blocks_out, low_out, bias_grad, hidden, turned):
    step = pl.program_id(0)

    @pl.when(step == 0)
    def _():
        rows = grad.shape[1]
        sums = 0.0
        for image in range(grad.shape[0]):
            out = scale[image, 3] * grad[image].astype(jnp.float32)
            sums = sums + jnp.sum(out, 0, keepdims=True)
            low_out[image * rows : (image + 1) * rows] = out.astype(jnp.bfloat16)
        bias_grad[...] = sums
        turned[...] = low_out[...].T

    @pl.when(step < 4)
    def _():
        def product(part):
            return dot(v[part], w_in[...], 1, 0) + bias[...]

        def finish(part, found):
            value, slope = gelu_pair(found)
            hidden_out[0, part] = value
            hidden[step & 3, part] = value
            slope_out[0, part] = slope

        staggered(chunks(v.shape[0], 4), product, finish)

    @pl.when(step >= 4)
    def _():
        found = dot(turned[...], hidden[step & 3], 1, 0).astype(jnp.bfloat16)
        size = blocks_out.shape[2]
        for k in range(blocks_out.shape[0]):
            blocks_out[k] = found[:, k * size : (k + 1) * size]


def last_out(place, scale, hidden, middle, bias, w_out, x_out, total):
    step = pl.program_id(0)

    @pl.when(step == 0)
    def _():
        total[...] = jnp.zeros_like(total)

    total[...] += dot(hidden[0], w_out[...], 1, 0)

    @pl.when(step == pl.num_programs(0) - 1)
    def _():
        for image in range(middle.shape[0]):
            rows = middle.shape[1]
            branch = total[image * rows : (image + 1) * rows] + bias[...]
            x_out[image] = (middle[image] + scale[image, 3] * branch).astype(x_out.dtype)


def last_backward(place, low, v, slope, w_out, w_in, in_out, back_out, bias_grad, turned, pre):
    @pl.when(pl.program_id(0) == 0)
    def _():
        turned[...] = v[...].T
        back_out[...] = jnp.zeros_like(back_out)

    sums = []

    def product(part):
        return dot(low[part], w_out[...], 1, 1)

    def finish(part, found):
        grad = found * slope[0, part].astype(jnp.float32)
        sums.append(jnp.sum(grad, 0, keepdims=True))
        pre[part] = grad.astype(jnp.bfloat16)

    staggered(chunks(low.shape[0], 2), product, finish)
    bias_grad[0] = sum(sums)
    for part in chunks(turned.shape[0], 3):
        in_out[part] = dot(turned[part], pre[...], 1, 0).astype(jnp.bfloat16)
    back_out[...] += dot(pre[...], w_in[...], 1, 1)


def channel_backward(place, low, v, slope, *rest, layer):
    mine, theirs, back_out, bias_grad, w_out, w_in, turned, pre, whole, sem_out, sem_in = rest[14:]
    z, c = place[0], place[1]
    step = pl.program_id(0)

    @pl.when(step == 0)
    def _():
        fetch_out(place, layer, Weight(rest[:14], 1), w_out, sem_out)
        fetch_in(place, layer, Weight(rest[:14], 0), w_in, sem_in)
        turned[...] = v[...].T
        back_out[...] = jnp.zeros_like(back_out)

    j = step ^ z
    arrive(w_out, sem_out, j)
    arrive(w_in, sem_in, j)
    sums = []

    def product(part):
        return dot(low[part], w_out[j], 1, 1)

    def finish(part, found):
        grad = found * slope[0, part].astype(jnp.float32)
        sums.append(jnp.sum(grad, 0, keepdims=True))
        pre[part] = grad.astype(jnp.bfloat16)

    staggered(chunks(low.shape[0], 2), product, finish)
    bias_grad[0] = sum(sums)
    for part in chunks(turned.shape[0], 3):
        whole[part] = dot(turned[part], pre[...], 1, 0).astype(jnp.bfloat16)
    lines = mine.shape[1]
    rows = whole.shape[0] // (2 * lines)
    for i in range(lines):
        for side, target in ((c, mine), (1 - c, theirs)):
            start = pl.multiple_of((2 * (i ^ z) + side) * rows, rows)
            target[0, i] = whole[pl.ds(start, rows)]
    back_out[...] += dot(pre[...], w_in[j], 1, 1)


def finish_last(place, grad_in, got_in, grad_out, got_out, in_out, out_out):
    in_out[0] = grad_in[...].astype(jnp.float32) + got_in[...].astype(jnp.float32)
    out_out[0] = (grad_out[0].astype(jnp.float32) + got_out[0].astype(jnp.float32)).T


def finish_first(place, *refs):
    parts_in, parts_out = refs[:4], refs[4:8]
    in_out, out_out, whole = refs[-3:]
    for j in range(4):
        columns = parts_in[j].shape[2]
        start = pl.multiple_of((j ^ place[2]) * columns, columns)
        in_out[0, :, pl.ds(start, columns)] = parts_in[j][0].astype(jnp.float32)
        rows, columns = parts_out[j].shape[1:]
        for half in range(2):
            start = pl.multiple_of((2 * (j ^ place[2]) + half) * rows, rows)
            part = parts_out[j][0, :, half * columns // 2 : (half + 1) * columns // 2]
            whole[pl.ds(start, rows)] = part.astype(jnp.float32)
    out_out[0] = whole[...].T


class Kernels:
    def __init__(self, place, slots, rows, width, inner, hidden, lines, block):
        self.place = place
        self.slots, self.rows, self.width = slots, rows, width
        self.inner, self.hidden = inner, hidden
        self.lines, self.block = lines, block
        self.part = hidden // 4
        self.wide = 256

    def run(self, body, steps, inputs, outputs, scratch, flops, aliases=None, **fixed):
        sizes = sum(a.size * a.dtype.itemsize for a, _, _ in inputs)
        sizes += sum(math.prod(o[0]) * jnp.dtype(o[1]).itemsize for o in outputs)

        def spec(block, index):
            if isinstance(block, tuple):
                return pl.BlockSpec(block, index)
            return pl.BlockSpec(memory_space=block)

        return pl.pallas_call(
            functools.partial(body, **fixed) if fixed else body,
            name=body.__name__,
            grid_spec=pltpu.PrefetchScalarGridSpec(
                num_scalar_prefetch=1,
                grid=(steps,),
                in_specs=[spec(block, index) for _, block, index in inputs],
                out_specs=[spec(o[2], o[3]) for o in outputs],
                scratch_shapes=scratch,
            ),
            out_shape=[jax.ShapeDtypeStruct(o[0], o[1]) for o in outputs],
            input_output_aliases=aliases or {},
            compiler_params=pltpu.CompilerParams(
                dimension_semantics=("arbitrary",), vmem_limit_bytes=VMEM_BYTES
            ),
            cost_estimate=pl.CostEstimate(flops=flops, bytes_accessed=sizes, transcendentals=0),
        )(self.place, *[a for a, _, _ in inputs])

    def image(self, array):
        return (array, (1,) + array.shape[1:], lambda i, s: (i, 0, 0))

    def fixed(self, array):
        zeros = (0,) * array.ndim
        return (array, array.shape, lambda i, s: zeros)

    def scalars(self, array):
        return (array, pltpu.SMEM, None)

    def in_hbm(self, arrays):
        return [(a, pltpu.HBM, None) for a in arrays]

    def fixed_out(self, shape, dtype):
        zeros = (0,) * len(shape)
        return (shape, dtype, shape, lambda i, s: zeros)

    def columns(self, array, count):
        return (array, (array.shape[0], array.shape[1] // count), lambda i, s: (0, i))

    def columns_out(self, rows, columns, count, dtype):
        return ((rows, columns), dtype, (rows, columns // count), lambda i, s: (0, i))

    def late(self, step, start):
        return jnp.clip(step - start, 0, 3)

    def images_out(self, rows, dtype):
        block = (IMAGES, rows, self.width)
        return ((self.slots, rows, self.width), dtype, block, lambda i, s: (i, 0, 0))

    def images(self, array):
        return (array, (IMAGES,) + array.shape[1:], lambda i, s: (i, 0, 0))

    def rows_out(self):
        shape = (self.slots * self.rows, self.width)
        return (shape, jnp.bfloat16, (IMAGES * self.rows, self.width), lambda i, s: (i, 0))

    def quarters(self, array, which, start=0):
        return (array, (1,) + array.shape[1:], lambda i, s: (self.late(i, start) ^ s[which], 0, 0))

    def quarters_out(self, which, start=0):
        rows = self.slots * self.rows
        block = (1, rows, self.part)
        return ((4,) + block[1:], jnp.bfloat16, block, lambda i, s: (self.late(i, start) ^ s[which], 0, 0))

    def row(self, array, which, start=0):
        return (array, (1, self.part), lambda i, s: (0, self.late(i, start) ^ s[which]))

    def out_blocks_out(self, start=0):
        block = (4, 1, self.block, self.width)
        shape = (4, self.lines) + block[2:]
        return (shape, jnp.bfloat16, block, lambda i, s: (0, self.late(i, start), 0, 0))

    def product(self):
        return 2 * self.slots * self.rows * self.width * self.hidden

    def unpack_small(self, own, other, layers, shards, extra):
        bf16, f32 = jnp.bfloat16, jnp.float32
        inner, wide, width = self.inner, self.wide, self.width
        outputs = [((inner, wide), bf16), ((wide, inner), bf16)] * 2
        outputs += [((1, width), f32)] * 5 + [((1, self.hidden), f32)]
        found = self.run(
            unpack_small,
            1,
            [self.fixed(own), self.fixed(other)],
            [self.fixed_out(*part) for part in outputs * layers],
            [pltpu.VMEM((shards, layers, extra, wide), bf16)],
            0,
        )
        return [list(found[10 * layer : 10 * layer + 10]) for layer in range(layers)]

    def token_product(self):
        return 2 * self.slots * self.wide * self.width * self.inner

    def b_out(self, array, layer):
        return (array, (1,) + array.shape[1:], lambda i, s: (layer, 0, 0))

    def token_outs(self):
        bf16 = jnp.bfloat16
        outs = [self.images_out(rows, bf16) for rows in (self.wide, self.inner, self.inner)]
        return outs + [self.images_out(self.rows, jnp.float32), self.rows_out()]

    def token_forward(self, scale, x, b_out, small, layer):
        return self.run(
            token_forward,
            self.slots // IMAGES,
            [self.scalars(scale), self.images(x), self.b_out(b_out, layer)] + [self.fixed(a) for a in small],
            self.token_outs(),
            [],
            2 * self.token_product(),
            layer=layer,
        )

    def first_forward(self, scale, v, middle, bias_in, bias_out, weights):
        bf16, f32 = jnp.bfloat16, jnp.float32
        rows = self.slots * self.rows
        return self.run(
            first_forward,
            5,
            [self.scalars(scale), self.fixed(v), self.fixed(middle), self.row(bias_in, 2), self.fixed(bias_out)]
            + self.in_hbm(weights),
            [self.quarters_out(2)] * 2 + [self.fixed_out((self.slots, self.rows, self.width), f32)],
            [
                self.weight(),
                self.weight(),
                pltpu.VMEM((4, rows, self.part), bf16),
                pltpu.SemaphoreType.DMA((4,)),
                pltpu.SemaphoreType.DMA((4,)),
            ],
            2 * self.product(),
        )

    def steps(self, array):
        return (array, (1,) + array.shape[1:], lambda i, s: (jnp.minimum(i, 3), 0, 0))

    def steps_out(self):
        block = (1, self.slots * self.rows, self.part)
        return ((4,) + block[1:], jnp.bfloat16, block, lambda i, s: (jnp.minimum(i, 3), 0, 0))

    def columns_in(self, array):
        return (array, (array.shape[0], self.part), lambda i, s: (0, jnp.minimum(i, 3)))

    def rows_in(self, array):
        return (array, (self.part, array.shape[1]), lambda i, s: (i, 0))

    def last_hidden(self, scale, v, bias, grad, w_in):
        bf16, f32 = jnp.bfloat16, jnp.float32
        rows = self.slots * self.rows
        block = (2, self.width, self.part // 2)
        return self.run(
            last_hidden,
            8,
            [self.scalars(scale), self.fixed(v), self.columns_in(bias), self.fixed(grad), self.columns_in(w_in)],
            [self.steps_out()] * 2
            + [((8,) + block[1:], bf16, block, lambda i, s: (jnp.maximum(i - 4, 0), 0, 0))]
            + [self.fixed_out((rows, self.width), bf16), self.fixed_out((1, self.width), f32)],
            [pltpu.VMEM((4, rows, self.part), bf16), pltpu.VMEM((self.width, rows), bf16)],
            2 * self.product(),
        )

    def last_out(self, scale, hidden, middle, bias, w_out):
        return self.run(
            last_out,
            4,
            [self.scalars(scale), self.steps(hidden), self.fixed(middle), self.fixed(bias), self.rows_in(w_out)],
            [self.fixed_out(middle.shape, jnp.bfloat16)],
            [pltpu.VMEM((self.slots * self.rows, self.width), jnp.float32)],
            self.product(),
        )[0]

    def last_backward(self, low, v, slope, w_out, w_in):
        bf16, f32 = jnp.bfloat16, jnp.float32
        rows = self.slots * self.rows
        return self.run(
            last_backward,
            4,
            [self.fixed(low), self.fixed(v), self.steps(slope), self.rows_in(w_out), self.columns_in(w_in)],
            [
                ((self.width, self.hidden), bf16, (self.width, self.part), lambda i, s: (0, i)),
                self.fixed_out((rows, self.width), f32),
                ((4, 1, self.part), f32, (1, 1, self.part), lambda i, s: (i, 0, 0)),
            ],
            [pltpu.VMEM((self.width, rows), bf16), pltpu.VMEM((rows, self.part), bf16)],
            3 * self.product(),
        )

    def token_backward(self, scale, grad, back, kept, small, g_cout, g_cin, keys, earlier=()):
        bf16, f32 = jnp.bfloat16, jnp.float32
        width = self.width
        middle, x, u, hidden, slope = kept
        inputs = [self.scalars(scale), self.images(grad)]
        inputs += [(back, (IMAGES * self.rows, width), lambda i, s: (i, 0))]
        inputs += [self.images(a) for a in (middle, x, u, hidden, slope)]
        inputs += [self.fixed(a) for a in tuple(small) + (g_cout, g_cin) + tuple(earlier)]
        outputs = [self.images_out(self.rows, f32)]
        outputs += [self.fixed_out((self.lines, 4 if earlier else 2, keys, self.wide), bf16)] * 2
        outputs += [self.fixed_out((32 if earlier else 16, width), f32)]
        if not earlier:
            outputs += [self.rows_out(), self.fixed_out((1, width), f32)]
        return self.run(
            token_backward,
            self.slots // IMAGES,
            inputs,
            outputs,
            [
                pltpu.VMEM((IMAGES, self.wide, width), bf16),
                pltpu.VMEM((self.inner, self.wide), f32),
                pltpu.VMEM((self.inner, self.wide), f32),
                pltpu.VMEM((2, self.inner, self.wide), bf16),
            ],
            4 * self.token_product(),
        )

    def out_weight_grad(self, low, hidden):
        rows = self.slots * self.rows
        return self.run(
            out_weight_grad,
            4,
            [self.fixed(low), self.quarters(hidden, 0)],
            [self.out_blocks_out()] * 2,
            [pltpu.VMEM((self.width, rows), jnp.bfloat16), pltpu.VMEM((self.width, self.part), jnp.bfloat16)],
            self.product(),
        )

    def weight(self):
        return pltpu.VMEM((4, self.width, self.part), jnp.bfloat16)

    def out_forward(self, scale, hidden, middle, bias, weights, layer, dtype):
        return self.run(
            out_forward,
            4,
            [self.scalars(scale), self.quarters(hidden, 0), self.fixed(middle), self.fixed(bias)]
            + self.in_hbm(weights),
            [self.fixed_out(middle.shape, dtype)],
            [
                self.weight(),
                pltpu.VMEM((self.slots * self.rows, self.width), jnp.float32),
                pltpu.SemaphoreType.DMA((4,)),
            ],
            self.product(),
            layer=layer,
        )[0]

    def channel_backward(self, low, v, slope, weights, layer):
        bf16, f32 = jnp.bfloat16, jnp.float32
        rows = self.slots * self.rows
        block = (1, self.lines, self.block, self.width)
        shape = (4, self.lines, self.block, self.width)
        blocks = (shape, bf16, block, lambda j, s: (position(j ^ s[0] ^ s[2]), 0, 0, 0))
        return self.run(
            channel_backward,
            4,
            [self.fixed(low), self.fixed(v), self.quarters(slope, 0)]
            + self.in_hbm(weights),
            [
                blocks,
                blocks,
                self.fixed_out((rows, self.width), f32),
                ((4, 1, self.part), f32, (1, 1, self.part), lambda i, s: (i ^ s[0], 0, 0)),
            ],
            [
                self.weight(),
                self.weight(),
                pltpu.VMEM((self.width, rows), bf16),
                pltpu.VMEM((rows, self.part), bf16),
                pltpu.VMEM((self.width, self.part), bf16),
                pltpu.SemaphoreType.DMA((4,)),
                pltpu.SemaphoreType.DMA((4,)),
            ],
            3 * self.product(),
            layer=layer,
        )

    def shard_outs(self, layer, layers):
        shapes = (layers, self.block, self.hidden), (layers, self.part // 2, self.width)
        return [(shape, jnp.float32, (1,) + shape[1:], lambda i, s: (layer, 0, 0)) for shape in shapes]

    def finish_last(self, whole, layer, layers):
        inputs = [self.fixed(a) for a in (whole.values[0], whole.got0, whole.values[1], whole.got1)]
        return self.run(finish_last, 1, inputs, self.shard_outs(layer, layers), [], 0)

    def finish_first(self, parts_in, parts_out, layer, layers, earlier):
        def one(part):
            array, index = part
            return (array, (1,) + array.shape[1:], lambda i, s: (index, 0, 0))

        inputs = [one(part) for part in parts_in + parts_out]
        return self.run(
            finish_first,
            1,
            inputs + self.in_hbm(earlier),
            self.shard_outs(layer, layers),
            [pltpu.VMEM((self.width, self.part // 2), jnp.float32)],
            0,
            {1 + len(inputs): 0, 2 + len(inputs): 1},
        )


class Moves:
    def __init__(self):
        self.lines = lax.axis_size("fsdp") // 2
        self.copies = lax.axis_size("dp")
        me = lax.axis_index("fsdp")
        self.z, self.c, self.q = me // 2, me % 2, lax.axis_index("dp")

    def along(self, values, bits):
        return lax.ppermute(values, "fsdp", [(f, f ^ (2 * bits)) for f in range(2 * self.lines)])

    def core(self, values):
        return lax.ppermute(values, "fsdp", [(f, f ^ 1) for f in range(2 * self.lines)])

    def across(self, values, bits):
        return lax.ppermute(values, "dp", [(q, q ^ bits) for q in range(self.copies)])


class Held:
    def __init__(self, moves):
        self.moves, self.fresh = moves, []
        self.half = moves.lines // 2

    def bring(self, **arrays):
        for name, array in arrays.items():
            setattr(self, name, array)
            self.fresh.append(name)


def settle(held, *values):
    names = [(part, name) for part in held for name in part.fresh]
    arrays = tuple(getattr(part, name) for part, name in names)
    arrays = lax.optimization_barrier(tuple(values) + arrays)
    for (part, name), array in zip(names, arrays[len(values) :]):
        setattr(part, name, array)
    for part in held:
        part.fresh = []
    return arrays[: len(values)]


class Gather(Held):
    def __init__(self, moves, part):
        super().__init__(moves)
        self.part = part

    def direct(self):
        self.bring(**{"z%d" % i: self.moves.along(self.part, i) for i in range(1, self.moves.lines)})

    def join(self):
        self.line = jnp.stack([getattr(self, "z%d" % i) for i in range(1, self.moves.lines)])

    def first(self):
        self.bring(x=self.moves.across(self.line, 1), y=self.moves.across(self.line, 2))

    def second(self):
        self.bring(low=self.moves.across(self.y[:, :1], 1), high=self.moves.across(self.x[:, 1:], 2))

    def core(self, *names):
        self.bring(**{name + "_core": self.moves.core(getattr(self, name)) for name in names})

    def whole(self):
        names = ("line", "x", "y", "low", "high")
        return [getattr(self, name) for name in names] + [getattr(self, name + "_core") for name in names]


class Sum(Held):
    def __init__(self, moves, mine, other):
        super().__init__(moves)
        self.mine, self.theirs = mine, other
        self.low, self.high = slice(0, self.half), slice(self.half, None)

    def both(self, copies, part):
        return self.mine[copies, part] + self.got[copies, part]

    def core(self):
        self.bring(got=self.moves.core(self.theirs))

    def first(self):
        self.bring(
            from_x=self.moves.across(self.both(slice(2, 4), self.low), 1),
            from_y=self.moves.across(self.both(slice(1, 3), self.high), 2),
        )

    def second(self):
        self.bring(
            low2=self.moves.across(self.both(1, self.low) + self.from_x[0], 2),
            high1=self.moves.across(self.both(3, self.high) + self.from_y[1], 1),
        )

    def halves(self):
        low = self.both(0, self.low) + self.from_x[1] + self.low2
        high = self.both(0, self.high) + self.from_y[0] + self.high1
        return low, high

    def once(self):
        low, high = self.halves()
        self.block = low[0]
        blocks = [low[i] for i in range(1, self.half)] + [high[i] for i in range(self.half)]
        self.bring(**{"z%d" % (i + 1): self.moves.along(block, i + 1) for i, block in enumerate(blocks)})

    def far(self):
        self.block, high = self.halves()
        self.bring(z=self.moves.along(high, 2))

    def near(self):
        pair = self.block + self.z
        self.block = pair[0]
        self.bring(z1=self.moves.along(pair[1], 1))

    def total(self):
        total = self.block.astype(jnp.float32)
        for i in range(1, self.moves.lines):
            if hasattr(self, "z%d" % i):
                total = total + getattr(self, "z%d" % i).astype(jnp.float32)
        return total.astype(jnp.bfloat16)


class Share(Held):
    def __init__(self, moves, part, axis):
        super().__init__(moves)
        self.part, self.axis = part, axis

    def first(self):
        self.bring(near=self.moves.across(self.part, self.axis))

    def second(self):
        self.bring(far=self.moves.across(jnp.stack([self.part, self.near]), 3 - self.axis))

    def parts(self):
        near, far = (self.near[None], 0), (self.far, 0)
        return [(self.part[None], 0)] + ([near, far] if self.axis == 1 else [far, near]) + [(self.far, 1)]


class SumSmall(Held):
    def __init__(self, moves, mine, other):
        super().__init__(moves)
        self.mine, self.theirs = mine, other

    def core(self):
        self.bring(got=self.moves.core(self.theirs))

    def along(self):
        both = self.mine + self.got
        self.value = both[0]
        self.bring(**{"z%d" % i: self.moves.along(both[i], i) for i in range(1, self.moves.lines)})

    def across(self, bits):
        if bits == 1:
            parts = [self.value] + [getattr(self, "z%d" % i) for i in range(1, self.moves.lines)]
            self.value = sum(part.astype(jnp.float32) for part in parts).astype(jnp.bfloat16)
        else:
            self.value = self.value + self.got
        self.bring(got=self.moves.across(self.value, bits))

    def total(self):
        return self.value.astype(jnp.float32) + self.got.astype(jnp.float32)


class Copies(Held):
    def __init__(self, moves, *values):
        super().__init__(moves)
        self.values = list(values)

    def step(self, *axes):
        got = [self.moves.across(value, bits) for value, bits in zip(self.values, axes)]
        self.bring(got0=got[0], got1=got[1])

    def add(self):
        self.values = [self.values[0] + self.got0, self.values[1] + self.got1]


class SumAll(Held):
    def __init__(self, moves, value):
        super().__init__(moves)
        self.value, self.bit = value, 1

    def step(self):
        count = 2 * self.moves.lines
        got = lax.ppermute(self.value, "fsdp", [(i, i ^ self.bit) for i in range(count)])
        self.bit *= 2
        self.bring(value=self.value + got)

    def copies(self):
        self.bring(**{"q%d" % bits: self.moves.across(self.value, bits) for bits in (1, 2, 3)})

    def total(self):
        return (self.value + self.q1) + (self.q2 + self.q3)


def blocked_shards(
    tokens, image_counts, skip_mask, norm1_gain, norm1_bias, token_in, token_in_bias, token_out,
    token_out_bias, norm2_gain, norm2_bias, channel_in, channel_in_bias, channel_out,
    channel_out_bias, cotangent,
):
    f32, bf16 = jnp.float32, jnp.bfloat16
    slots, patches, width = tokens.shape
    layers, in_rows, hidden = channel_in.shape
    keys = token_out.shape[1]
    moves = Moves()
    shards_count = 2 * moves.lines
    inner = keys * shards_count
    rows = -(-patches // 16) * 16
    place = jnp.stack([moves.z, moves.c, moves.q]).astype(jnp.int32)
    kernels = Kernels(place, slots, rows, width, inner, hidden, moves.lines, in_rows)
    wide = kernels.wide

    live = (jnp.arange(slots, dtype=jnp.int32) < image_counts[0]).astype(f32)
    scale = live[:, None, None] * skip_mask.astype(f32)

    def padded(images):
        return jnp.pad(images, ((0, 0), (0, rows - patches), (0, 0)))

    def quarter(array, axis):
        size = array.shape[axis] // 4
        return lax.dynamic_slice_in_dim(array, moves.q * size, size, axis)

    def widen(array):
        return jnp.pad(array, ((0, 0), (0, 0), (0, wide - array.shape[2])))

    gap = jnp.zeros((layers, keys, rows - patches), bf16)
    with_bias = jnp.concatenate([jnp.swapaxes(token_in, 1, 2), gap, token_in_bias[:, :, None]], 2)
    vectors = jnp.stack([norm1_gain, norm1_bias, norm2_gain, norm2_bias, channel_out_bias], 1)
    biases = jnp.pad(channel_in_bias, ((0, 0), (0, 2 * wide - channel_in_bias.shape[1])))
    vectors = jnp.concatenate([widen(vectors), biases.reshape(layers, 2, wide)], 1)
    extra = 16
    vectors = jnp.pad(vectors, ((0, 0), (0, extra - vectors.shape[1]), (0, 0)))
    vectors = jnp.pad(vectors, ((0, 0), (0, keys - extra), (0, 0)))
    packs = jnp.concatenate([widen(with_bias), widen(token_out), vectors], 2).reshape(layers * keys, width)
    b_outs = jnp.pad(token_out_bias.astype(f32), ((0, 0), (0, wide - patches)))[:, :, None]
    scale = scale.reshape(slots, 2 * layers)

    first = Gather(moves, jnp.stack([quarter(channel_in[0], 1), quarter(channel_out[0], 0)]))
    small = Gather(moves, packs)
    shards_held = Held(moves)
    small.direct()
    first.direct()
    shards_held.bring(ins=moves.core(channel_in[0]), outs=moves.core(channel_out[0]))
    first.fresh = ["z1", "z2"]
    shard_in, shard_out = settle((small, first), channel_in[1], channel_out[1])
    first.fresh = ["z3"]
    settle((first, shards_held))
    first.join()
    small.line = jnp.stack([small.part, small.z1, small.z2, small.z3])

    w_cin1 = lax.all_gather(shard_in, "fsdp", axis=0, tiled=True)
    w_cout1 = lax.all_gather(shard_out, "fsdp", axis=0, tiled=True)

    small.core("line")
    first.first()
    began, first.fresh = first.fresh, []
    first.core("line")
    (first.line,) = settle((first, small), first.line)
    first.fresh = began
    found = kernels.unpack_small(small.line, small.line_core, layers, shards_count, extra)
    x0 = padded(tokens)
    (w_in0, w_in_t0, w_out0, w_out_t0, gain1_0, shift1_0, gain2_0, shift2_0, b_cout0, b_cin0) = found[0]
    (w_in1, w_in_t1, w_out1, w_out_t1, gain1_1, shift1_1, gain2_1, shift2_1, b_cout1, b_cin1) = found[1]
    u0, h0, d0, mid0, v0 = kernels.token_forward(
        scale, x0, b_outs, (gain1_0, shift1_0, w_in0, w_out_t0, gain2_0, shift2_0), 0
    )
    (v0,) = settle((first,), v0)

    first.second()
    first.core("x", "y")
    (v0,) = settle((first,), v0)
    first.core("low", "high")
    (v0,) = settle((first,), v0)
    weights = [channel_in, channel_out, shards_held.ins[None], shards_held.outs[None]] + first.whole()
    hid0, slope0, x1 = kernels.first_forward(scale, v0, mid0, b_cin0, b_cout0, weights)
    u1, h1, d1, mid1, v1 = kernels.token_forward(
        scale, x1, b_outs, (gain1_1, shift1_1, w_in1, w_out_t1, gain2_1, shift2_1), 1
    )
    grad2 = padded(cotangent)
    hid1, slope1, blocks1, low1, g_cout1 = kernels.last_hidden(scale, v1, b_cin1, grad2, w_cin1)

    grad_cout1 = lax.psum_scatter(blocks1, "fsdp", scatter_dimension=0, tiled=True)
    grad_cin1, back, g_cin1 = kernels.last_backward(low1, v1, slope1, w_cout1, w_cin1)
    grad_cin1 = lax.psum_scatter(grad_cin1, "fsdp", scatter_dimension=0, tiled=True)
    grad1, *tokens1, vector1, low0, g_cout0 = kernels.token_backward(
        scale, grad2, back, (mid1, x1, u1, h1, d1), (w_in_t1, w_out1, gain1_1, gain2_1), g_cout1, g_cin1, keys
    )
    mine, theirs = kernels.out_weight_grad(low0, hid0)
    mine, theirs, grad1 = settle((), mine, theirs, grad1)

    sum_out0 = Sum(moves, mine, theirs)
    sum_out0.core()
    mine, theirs, back, g_cin0 = kernels.channel_backward(low0, v0, slope0, weights, 0)
    mine, theirs, back, grad_cout1 = settle((sum_out0,), mine, theirs, back, grad_cout1)

    sum_in0 = Sum(moves, mine, theirs)
    sum_in0.core()
    sum_out0.first()
    grad0, *tokens, vector = kernels.token_backward(
        scale, grad1, back, (mid0, x0, u0, h0, d0), (w_in_t0, w_out0, gain1_0, gain2_0), g_cout0, g_cin0, keys,
        (*tokens1, vector1),
    )
    hid1, grad0, *tokens, vector = settle((sum_in0, sum_out0), hid1, grad0, *tokens, vector)

    sum_tokens = SumSmall(moves, *tokens)
    sum_tokens.core()
    sum_in0.first()
    sum_out0.second()
    vector_sum = SumAll(moves, vector)
    vector_sum.step()
    output = kernels.last_out(scale, hid1, mid1, b_cout1, w_cout1)
    output, grad_cin1, grad_cout1 = settle(
        (sum_in0, sum_out0, sum_tokens, vector_sum), output, grad_cin1, grad_cout1
    )

    sum_in0.second()
    sum_out0.once()
    sum_tokens.along()
    vector_sum.step()
    whole = Copies(moves, grad_cin1, grad_cout1)
    whole.step(1, 2)
    output = with_layout_constraint(output[:, :patches], ROWS_FIRST)
    (output,) = settle((sum_in0, sum_out0, sum_tokens, whole, vector_sum), output)

    sum_in0.once()
    sum_tokens.across(1)
    vector_sum.step()
    share_out0 = Share(moves, sum_out0.total(), 2)
    share_out0.first()
    whole.add()
    whole.step(2, 1)
    input_grad = with_layout_constraint(grad0[:, :patches], ROWS_FIRST)
    (input_grad,) = settle((sum_in0, sum_tokens, share_out0, whole, vector_sum), input_grad)

    total = sum_in0.total()
    near = [moves.across(total, bits) for bits in (1, 2, 3)]
    share_out0.second()
    sum_tokens.across(2)
    vector_sum.copies()
    finished = kernels.finish_last(whole, 1, layers)
    near = settle((share_out0, sum_tokens, vector_sum), *near)
    parts = [(part[None], 0) for part in [total] + list(near)]
    grad_in, grad_out = kernels.finish_first(parts, share_out0.parts(), 0, layers, finished)
    near = sum_tokens.total()

    near = near.reshape(layers, 2, keys, wide)
    grad_t_in = jnp.swapaxes(near[:, 0, :, :patches], 1, 2)
    grad_b_in = near[:, 0, :, rows]
    grad_t_out = near[:, 1, :, :patches]
    sums = vector_sum.total().reshape(layers, 16, width)
    me = lax.axis_index("fsdp")

    def owned(row):
        size = width // shards_count
        return lax.dynamic_slice_in_dim(sums[:, row], me * size, size, 1)

    grad_gain1, grad_shift1, grad_gain2, grad_shift2, grad_b_cout = [owned(row) for row in range(5)]
    size = hidden // shards_count
    grad_b_cin = lax.dynamic_slice(sums, (0, 8 + me // 2, (me % 2) * size), (layers, 1, size))[:, 0]
    bias_total = sums[:, 5, :patches]
    return (
        output, input_grad, grad_gain1, grad_shift1, grad_t_in, grad_b_in, grad_t_out, bias_total,
        grad_gain2, grad_shift2, grad_in, grad_b_cin, grad_out, grad_b_cout,
    )


def fits(mesh):
    return mesh.shape["dp"] == 4 and mesh.shape["fsdp"] == 8


def solution(mesh):
    in_specs = (
        P(("dp", "fsdp"), None, None),
        P(("dp", "fsdp")),
        P(("dp", "fsdp"), None, None),
        P(None, "fsdp"),
        P(None, "fsdp"),
        P(None, None, "fsdp"),
        P(None, "fsdp"),
        P(None, "fsdp", None),
        P(),
        P(None, "fsdp"),
        P(None, "fsdp"),
        P(None, "fsdp", None),
        P(None, "fsdp"),
        P(None, "fsdp", None),
        P(None, "fsdp"),
        P(("dp", "fsdp"), None, None),
    )
    out_specs = (
        P(("dp", "fsdp"), None, None),
        P(("dp", "fsdp"), None, None),
        P(None, "fsdp"),
        P(None, "fsdp"),
        P(None, None, "fsdp"),
        P(None, "fsdp"),
        P(None, "fsdp", None),
        P(),
        P(None, "fsdp"),
        P(None, "fsdp"),
        P(None, "fsdp", None),
        P(None, "fsdp"),
        P(None, "fsdp", None),
        P(None, "fsdp"),
    )
    program = blocked_shards if fits(mesh) else shards
    return jax.shard_map(program, mesh=mesh, in_specs=in_specs, out_specs=out_specs, check_vma=False)
```
